32 devices in a mesh: rows: 4 (over y, x), seq: 4 (over z), fsdp: 2 (over core).
Axes of the slice: x: 2, y: 2, z: 4, core: 2. Of those that a mesh axis runs over, the one named last changes fastest.
Arguments:
- states: bfloat16 [4, 4, 2048, 2048], P('rows', None, 'seq'), may hold values from -6 to 6
- doc_ids: int32 [4, 4, 2048], P('rows'), may hold values from 0 to 12, as said below
- w_qkv: bfloat16 [3, 2048, 2048], P(None, ('rows', 'seq'), 'fsdp'), may hold values from -0.125 to 0.125
- w_out: bfloat16 [2048, 2048], P('fsdp', ('rows', 'seq')), may hold values from -1 to 1
- w_up: bfloat16 [2048, 8192], P(('rows', 'seq'), 'fsdp'), may hold values from -0.125 to 0.125
- w_down: bfloat16 [8192, 2048], P('fsdp', ('rows', 'seq')), may hold values from -0.0625 to 0.0625
- bias_qv: bfloat16 [2, 32, 64], P(None, 'fsdp', ('rows', 'seq')), may hold values from -3 to 3
- bias_out: bfloat16 [2048], P(('rows', 'seq')), may hold values from -2 to 2
- bias_up: bfloat16 [128, 64], P('fsdp', ('rows', 'seq')), may hold values from -3 to 3
- bias_down: bfloat16 [2048], P(('rows', 'seq')), may hold values from -2 to 2
- gain_one: bfloat16 [2048], P(('rows', 'seq')), may hold values from 0.5 to 1.5
- shift_one: bfloat16 [2048], P(('rows', 'seq')), may hold values from -1.5 to 1.5
- gain_two: bfloat16 [2048], P(('rows', 'seq')), may hold values from 0.5 to 1.5
- shift_two: bfloat16 [2048], P(('rows', 'seq')), may hold values from -1.5 to 1.5
- cotangent: bfloat16 [4, 4, 2048, 2048], P('rows', None, 'seq'), may hold values from -6 to 6
Outputs:
- out_states: bfloat16 [4, 4, 2048, 2048], P('rows', None, 'seq')
- grad_states: bfloat16 [4, 4, 2048, 2048], P('rows', None, 'seq')
- grad_w_qkv: float32 [3, 2048, 2048], P(None, ('rows', 'seq'), 'fsdp')
- grad_w_out: float32 [2048, 2048], P('fsdp', ('rows', 'seq'))
- grad_w_up: float32 [2048, 8192], P(('rows', 'seq'), 'fsdp')
- grad_w_down: float32 [8192, 2048], P('fsdp', ('rows', 'seq'))
- grad_bias_qv: float32 [2, 32, 64], P(None, 'fsdp', ('rows', 'seq'))
- grad_bias_out: float32 [2048], P(('rows', 'seq'))
- grad_bias_up: float32 [128, 64], P('fsdp', ('rows', 'seq'))
- grad_bias_down: float32 [2048], P(('rows', 'seq'))
- grad_gain_one: float32 [2048], P(('rows', 'seq'))
- grad_shift_one: float32 [2048], P(('rows', 'seq'))
- grad_gain_two: float32 [2048], P(('rows', 'seq'))
- grad_shift_two: float32 [2048], P(('rows', 'seq'))
The draws below stay inside these ranges and needn't reach their ends.
Inputs may be any that keep to these rules, and one draw needn't show every extreme that they name: `doc_ids`: within each row the numbers never fall from one position to the next; a row starts at 0 and ends at 12; in each row one whole segment, drawn from the seed, belongs to a single document.
All inputs are finite; a program needn't handle non-finite values.
Results may differ from the reference program's by a relative error of at most 0.019.
Values may be sent and summed in bfloat16 or wider, within the bound.
A program may use at most 1.125 GiB of HBM per device.

```python
import jax
import jax.numpy as jnp
from jax import lax

D = 2048
HEADS = 32
HEAD = 64
FF = 8192
SUMM = 50
SEG = 2048
SEGS = 4
ROWS = 4
DOCS = 12


def draw_doc_ids(key, part):
    key = jax.random.fold_in(key, 11)
    key_whole, key_cuts = jax.random.split(key)
    length = SEGS * SEG
    whole_seg = jax.random.randint(key_whole, (ROWS, 1), 0, SEGS)
    boundary = jax.random.randint(key_cuts, (ROWS, DOCS), 1, length - SEG)
    boundary = jnp.where(boundary > whole_seg * SEG, boundary + SEG, boundary)
    places = jnp.arange(length, dtype=jnp.int32)
    counts = jnp.sum((places[None, None, :] >= boundary[:, :, None]).astype(jnp.int32), axis=1)
    return counts.reshape(ROWS, SEGS, SEG).astype(jnp.int32)


def raised(values, own_key, source, target, blocks, factor):
    def block_of(axis_at):
        return (jnp.arange(values.shape[axis_at]) // (values.shape[axis_at] // blocks)).reshape((-1,) + (1,) * (values.ndim - 1 - axis_at))

    first = jax.random.permutation(own_key, blocks)[block_of(target)]
    far = (block_of(target) + blocks // 2) % blocks
    return jnp.where((block_of(source) == first) | (block_of(source) == far), factor * values, values)


def shard_levels(own_key, extent, shards, least, largest):
    def one(axis_at, blocks):
        steps = jax.random.uniform(jax.random.fold_in(jax.random.fold_in(own_key, 6), axis_at), (blocks,), jnp.float32, least / len(shards), largest / len(shards))
        return jnp.repeat(jnp.exp(steps), extent[axis_at] // blocks).reshape((-1,) + (1,) * (len(extent) - axis_at - 1))

    loudness = one(*shards[0])
    for cut in shards[1:]:
        loudness = loudness * one(*cut)
    return loudness


def bell_draw(stream_key, shape, spread, reach, pieces=(), held_as=jnp.bfloat16):
    factor_of = shard_levels(stream_key, shape, pieces, -0.22, 0.18) if pieces else 1.0
    values = jax.random.normal(stream_key, shape, jnp.float32) * spread * factor_of
    return jnp.minimum(jnp.maximum(values, -reach), reach).astype(held_as)


def noise_with(key, extent, deviation, bound, pieces, heavy, kind=jnp.bfloat16):
    values = deviation * jax.random.normal(key, extent, jnp.float32)
    if pieces:
        values = values * shard_levels(key, extent, pieces, -0.22, 0.18)
    return jnp.clip(raised(values, jax.random.fold_in(key, 3), *heavy), -bound, bound).astype(kind)


def setup_inputs(seed: int = 0) -> dict:
    arg_keys = jax.random.split(jax.random.key(seed), 16)
    return {
        "states": bell_draw(arg_keys[0], (ROWS, SEGS, SEG, D), 1.0, 6.0, ((0, 4), (2, 4))),
        "doc_ids": draw_doc_ids(jax.random.fold_in(arg_keys[15], 71), 0),
        "w_qkv": bell_draw(arg_keys[2], (3, D, D), D ** -0.5, 0.125, ((1, 16), (2, 2))),
        "w_out": bell_draw(arg_keys[3], (D, D), (D // 64) ** -0.5, 1.0, ((0, 2), (1, 16))),
        "w_up": bell_draw(arg_keys[4], (D, FF), D ** -0.5, 0.125, ((0, 16), (1, 2))),
        "w_down": bell_draw(arg_keys[5], (FF, D), FF ** -0.5, 0.0625, ((0, 2), (1, 16))),
        "bias_qv": bell_draw(arg_keys[6], (2, D // 64, 64), 0.5, 3.0, ((1, 2), (2, 16))),
        "bias_out": bell_draw(arg_keys[7], (D,), 0.3, 2.0, ((0, 16),)),
        "bias_up": bell_draw(arg_keys[8], (FF // 64, 64), 0.5, 3.0, ((0, 2), (1, 16))),
        "bias_down": bell_draw(arg_keys[9], (D,), 0.3, 2.0, ((0, 16),)),
        "gain_one": jnp.clip(1.0 + 0.1 * jax.random.normal(arg_keys[10], (D,), jnp.float32), 0.5, 1.5).astype(jnp.bfloat16),
        "shift_one": bell_draw(arg_keys[11], (D,), 0.2, 1.5, ((0, 16),)),
        "gain_two": jnp.clip(1.0 + 0.1 * jax.random.normal(arg_keys[12], (D,), jnp.float32), 0.5, 1.5).astype(jnp.bfloat16),
        "shift_two": bell_draw(arg_keys[13], (D,), 0.2, 1.5, ((0, 16),)),
        "cotangent": noise_with(arg_keys[14], (ROWS, SEGS, SEG, D), 1.0, 6.0, ((0, 4), (2, 4)), (2, 3, 4, 2.0)),
    }


@jax.custom_vjp
def low(v):
    return lax.optimization_barrier(v.astype(jnp.bfloat16)).astype(jnp.float32)

@jax.custom_vjp
def low_back(v):
    return v

def low_keep(v):
    return (low(v), None)

def low_pass(kept, grad):
    return (grad,)

def back_keep(v):
    return (v, None)

def back_low(kept, grad):
    return (low(grad),)
low.defvjp(low_keep, low_pass)
low_back.defvjp(back_keep, back_low)
neg_big = -1e+30
norm_eps = 1e-05

def layer_norm(field, gain_vec, shift_vec):
    row_mean = lax.optimization_barrier(jnp.mean(field, axis=-1, keepdims=True))
    centered = field - row_mean
    variance = lax.optimization_barrier(jnp.mean(centered * centered, axis=-1, keepdims=True))
    return centered * lax.rsqrt(variance + norm_eps) * gain_vec + shift_vec

def gelu_exact(field):
    return jax.nn.gelu(field, approximate=False)

def earlier(field, offset, fill_value):
    widths = tuple(((offset, 0) if dim_index == 1 else (0, 0) for dim_index in range(field.ndim)))
    return jnp.pad(field, widths, constant_values=fill_value)[:, :field.shape[1]]

def to_blocks(field):
    rows_all = field.shape[0]
    segs_all = field.shape[1]
    length = field.shape[2]
    split = field.reshape(rows_all * segs_all, length, HEADS, HEAD)
    return jnp.transpose(split, (0, 2, 1, 3)).reshape(rows_all * segs_all * HEADS, length, HEAD)

def attend_block(block_items):
    query_blk, key_blk, value_blk, qdoc_blk, kdoc_blk = block_items
    highest = lax.Precision.HIGHEST
    scores = low_back(jnp.dot(query_blk, key_blk.T, precision=highest))
    places = jnp.arange(key_blk.shape[0])
    causal = places[None, :] <= jnp.arange(query_blk.shape[0])[:, None]
    causal = causal | (places[None, :] >= query_blk.shape[0])
    allowed = causal & (qdoc_blk[:, None] == kdoc_blk[None, :])
    scores = jnp.where(allowed, scores, neg_big)
    row_top = lax.optimization_barrier(jnp.max(scores, axis=-1, keepdims=True))
    exponent = jnp.where(allowed, jnp.exp(scores - row_top), 0.0)
    attn_probs = exponent / lax.optimization_barrier(jnp.sum(exponent, axis=-1, keepdims=True))
    return jnp.dot(low(attn_probs), value_blk, precision=highest)

def forward(states, w_qkv, w_out, w_up, w_down, bias_qv, bias_out, bias_up, bias_down, gain_one, shift_one, gain_two, shift_two, doc_ids):
    highest = lax.Precision.HIGHEST
    normed_one = low(layer_norm(states, gain_one, shift_one))
    projected = jnp.einsum('rsid,kde->krsie', normed_one, w_qkv, precision=highest)
    bias_pair = bias_qv.reshape(2, D)
    query = low_back(low((projected[0] + bias_pair[0]) * HEAD ** (-0.5)))
    keys = low_back(low(projected[1]))
    values = low_back(low(projected[2] + bias_pair[1]))
    sum_keys = keys[:, :, SEG - SUMM:]
    sum_values = values[:, :, SEG - SUMM:]
    sum_docs = doc_ids[:, :, SEG - SUMM:]
    keys_all = jnp.concatenate((keys, earlier(sum_keys, 1, 0.0), earlier(sum_keys, 2, 0.0)), axis=2)
    values_all = jnp.concatenate((values, earlier(sum_values, 1, 0.0), earlier(sum_values, 2, 0.0)), axis=2)
    key_docs = jnp.concatenate((doc_ids, earlier(sum_docs, 1, -1), earlier(sum_docs, 2, -1)), axis=2)
    rows_all = states.shape[0]
    blocks = rows_all * SEGS
    query_docs = jnp.repeat(doc_ids.reshape(blocks, SEG), HEADS, axis=0)
    key_docs = jnp.repeat(key_docs.reshape(blocks, SEG + 2 * SUMM), HEADS, axis=0)
    mixed_blocks = lax.map(jax.checkpoint(attend_block), (to_blocks(query), to_blocks(keys_all), to_blocks(values_all), query_docs, key_docs))
    mixed = jnp.transpose(mixed_blocks.reshape(blocks, HEADS, SEG, HEAD), (0, 2, 1, 3)).reshape(rows_all, SEGS, SEG, D)
    mixed = low_back(low(mixed))
    attn_lin = low_back(jnp.einsum('rsie,ed->rsid', mixed, w_out, precision=highest))
    hidden = states + attn_lin + bias_out
    normed_two = low(layer_norm(hidden, gain_two, shift_two))
    up_proj = low_back(jnp.einsum('rsid,df->rsif', normed_two, w_up, precision=highest) + bias_up.reshape(FF))
    activated = low(gelu_exact(up_proj))
    return hidden + jnp.einsum('rsif,fd->rsid', activated, w_down, precision=highest) + bias_down

def reference(states, doc_ids, w_qkv, w_out, w_up, w_down, bias_qv, bias_out, bias_up, bias_down, gain_one, shift_one, gain_two, shift_two, cotangent):
    floats = tuple((item.astype(jnp.float32) for item in (states, w_qkv, w_out, w_up, w_down, bias_qv, bias_out, bias_up, bias_down, gain_one, shift_one, gain_two, shift_two)))

    def run_layer(*params):
        return forward(*params, doc_ids)
    result, pullback = jax.vjp(run_layer, *floats)
    grads = pullback(cotangent.astype(jnp.float32))
    return (result.astype(jnp.bfloat16), grads[0].astype(jnp.bfloat16), grads[1], grads[2], grads[3], grads[4], grads[5], grads[6], grads[7], grads[8], grads[9], grads[10], grads[11], grads[12])
```

```python
import functools

import jax
import jax.numpy as jnp
from jax import lax
from jax.experimental import pallas as pl
from jax.experimental.pallas import tpu as pltpu
from jax.sharding import PartitionSpec as P

HEAD = 64
SUMM = 50
SEGS = 4
F32 = jnp.float32
BF = jnp.bfloat16


neg_big = -1e30
norm_eps = 1e-05


def spread(block, axis, source):
    block = jnp.where(lax.axis_index(axis) == source, block, jnp.zeros_like(block))
    return lax.psum(block, axis)


def layer_norm(field, gain_vec, shift_vec):
    row_mean = jnp.mean(field, axis=-1, keepdims=True)
    centered = field - row_mean
    variance = jnp.mean(centered * centered, axis=-1, keepdims=True)
    return centered * lax.rsqrt(variance + norm_eps) * gain_vec + shift_vec


def gelu_exact(field):
    return jax.nn.gelu(field, approximate=False)


def earlier(field, offset, fill_value):
    widths = tuple(((offset, 0) if dim_index == 1 else (0, 0) for dim_index in range(field.ndim)))
    return jnp.pad(field, widths, constant_values=fill_value)[:, : field.shape[1]]


def later(field, offset):
    widths = tuple(((0, offset) if dim_index == 1 else (0, 0) for dim_index in range(field.ndim)))
    return jnp.pad(field, widths)[:, offset:]


def lead(field):
    return jnp.moveaxis(field, 1, 0)


def halves(field):
    return lax.psum(field.astype(jnp.bfloat16), "fsdp").astype(jnp.float32)


def local(
    states,
    doc_ids,
    w_qkv,
    w_out,
    w_up,
    w_down,
    bias_qv,
    bias_out,
    bias_up,
    bias_down,
    gain_one,
    shift_one,
    gain_two,
    shift_two,
    cotangent,
):
    attn_full = (
        lax.all_gather(w_qkv, ("rows", "seq"), axis=1, tiled=True),
        lax.all_gather(w_out, ("rows", "seq"), axis=1, tiled=True),
        lax.all_gather(bias_qv, ("rows", "seq"), axis=2, tiled=True),
        lax.all_gather(gain_one, ("rows", "seq"), axis=0, tiled=True),
        lax.all_gather(shift_one, ("rows", "seq"), axis=0, tiled=True),
        lax.all_gather(bias_out, ("rows", "seq"), axis=0, tiled=True),
    )
    qkv_full, out_full, bqv_full, gain_a, shift_a, bias_o = attn_full
    rows_dev, seg_count, width, model = states.shape
    seq_count = lax.axis_size("seq")
    seq_place = lax.axis_index("seq")
    seg_len = width * seq_count
    half_width = qkv_full.shape[2]
    heads_loc = half_width // HEAD
    score_scale = HEAD ** (-0.5)
    states_f = states.astype(jnp.float32)
    normed_f, norm_one_back = jax.vjp(
        layer_norm, states_f, gain_a.astype(jnp.float32), shift_a.astype(jnp.float32)
    )
    normed_one = normed_f.astype(jnp.bfloat16)
    projected = jnp.einsum(
        "rsid,kde->krsie", normed_one, qkv_full, preferred_element_type=jnp.float32
    )
    bias_pair = bqv_full.astype(jnp.float32).reshape(2, half_width)
    query = ((projected[0] + bias_pair[0]) * score_scale).astype(jnp.bfloat16)
    keys = projected[1].astype(jnp.bfloat16)
    values = (projected[2] + bias_pair[1]).astype(jnp.bfloat16)
    tail = jnp.stack((keys[:, :, width - SUMM :], values[:, :, width - SUMM :]))
    summary = spread(tail, "seq", seq_count - 1)
    sum_keys = jnp.concatenate((earlier(summary[0], 1, 0.0), earlier(summary[0], 2, 0.0)), axis=2)
    sum_values = jnp.concatenate((earlier(summary[1], 1, 0.0), earlier(summary[1], 2, 0.0)), axis=2)
    sum_src = doc_ids[:, :, seg_len - SUMM :]
    sum_docs = jnp.concatenate((earlier(sum_src, 1, -1), earlier(sum_src, 2, -1)), axis=2)
    sum_k5 = sum_keys.reshape(rows_dev, seg_count, 2 * SUMM, heads_loc, HEAD)
    sum_v5 = sum_values.reshape(rows_dev, seg_count, 2 * SUMM, heads_loc, HEAD)
    first_pos = seq_place * width
    query_docs = lax.dynamic_slice_in_dim(doc_ids, first_pos, width, 2)
    query_pos = first_pos + jnp.arange(width, dtype=jnp.int32)
    query5 = query.reshape(rows_dev, seg_count, width, heads_loc, HEAD)
    sum_allowed = (query_docs[:, :, :, None] == sum_docs[:, :, None, :])[:, :, None]
    sum_scores = jnp.einsum(
        "rsihe,rsjhe->rshij", query5, sum_k5, preferred_element_type=jnp.float32
    )
    sum_scores = jnp.where(sum_allowed, sum_scores, neg_big)
    start_max = jnp.max(sum_scores, axis=-1)
    start_exp = jnp.where(sum_allowed, jnp.exp(sum_scores - start_max[..., None]), 0.0)
    start_sum = jnp.sum(start_exp, axis=-1)
    start_acc = jnp.einsum(
        "rshij,rsjhe->rsihe",
        start_exp.astype(jnp.bfloat16),
        sum_v5,
        preferred_element_type=jnp.float32,
    )
    key_piece = lax.all_gather(keys, "seq", axis=2, tiled=True)
    value_piece = lax.all_gather(values, "seq", axis=2, tiled=True)
    count = key_piece.shape[2]
    key5 = key_piece.reshape(rows_dev, seg_count, count, heads_loc, HEAD)
    value5 = value_piece.reshape(rows_dev, seg_count, count, heads_loc, HEAD)
    key_pos = jnp.arange(count, dtype=jnp.int32)
    causal = (key_pos[None, :] <= query_pos[:, None])[None, None, None]
    allowed = causal & (query_docs[:, :, :, None] == doc_ids[:, :, None, :])[:, :, None]
    scores = jnp.einsum("rsihe,rsjhe->rshij", query5, key5, preferred_element_type=jnp.float32)
    scores = jnp.where(allowed, scores, neg_big)
    new_max = jnp.maximum(start_max, jnp.max(scores, axis=-1))
    factor = jnp.exp(start_max - new_max)
    exponent = jnp.where(allowed, jnp.exp(scores - new_max[..., None]), 0.0)
    new_sum = start_sum * factor + jnp.sum(exponent, axis=-1)
    gained = jnp.einsum(
        "rshij,rsjhe->rsihe",
        exponent.astype(jnp.bfloat16),
        value5,
        preferred_element_type=jnp.float32,
    )
    new_acc = start_acc * jnp.swapaxes(factor, 2, 3)[..., None] + gained
    log_sum = new_max + jnp.log(new_sum)
    mixed_f = new_acc / jnp.swapaxes(new_sum, 2, 3)[..., None]
    mixed = mixed_f.reshape(rows_dev, seg_count, width, half_width).astype(jnp.bfloat16)
    attn_lin = halves(
        jnp.einsum("rsie,ed->rsid", mixed, out_full, preferred_element_type=jnp.float32)
    )
    hidden = states_f + attn_lin + bias_o.astype(jnp.float32)
    ffn_full = (
        lax.all_gather(w_up, ("rows", "seq"), axis=0, tiled=True),
        lax.all_gather(w_down, ("rows", "seq"), axis=1, tiled=True),
        lax.all_gather(bias_up, ("rows", "seq"), axis=1, tiled=True),
        lax.all_gather(gain_two, ("rows", "seq"), axis=0, tiled=True),
        lax.all_gather(shift_two, ("rows", "seq"), axis=0, tiled=True),
        lax.all_gather(bias_down, ("rows", "seq"), axis=0, tiled=True),
    )
    up_full, down_full, bias_u, gain_b, shift_b, bias_d = ffn_full
    normed_two_f, norm_two_back = jax.vjp(
        layer_norm, hidden, gain_b.astype(jnp.float32), shift_b.astype(jnp.float32)
    )
    normed_two = normed_two_f.astype(jnp.bfloat16)
    up_proj = jnp.einsum(
        "rsid,df->rsif", normed_two, up_full, preferred_element_type=jnp.float32
    ) + bias_u.astype(jnp.float32).reshape(-1)
    activated_f, gelu_back = jax.vjp(gelu_exact, up_proj)
    activated = activated_f.astype(jnp.bfloat16)
    down_proj = halves(
        jnp.einsum("rsif,fd->rsid", activated, down_full, preferred_element_type=jnp.float32)
    )
    out_states = (hidden + down_proj + bias_d.astype(jnp.float32)).astype(jnp.bfloat16)
    up_back, down_back = (
        lax.all_gather(w_up, ("rows", "seq"), axis=0, tiled=True),
        lax.all_gather(w_down, ("rows", "seq"), axis=1, tiled=True),
    )
    qkv_back, out_back = (
        lax.all_gather(w_qkv, ("rows", "seq"), axis=1, tiled=True),
        lax.all_gather(w_out, ("rows", "seq"), axis=1, tiled=True),
    )
    grad_out = cotangent.astype(jnp.float32)
    grad_bias_down = jnp.sum(grad_out, axis=(0, 1, 2))
    grad_w_down = jnp.einsum(
        "rsif,rsid->fd", activated, cotangent, preferred_element_type=jnp.float32
    )
    d_act = jnp.einsum("rsid,fd->rsif", cotangent, down_back, preferred_element_type=jnp.float32)
    (d_up,) = gelu_back(d_act)
    d_up_low = d_up.astype(jnp.bfloat16)
    grad_bias_up = jnp.sum(d_up_low, axis=(0, 1, 2), dtype=jnp.float32).reshape(bias_u.shape)
    grad_w_up = jnp.einsum(
        "rsid,rsif->df", normed_two, d_up_low, preferred_element_type=jnp.float32
    )
    d_norm_two = halves(
        jnp.einsum("rsif,df->rsid", d_up_low, up_back, preferred_element_type=jnp.float32)
    )
    d_hidden_ln, grad_gain_two, grad_shift_two = norm_two_back(d_norm_two)
    d_hidden = grad_out + d_hidden_ln
    ffn_grads = (
        lax.psum_scatter(grad_w_up, ("rows", "seq"), scatter_dimension=0, tiled=True),
        lax.psum_scatter(grad_w_down, ("rows", "seq"), scatter_dimension=1, tiled=True),
        lax.psum_scatter(grad_bias_up, ("rows", "seq"), scatter_dimension=1, tiled=True),
        lax.psum_scatter(grad_gain_two, ("rows", "seq"), scatter_dimension=0, tiled=True),
        lax.psum_scatter(grad_shift_two, ("rows", "seq"), scatter_dimension=0, tiled=True),
        lax.psum_scatter(grad_bias_down, ("rows", "seq"), scatter_dimension=0, tiled=True),
    )
    grad_bias_out = jnp.sum(d_hidden, axis=(0, 1, 2))
    d_hidden_low = d_hidden.astype(jnp.bfloat16)
    grad_w_out = jnp.einsum(
        "rsie,rsid->ed", mixed, d_hidden_low, preferred_element_type=jnp.float32
    )
    d_mixed = jnp.einsum(
        "rsid,ed->rsie", d_hidden_low, out_back, preferred_element_type=jnp.float32
    ).astype(jnp.bfloat16)
    d_mixed5 = d_mixed.reshape(rows_dev, seg_count, width, heads_loc, HEAD)
    keys_all, values_all = (
        lax.all_gather(keys, "seq", axis=2, tiled=True),
        lax.all_gather(values, "seq", axis=2, tiled=True),
    )
    key_lead = lead(keys_all.reshape(rows_dev, seg_count, seg_len, heads_loc, HEAD))
    value_lead = lead(values_all.reshape(rows_dev, seg_count, seg_len, heads_loc, HEAD))
    query_lead = lead(query5)
    grad_lead = lead(d_mixed5)
    key_positions = jnp.arange(seg_len, dtype=jnp.int32)

    def segment_back(seg_items):
        q_seg, do_seg, lse_seg, qdoc_seg, k_seg, v_seg, kdoc_seg, sk_seg, sv_seg, sdoc_seg = (
            seg_items
        )
        causal = (key_positions[None, :] <= query_pos[:, None])[None, None]
        allowed = causal & (qdoc_seg[:, :, None] == kdoc_seg[:, None, :])[:, None]
        scores = jnp.einsum("rihe,rjhe->rhij", q_seg, k_seg, preferred_element_type=jnp.float32)
        attn_probs = jnp.where(allowed, jnp.exp(scores - lse_seg[..., None]), 0.0)
        d_probs = jnp.einsum("rihe,rjhe->rhij", do_seg, v_seg, preferred_element_type=jnp.float32)
        summ_allowed = (qdoc_seg[:, :, None] == sdoc_seg[:, None, :])[:, None]
        summ_scores = jnp.einsum(
            "rihe,rjhe->rhij", q_seg, sk_seg, preferred_element_type=jnp.float32
        )
        summ_probs = jnp.where(summ_allowed, jnp.exp(summ_scores - lse_seg[..., None]), 0.0)
        summ_dprobs = jnp.einsum(
            "rihe,rjhe->rhij", do_seg, sv_seg, preferred_element_type=jnp.float32
        )
        delta = jnp.sum(attn_probs * d_probs, axis=-1) + jnp.sum(summ_probs * summ_dprobs, axis=-1)
        d_scores = (attn_probs * (d_probs - delta[..., None])).astype(jnp.bfloat16)
        d_summ = (summ_probs * (summ_dprobs - delta[..., None])).astype(jnp.bfloat16)
        d_query = jnp.einsum("rhij,rjhe->rihe", d_scores, k_seg, preferred_element_type=jnp.float32)
        d_query = d_query + jnp.einsum(
            "rhij,rjhe->rihe", d_summ, sk_seg, preferred_element_type=jnp.float32
        )
        d_sum_keys = jnp.einsum(
            "rhij,rihe->rjhe", d_summ, q_seg, preferred_element_type=jnp.float32
        )
        d_sum_values = jnp.einsum(
            "rhij,rihe->rjhe",
            summ_probs.astype(jnp.bfloat16),
            do_seg,
            preferred_element_type=jnp.float32,
        )
        return (d_query, d_scores, attn_probs.astype(jnp.bfloat16), d_sum_keys, d_sum_values, delta)

    seg_inputs = (
        query_lead,
        grad_lead,
        lead(log_sum),
        lead(query_docs),
        key_lead,
        value_lead,
        lead(doc_ids),
        lead(sum_k5),
        lead(sum_v5),
        lead(sum_docs),
    )
    d_query_lead, d_scores_all, probs_all, d_sk_lead, d_sv_lead, delta_lead = lax.map(
        segment_back, seg_inputs
    )
    d_key_part = jnp.einsum(
        "srhij,srihe->jrshe", d_scores_all, query_lead, preferred_element_type=jnp.float32
    )
    d_value_part = jnp.einsum(
        "srhij,srihe->jrshe", probs_all, grad_lead, preferred_element_type=jnp.float32
    )
    key_grads = lax.psum_scatter(
        jnp.stack((d_key_part, d_value_part), axis=3)
        .reshape(width * lax.axis_size("seq"), rows_dev, seg_count, 2, half_width)
        .astype(jnp.bfloat16),
        "seq",
        scatter_dimension=0,
        tiled=True,
    ).astype(jnp.float32)
    key_grads = jnp.transpose(key_grads, (3, 1, 2, 0, 4))
    d_sk = jnp.moveaxis(d_sk_lead, 0, 1).reshape(rows_dev, seg_count, 2 * SUMM, half_width)
    d_sv = jnp.moveaxis(d_sv_lead, 0, 1).reshape(rows_dev, seg_count, 2 * SUMM, half_width)
    src_keys = later(d_sk[:, :, :SUMM], 1) + later(d_sk[:, :, SUMM:], 2)
    src_values = later(d_sv[:, :, :SUMM], 1) + later(d_sv[:, :, SUMM:], 2)
    summ_grads = lax.psum(jnp.stack((src_keys, src_values)).astype(jnp.bfloat16), "seq").astype(
        jnp.float32
    )
    owner_grads = jnp.where(seq_place == seq_count - 1, summ_grads, 0.0)
    owner_grads = jnp.pad(owner_grads, ((0, 0), (0, 0), (0, 0), (width - SUMM, 0), (0, 0)))
    key_grads = key_grads + owner_grads
    d_keys_low = key_grads[0].astype(jnp.bfloat16)
    d_values_low = key_grads[1].astype(jnp.bfloat16)
    d_query = jnp.moveaxis(d_query_lead, 0, 1).reshape(rows_dev, seg_count, width, half_width)
    d_query_low = d_query.astype(jnp.bfloat16)
    d_pre = (d_query_low.astype(jnp.float32) * score_scale).astype(jnp.bfloat16)
    grad_bias_qv = jnp.stack(
        (
            jnp.sum(d_pre, axis=(0, 1, 2), dtype=jnp.float32),
            jnp.sum(d_values_low, axis=(0, 1, 2), dtype=jnp.float32),
        )
    ).reshape(bqv_full.shape)
    d_qkv = jnp.stack((d_pre, d_keys_low, d_values_low))
    grad_w_qkv = jnp.einsum(
        "rsid,krsie->kde", normed_one, d_qkv, preferred_element_type=jnp.float32
    )
    d_norm_one = halves(
        jnp.einsum("krsie,kde->rsid", d_qkv, qkv_back, preferred_element_type=jnp.float32)
    )
    d_states_ln, grad_gain_one, grad_shift_one = norm_one_back(d_norm_one)
    grad_states = (d_hidden + d_states_ln).astype(jnp.bfloat16)
    attn_grads = (
        lax.psum_scatter(grad_w_qkv, ("rows", "seq"), scatter_dimension=1, tiled=True),
        lax.psum_scatter(grad_w_out, ("rows", "seq"), scatter_dimension=1, tiled=True),
        lax.psum_scatter(grad_bias_qv, ("rows", "seq"), scatter_dimension=2, tiled=True),
        lax.psum_scatter(grad_gain_one, ("rows", "seq"), scatter_dimension=0, tiled=True),
        lax.psum_scatter(grad_shift_one, ("rows", "seq"), scatter_dimension=0, tiled=True),
        lax.psum_scatter(grad_bias_out, ("rows", "seq"), scatter_dimension=0, tiled=True),
    )
    return (
        out_states,
        grad_states,
        attn_grads[0],
        attn_grads[1],
        ffn_grads[0],
        ffn_grads[1],
        attn_grads[2],
        attn_grads[5],
        ffn_grads[2],
        ffn_grads[5],
        attn_grads[3],
        attn_grads[4],
        ffn_grads[3],
        ffn_grads[4],
    )


def dot_nt(a,b): return lax.dot_general(a,b,(((1,),(1,)),((),())),preferred_element_type=F32)
def dot_nn(a,b): return lax.dot_general(a,b,(((1,),(0,)),((),())),preferred_element_type=F32)

def fwd_kernel(tile, flags, q_ref, k_ref, v_ref, sk_ref, sv_ref, start_ref, doc_ref, sdoc_ref, o_ref, lse_ref, km, vt, acc, top, total):
    i = pl.program_id(1)
    seg = k_ref.shape[0]
    lanes = lax.broadcasted_iota(jnp.int32, (1, 128), 1)
    masks = [(lanes < HEAD).astype(BF), (lanes >= HEAD).astype(BF)]
    @pl.when(i == 0)
    def _():
        for h in range(2):
            km[h, pl.ds(0, seg)] = k_ref[...] * masks[h]
            km[h, pl.ds(seg, 128)] = sk_ref[...] * masks[h]
        vt[:, pl.ds(0, seg)] = v_ref[...].T
        vt[:, pl.ds(seg, 128)] = sv_ref[...].T
    q = q_ref[...]
    allowed = sdoc_ref[...] == doc_ref[...]
    for h in range(2):
        s = dot_nt(km[h, pl.ds(seg, 128)], q)
        s = jnp.where(allowed, s, neg_big)
        m = jnp.max(s, axis=0, keepdims=True)
        p = jnp.where(allowed, jnp.exp(s - m), 0.0)
        top[h] = m
        total[h] = jnp.sum(p, axis=0, keepdims=True)
        acc[h] = dot_nn(vt[pl.ds(h * HEAD, HEAD), pl.ds(seg, 128)], p.astype(BF))
    def step(j, masked):
        at = pl.multiple_of(j * tile, tile)
        if masked:
            places = at + lax.broadcasted_iota(jnp.int32, (tile, tile), 0)
            mine = i * tile + lax.broadcasted_iota(jnp.int32, (tile, tile), 1)
            okay = (places <= mine) & (places >= start_ref[...])
        ss=[]
        for h in range(2):
            s = dot_nt(km[h, pl.ds(at, tile)], q)
            if masked:
                s = jnp.where(okay, s, neg_big)
            ss.append(s)
        for h in range(2):
            s = ss[h]
            m_old = top[h]
            m = jnp.maximum(m_old, jnp.max(s, axis=0, keepdims=True))
            p = jnp.exp(s - m)
            if masked:
                p = jnp.where(okay, p, 0.0)
            alpha = jnp.exp(m_old - m)
            top[h] = m
            total[h] = total[h] * alpha + jnp.sum(p, axis=0, keepdims=True)
            acc[h] = acc[h] * alpha + dot_nn(vt[pl.ds(h * HEAD, HEAD), pl.ds(at, tile)], p.astype(BF))
    count = pl.num_programs(1)
    def loop(j, _):
        flag = flags[i * count + j]
        @pl.when(flag == 2)
        def _(): step(j, False)
        @pl.when(flag == 1)
        def _(): step(j, True)
        return 0
    lax.fori_loop(0, i + 1, loop, 0)
    out = [acc[h] / total[h] for h in range(2)]
    o_ref[...] = jnp.concatenate(out, axis=0).T.astype(BF)
    for h in range(2):
        lse_ref[0, pl.ds(h, 1)] = top[h] + jnp.log(total[h])

def attn_fwd(q, k, v, sk, sv, start, doc, sdoc, flags, tile=512, offs=(0,0,0)):
    seg, = (q.shape[0],)
    pairs = sk.shape[1] // 128
    count = seg // tile
    row = lambda shape, f: pl.BlockSpec(shape, f)
    return pl.pallas_call(
        functools.partial(fwd_kernel, tile),
        grid_spec=pltpu.PrefetchScalarGridSpec(
            num_scalar_prefetch=1, grid=(pairs, count),
            in_specs=[
                row((tile,128), lambda h,i,f: (i,h+offs[0])),
                row((seg,128), lambda h,i,f: (0,h+offs[1])),
                row((seg,128), lambda h,i,f: (0,h+offs[2])),
                row((128,128), lambda h,i,f: (0,h)),
                row((128,128), lambda h,i,f: (0,h)),
                row((1,tile), lambda h,i,f: (0,i)),
                row((1,tile), lambda h,i,f: (0,i)),
                row((128,1), lambda h,i,f: (0,0)),
            ],
            out_specs=[row((tile,128), lambda h,i,f: (i,h)), row((1,2,tile), lambda h,i,f: (h,0,i))],
            scratch_shapes=[pltpu.VMEM((2,seg+128,128),BF), pltpu.VMEM((128,seg+128),BF), pltpu.VMEM((2,HEAD,tile),F32), pltpu.VMEM((2,1,tile),F32), pltpu.VMEM((2,1,tile),F32)],
        ),
        out_shape=[jax.ShapeDtypeStruct((seg,pairs*128),BF), jax.ShapeDtypeStruct((pairs,2,seg),F32)],
        compiler_params=pltpu.CompilerParams(vmem_limit_bytes=48*2**20),
    )(flags, q, k, v, sk, sv, start, doc, sdoc)

def bwd_kernel(tile, flags, q_ref, k_ref, v_ref, do_ref, o_ref, sk_ref, sv_ref, lse_ref, start_ref, doc_ref, sdoc_ref,
               dq_ref, dk_ref, dv_ref, dsk_ref, dsv_ref, qm, dom, dqt, delta):
    j = pl.program_id(1)
    seg = q_ref.shape[0]
    count = seg // tile
    lanes = lax.broadcasted_iota(jnp.int32, (1, 128), 1)
    masks = [(lanes < HEAD).astype(BF), (lanes >= HEAD).astype(BF)]
    @pl.when(j == 0)
    def _():
        dqt[...] = jnp.zeros_like(dqt)
        for h in range(2):
            qm[h] = q_ref[...] * masks[h]
            dom[h] = do_ref[...] * masks[h]
        def one(i, _):
            at = pl.multiple_of(i * tile, tile)
            prod = (do_ref[pl.ds(at, tile)].astype(F32) * o_ref[pl.ds(at, tile)].astype(F32)).T
            for h in range(2):
                delta[h, :, pl.ds(at, tile)] = jnp.sum(prod[h * HEAD:(h + 1) * HEAD], axis=0, keepdims=True)
            return 0
        lax.fori_loop(0, count, one, 0)
    def block(i, kt, k_blk, v_blk, okay):
        at = pl.multiple_of(i * tile, tile)
        gk = gv = None
        for h in range(2):
            qh = qm[h, pl.ds(at, tile)]
            dh = dom[h, pl.ds(at, tile)]
            s = dot_nt(k_blk, qh)
            dp = dot_nt(v_blk, dh)
            p = jnp.exp(s - lse_ref[0, pl.ds(h, 1), pl.ds(at, tile)])
            if okay is not None:
                p = jnp.where(okay, p, 0.0)
            ds = (p * (dp - delta[h, :, pl.ds(at, tile)])).astype(BF)
            a = dot_nn(p.astype(BF), dh)
            b = dot_nn(ds, qh)
            gv = a if gv is None else gv + a
            gk = b if gk is None else gk + b
            dqt[pl.ds(h * HEAD, HEAD), pl.ds(at, tile)] += dot_nn(kt[h * HEAD:(h + 1) * HEAD], ds)
        return gk, gv
    @pl.when(j < count)
    def _():
        at_k = pl.multiple_of(j * tile, tile)
        k_blk = k_ref[...]
        v_blk = v_ref[...]
        kt = k_blk.T
        def masked_of(i):
            places = at_k + lax.broadcasted_iota(jnp.int32, (tile, tile), 0)
            mine = i * tile + lax.broadcasted_iota(jnp.int32, (tile, tile), 1)
            return (places <= mine) & (places >= start_ref[:, pl.ds(pl.multiple_of(i * tile, tile), tile)])
        gk, gv = block(j, kt, k_blk, v_blk, masked_of(j))
        dkacc, dvacc = gk, gv
        def loop(i, carry):
            flag = flags[i * count + j]
            def full(c):
                gk, gv = block(i, kt, k_blk, v_blk, None)
                return c[0] + gk, c[1] + gv
            def part(c):
                gk, gv = block(i, kt, k_blk, v_blk, masked_of(i))
                return c[0] + gk, c[1] + gv
            return lax.switch(flag, [lambda c: c, part, full], carry)
        dkacc, dvacc = lax.fori_loop(j + 1, count, loop, (dkacc, dvacc))
        dk_ref[...] = dkacc.astype(BF)
        dv_ref[...] = dvacc.astype(BF)
    @pl.when(j == count)
    def _():
        kt = sk_ref[...].T
        def loop(i, carry):
            okay = sdoc_ref[...] == doc_ref[:, pl.ds(pl.multiple_of(i * tile, tile), tile)]
            gk, gv = block(i, kt, sk_ref[...], sv_ref[...], okay)
            return carry[0] + gk, carry[1] + gv
        z = jnp.zeros((128, 128), F32)
        a, b = lax.fori_loop(0, count, loop, (z, z))
        dsk_ref[...] = a.astype(BF)
        dsv_ref[...] = b.astype(BF)
        def fin(i, _):
            at = pl.multiple_of(i * tile, tile)
            dq_ref[pl.ds(at, tile)] = (dqt[:, pl.ds(at, tile)].T.astype(BF).astype(F32) * HEAD ** -0.5).astype(BF)
            return 0
        lax.fori_loop(0, count, fin, 0)

def attn_bwd(q, k, v, do, o, sk, sv, lse, start, doc, sdoc, flags, tile=512, offs=(0,0,0)):
    seg = q.shape[0]
    pairs = sk.shape[1] // 128
    count = seg // tile
    row = lambda shape, f: pl.BlockSpec(shape, f)
    last = count - 1
    return pl.pallas_call(
        functools.partial(bwd_kernel, tile),
        grid_spec=pltpu.PrefetchScalarGridSpec(
            num_scalar_prefetch=1, grid=(pairs, count + 1),
            in_specs=[
                row((seg,128), lambda h,j,f: (0,h+offs[0])),
                row((tile,128), lambda h,j,f: (jnp.minimum(j,last),h+offs[1])),
                row((tile,128), lambda h,j,f: (jnp.minimum(j,last),h+offs[2])),
                row((seg,128), lambda h,j,f: (0,h)),
                row((seg,128), lambda h,j,f: (0,h)),
                row((128,128), lambda h,j,f: (0,h)),
                row((128,128), lambda h,j,f: (0,h)),
                row((1,2,seg), lambda h,j,f: (h,0,0)),
                row((1,seg), lambda h,j,f: (0,0)),
                row((1,seg), lambda h,j,f: (0,0)),
                row((128,1), lambda h,j,f: (0,0)),
            ],
            out_specs=[row((seg,128), lambda h,j,f: (0,h)),
                       row((tile,128), lambda h,j,f: (jnp.minimum(j,last),h)),
                       row((tile,128), lambda h,j,f: (jnp.minimum(j,last),h)),
                       row((128,128), lambda h,j,f: (0,h)), row((128,128), lambda h,j,f: (0,h))],
            scratch_shapes=[pltpu.VMEM((2,seg,128),BF), pltpu.VMEM((2,seg,128),BF), pltpu.VMEM((128,seg),F32), pltpu.VMEM((2,1,seg),F32)],
        ),
        out_shape=[jax.ShapeDtypeStruct((seg,pairs*128),BF)]*3 + [jax.ShapeDtypeStruct((128,pairs*128),BF)]*2,
        compiler_params=pltpu.CompilerParams(vmem_limit_bytes=48*2**20),
    )(flags, q, k, v, do, o, sk, sv, lse, start, doc, sdoc)

def make_meta(doc, tile):
    seg=doc.shape[0]; count=seg//tile
    place=jnp.arange(seg,dtype=jnp.int32)
    new=jnp.concatenate([jnp.ones((1,),bool), doc[1:]!=doc[:-1]])
    start=lax.cummax(jnp.where(new,place,0))
    lo=doc[::tile]; hi=doc[tile-1::tile]
    i=jnp.arange(count)
    full=(lo[None,:]==hi[:,None])&(i[None,:]<i[:,None])
    none=(hi[None,:]<lo[:,None])
    flags=jnp.where(full,2,jnp.where(none,0,1)).astype(jnp.int32).reshape(-1)
    return start.reshape(1,seg), flags


X_FLIP = ((0, 1), (1, 0), (2, 3), (3, 2))
Y_FLIP = ((0, 2), (2, 0), (1, 3), (3, 1))
BOTH = ("rows", "seq")


def over_x(block):
    return lax.ppermute(block, "rows", X_FLIP)


def over_y(block):
    return lax.ppermute(block, "rows", Y_FLIP)


def other_core(block):
    return lax.ppermute(block, "fsdp", ((0, 1), (1, 0)))


def cut(field, axis, parts):
    size = field.shape[axis] // parts
    return [lax.slice_in_dim(field, n * size, (n + 1) * size, axis=axis) for n in range(parts)]


def gather(shard, axis, split):
    me = lax.axis_index("rows")
    block = lax.all_gather(shard, "seq", axis=axis, tiled=True)
    first, second = cut(block, split, 2)
    width = block.shape[axis]
    from_x, from_y = over_x(first), over_y(second)
    pieces = (
        (0, first, second),
        (1, from_x, over_x(second)),
        (2, over_y(first), from_y),
        (3, over_y(from_x), over_x(from_y)),
    )
    shape = list(block.shape)
    shape[axis] = width * 4
    whole = jnp.zeros(shape, block.dtype)
    half = block.shape[split] // 2
    for away, a, b in pieces:
        for n, part in enumerate((a, b)):
            at = [0] * len(shape)
            at[axis] = (me ^ away) * width
            at[split] = n * half
            whole = lax.dynamic_update_slice(whole, part, at)
    return whole


def scatter(partial, axis, split):
    me = lax.axis_index("rows")
    width = partial.shape[axis] // 4

    def block(field, away):
        return lax.dynamic_slice_in_dim(field, (me ^ away) * width, width, axis)

    first, second = cut(partial, split, 2)

    def plus(own, moved):
        return (own.astype(F32) + moved.astype(F32)).astype(BF)

    far_a = over_x(block(first, 3))
    far_b = over_y(block(second, 3))
    near_a = over_x(block(first, 1))
    near_b = over_y(block(second, 2))
    last_a = over_y(plus(block(first, 2), far_a))
    last_b = over_x(plus(block(second, 1), far_b))
    sum_a = block(first, 0).astype(F32) + near_a.astype(F32) + last_a.astype(F32)
    sum_b = block(second, 0).astype(F32) + near_b.astype(F32) + last_b.astype(F32)
    mine = jnp.concatenate((sum_a.astype(BF), sum_b.astype(BF)), axis=split)
    return lax.psum_scatter(mine, "seq", scatter_dimension=axis, tiled=True).astype(F32)


def exchange(field):
    count = lax.axis_size("seq")
    me = lax.axis_index("seq")
    core = lax.axis_index("fsdp")
    half = field.shape[2] // 2
    mine = lax.dynamic_slice_in_dim(field, core * half, half, 2)
    got = jnp.zeros_like(mine)
    own = lax.dynamic_slice_in_dim(mine, me, 1, 0)
    got = lax.dynamic_update_slice_in_dim(got, own, me, 0)
    for away in range(1, count):
        block = lax.dynamic_slice_in_dim(mine, lax.rem(me + away, count), 1, 0)
        moved = lax.ppermute(block, "seq", [(n, (n + away) % count) for n in range(count)])
        got = lax.dynamic_update_slice_in_dim(got, moved, lax.rem(me + count - away, count), 0)
    other = other_core(got)
    low_half = jnp.where(core == 0, got, other)
    high_half = jnp.where(core == 0, other, got)
    return jnp.concatenate((low_half, high_half), axis=2)


def shift_by(field, away):
    count = lax.axis_size("seq")
    perm = [(n, n + away) for n in range(count) if 0 <= n + away < count]
    return lax.ppermute(field, "seq", perm)


def both_halves(field):
    low = field.astype(BF)
    return low.astype(F32) + other_core(low).astype(F32)


def norm_forward(field, gain_vec, shift_vec):
    row_mean = jnp.mean(field, axis=-1, keepdims=True)
    centered = field - row_mean
    variance = jnp.mean(centered * centered, axis=-1, keepdims=True)
    scale = lax.rsqrt(variance + norm_eps)
    return (centered * scale * gain_vec + shift_vec).astype(BF), row_mean, scale


def norm_backward(field, row_mean, scale, gain_vec, grad):
    unit = (field - row_mean) * scale
    scaled = grad * gain_vec
    mean_one = jnp.mean(scaled, axis=-1, keepdims=True)
    mean_two = jnp.mean(scaled * unit, axis=-1, keepdims=True)
    d_field = scale * (scaled - mean_one - unit * mean_two)
    return d_field, jnp.sum(grad * unit, axis=0), jnp.sum(grad, axis=0)


def mm(a, b):
    return dot_nn(a, b)


def mm_tn(a, b):
    return lax.dot_general(a, b, (((0,), (0,)), ((), ())), preferred_element_type=F32)


def mm_nt(a, b):
    return dot_nt(a, b)


def layer_by_segment(
    states,
    doc_ids,
    w_qkv,
    w_out,
    w_up,
    w_down,
    bias_qv,
    bias_out,
    bias_up,
    bias_down,
    gain_one,
    shift_one,
    gain_two,
    shift_two,
    cotangent,
):
    segs, width, model = states.shape[1:]
    seg_len = segs * width
    place = lax.axis_index("seq")
    half = w_qkv.shape[2]
    hidden_units = w_up.shape[1]
    tile = 512

    small = (bias_qv, bias_out, bias_up, bias_down, gain_one, shift_one, gain_two, shift_two)
    sizes = [item.size for item in small]
    packed = lax.all_gather(jnp.concatenate([item.reshape(-1) for item in small]), BOTH, axis=0)
    cuts = []
    at = 0
    for size in sizes:
        cuts.append(packed[:, at : at + size].astype(F32))
        at += size
    shards = packed.shape[0]

    def spread_last(field, lead):
        return jnp.moveaxis(field.reshape(shards, *lead, -1), 0, len(lead)).reshape(-1)

    bias_pair = jnp.moveaxis(cuts[0].reshape(shards, 2, half // HEAD, -1), 0, 2).reshape(2, half)
    bias_o = cuts[1].reshape(-1)
    bias_u = spread_last(cuts[2], (hidden_units // HEAD,))
    bias_d = cuts[3].reshape(-1)
    gain_a, shift_a, gain_b, shift_b = [item.reshape(-1) for item in cuts[4:]]

    qkv_full = gather(w_qkv, 1, 2)
    tokens = exchange(states[0]).reshape(seg_len, model)
    out_full = gather(w_out, 1, 0)
    up_full = gather(w_up, 0, 1)
    down_full = gather(w_down, 1, 0)
    grad_out = exchange(cotangent[0]).reshape(seg_len, model)

    docs = doc_ids[0]
    my_docs = lax.dynamic_index_in_dim(docs, place, 0, keepdims=False)
    start, flags = make_meta(my_docs, tile)
    tails = docs[:, seg_len - SUMM :]
    before_one = lax.dynamic_index_in_dim(tails, jnp.maximum(place - 1, 0), 0, keepdims=False)
    before_two = lax.dynamic_index_in_dim(tails, jnp.maximum(place - 2, 0), 0, keepdims=False)
    sum_docs = jnp.concatenate(
        (
            jnp.where(place >= 1, before_one, -1),
            jnp.where(place >= 2, before_two, -1),
            jnp.full((128 - 2 * SUMM,), -1, jnp.int32),
        )
    ).reshape(128, 1)
    doc_row = my_docs.reshape(1, seg_len)

    tokens_f = tokens.astype(F32)
    normed_one, mean_one, scale_one = norm_forward(tokens_f, gain_a, shift_a)
    query = ((mm(normed_one, qkv_full[0]) + bias_pair[0]) * HEAD**-0.5).astype(BF)
    keys = mm(normed_one, qkv_full[1]).astype(BF)
    values = (mm(normed_one, qkv_full[2]) + bias_pair[1]).astype(BF)
    tail = jnp.stack((keys[seg_len - SUMM :], values[seg_len - SUMM :]))
    lent = jnp.concatenate((shift_by(tail, 1), shift_by(tail, 2)), axis=1)
    lent = jnp.pad(lent, ((0, 0), (0, 128 - 2 * SUMM), (0, 0)))
    mixed, log_sum = attn_fwd(
        query, keys, values, lent[0], lent[1], start, doc_row, sum_docs, flags, tile
    )
    hidden = tokens_f + both_halves(mm(mixed, out_full)) + bias_o
    normed_two, mean_two, scale_two = norm_forward(hidden, gain_b, shift_b)
    up_proj = mm(normed_two, up_full) + bias_u
    bell = jnp.exp(-0.5 * up_proj * up_proj)
    area = 0.5 * (1.0 + lax.erf(up_proj * (0.5**0.5)))
    activated = (up_proj * area).astype(BF)
    slope = (area + up_proj * bell * 0.3989422804014327).astype(BF)

    grad_w_down = scatter(mm_tn(activated, grad_out).astype(BF), 1, 0)
    d_up = (mm_nt(grad_out, down_full) * slope.astype(F32)).astype(BF)
    grad_w_up = scatter(mm_tn(normed_two, d_up).astype(BF), 0, 1)
    d_norm_two = both_halves(mm_nt(d_up, up_full))
    d_hidden_ln, grad_gain_two, grad_shift_two = norm_backward(
        hidden, mean_two, scale_two, gain_b, d_norm_two
    )
    d_hidden = grad_out.astype(F32) + d_hidden_ln
    d_hidden_low = d_hidden.astype(BF)
    d_mixed = mm_nt(d_hidden_low, out_full).astype(BF)
    grad_w_out = scatter(mm_tn(mixed, d_hidden_low).astype(BF), 1, 0)

    out_tokens = (hidden + both_halves(mm(activated, down_full)) + bias_d).astype(BF)
    out_states = exchange(out_tokens.reshape(segs, width, model))[None]

    d_pre, d_keys, d_values, d_lent_k, d_lent_v = attn_bwd(
        query, keys, values, d_mixed, mixed, lent[0], lent[1], log_sum, start, doc_row, sum_docs, flags, tile
    )
    d_lent = jnp.stack((d_lent_k, d_lent_v))
    back = shift_by(d_lent[:, :SUMM], -1).astype(F32) + shift_by(
        d_lent[:, SUMM : 2 * SUMM], -2
    ).astype(F32)
    ends = jnp.stack((d_keys[seg_len - SUMM :], d_values[seg_len - SUMM :])).astype(F32) + back
    ends = ends.astype(BF)
    d_keys = lax.dynamic_update_slice(d_keys, ends[0], (seg_len - SUMM, 0))
    d_values = lax.dynamic_update_slice(d_values, ends[1], (seg_len - SUMM, 0))
    d_qkv = (d_pre, d_keys, d_values)
    grad_w_qkv = scatter(
        jnp.stack([mm_tn(normed_one, item).astype(BF) for item in d_qkv]), 1, 2
    )
    d_norm_one = both_halves(
        mm_nt(d_pre, qkv_full[0]) + mm_nt(d_keys, qkv_full[1]) + mm_nt(d_values, qkv_full[2])
    )
    d_tokens_ln, grad_gain_one, grad_shift_one = norm_backward(
        tokens_f, mean_one, scale_one, gain_a, d_norm_one
    )
    grad_tokens = (d_hidden + d_tokens_ln).astype(BF)
    grad_states = exchange(grad_tokens.reshape(segs, width, model))[None]

    def column_sum(field):
        return jnp.sum(field.astype(F32), axis=0)

    sums = (
        jnp.moveaxis(
            jnp.stack((column_sum(d_pre), column_sum(d_values))).reshape(2, half // HEAD, shards, -1), 2, 0
        ),
        column_sum(d_hidden),
        jnp.moveaxis(column_sum(d_up).reshape(hidden_units // HEAD, shards, -1), 1, 0),
        column_sum(grad_out),
        grad_gain_one,
        grad_shift_one,
        grad_gain_two,
        grad_shift_two,
    )
    vector = jnp.concatenate([item.reshape(shards, -1) for item in sums], axis=1)
    vector = lax.psum_scatter(vector, BOTH, scatter_dimension=0, tiled=False)
    small_grads = []
    at = 0
    for item, size in zip(small, sizes):
        small_grads.append(vector[at : at + size].reshape(item.shape))
        at += size
    return (out_states, grad_states, grad_w_qkv, grad_w_out, grad_w_up, grad_w_down, *small_grads)


def solution(mesh):
    whole_segments = mesh.shape["seq"] == SEGS and mesh.shape["rows"] == 4
    return jax.shard_map(
        layer_by_segment if whole_segments else local,
        mesh=mesh,
        in_specs=(
            P("rows", None, "seq", None),
            P("rows", None, None),
            P(None, ("rows", "seq"), "fsdp"),
            P("fsdp", ("rows", "seq")),
            P(("rows", "seq"), "fsdp"),
            P("fsdp", ("rows", "seq")),
            P(None, "fsdp", ("rows", "seq")),
            P(("rows", "seq")),
            P("fsdp", ("rows", "seq")),
            P(("rows", "seq")),
            P(("rows", "seq")),
            P(("rows", "seq")),
            P(("rows", "seq")),
            P(("rows", "seq")),
            P("rows", None, "seq", None),
        ),
        out_specs=(
            P("rows", None, "seq", None),
            P("rows", None, "seq", None),
            P(None, ("rows", "seq"), "fsdp"),
            P("fsdp", ("rows", "seq")),
            P(("rows", "seq"), "fsdp"),
            P("fsdp", ("rows", "seq")),
            P(None, "fsdp", ("rows", "seq")),
            P(("rows", "seq")),
            P("fsdp", ("rows", "seq")),
            P(("rows", "seq")),
            P(("rows", "seq")),
            P(("rows", "seq")),
            P(("rows", "seq")),
            P(("rows", "seq")),
        ),
        check_vma=False,
    )
```

```python
import functools

import jax
import jax.numpy as jnp
from jax import lax
from jax.experimental import pallas as pl
from jax.experimental.pallas import tpu as pltpu
from jax.sharding import PartitionSpec as P

HEAD = 64
SUMM = 50
SEGS = 4
F32 = jnp.float32
BF = jnp.bfloat16
SMALL_COST = pl.CostEstimate(flops=1000, bytes_accessed=1000, transcendentals=0)


neg_big = -1e30
norm_eps = 1e-05


def spread(block, axis, source):
    block = jnp.where(lax.axis_index(axis) == source, block, jnp.zeros_like(block))
    return lax.psum(block, axis)


def layer_norm(field, gain_vec, shift_vec):
    row_mean = jnp.mean(field, axis=-1, keepdims=True)
    centered = field - row_mean
    variance = jnp.mean(centered * centered, axis=-1, keepdims=True)
    return centered * lax.rsqrt(variance + norm_eps) * gain_vec + shift_vec


def gelu_exact(field):
    return jax.nn.gelu(field, approximate=False)


def earlier(field, offset, fill_value):
    widths = tuple(((offset, 0) if dim_index == 1 else (0, 0) for dim_index in range(field.ndim)))
    return jnp.pad(field, widths, constant_values=fill_value)[:, : field.shape[1]]


def later(field, offset):
    widths = tuple(((0, offset) if dim_index == 1 else (0, 0) for dim_index in range(field.ndim)))
    return jnp.pad(field, widths)[:, offset:]


def lead(field):
    return jnp.moveaxis(field, 1, 0)


def halves(field):
    return lax.psum(field.astype(jnp.bfloat16), "fsdp").astype(jnp.float32)


def local(
    states,
    doc_ids,
    w_qkv,
    w_out,
    w_up,
    w_down,
    bias_qv,
    bias_out,
    bias_up,
    bias_down,
    gain_one,
    shift_one,
    gain_two,
    shift_two,
    cotangent,
):
    attn_full = (
        lax.all_gather(w_qkv, ("rows", "seq"), axis=1, tiled=True),
        lax.all_gather(w_out, ("rows", "seq"), axis=1, tiled=True),
        lax.all_gather(bias_qv, ("rows", "seq"), axis=2, tiled=True),
        lax.all_gather(gain_one, ("rows", "seq"), axis=0, tiled=True),
        lax.all_gather(shift_one, ("rows", "seq"), axis=0, tiled=True),
        lax.all_gather(bias_out, ("rows", "seq"), axis=0, tiled=True),
    )
    qkv_full, out_full, bqv_full, gain_a, shift_a, bias_o = attn_full
    rows_dev, seg_count, width, model = states.shape
    seq_count = lax.axis_size("seq")
    seq_place = lax.axis_index("seq")
    seg_len = width * seq_count
    half_width = qkv_full.shape[2]
    heads_loc = half_width // HEAD
    score_scale = HEAD ** (-0.5)
    states_f = states.astype(jnp.float32)
    normed_f, norm_one_back = jax.vjp(
        layer_norm, states_f, gain_a.astype(jnp.float32), shift_a.astype(jnp.float32)
    )
    normed_one = normed_f.astype(jnp.bfloat16)
    projected = jnp.einsum(
        "rsid,kde->krsie", normed_one, qkv_full, preferred_element_type=jnp.float32
    )
    bias_pair = bqv_full.astype(jnp.float32).reshape(2, half_width)
    query = ((projected[0] + bias_pair[0]) * score_scale).astype(jnp.bfloat16)
    keys = projected[1].astype(jnp.bfloat16)
    values = (projected[2] + bias_pair[1]).astype(jnp.bfloat16)
    tail = jnp.stack((keys[:, :, width - SUMM :], values[:, :, width - SUMM :]))
    summary = spread(tail, "seq", seq_count - 1)
    sum_keys = jnp.concatenate((earlier(summary[0], 1, 0.0), earlier(summary[0], 2, 0.0)), axis=2)
    sum_values = jnp.concatenate((earlier(summary[1], 1, 0.0), earlier(summary[1], 2, 0.0)), axis=2)
    sum_src = doc_ids[:, :, seg_len - SUMM :]
    sum_docs = jnp.concatenate((earlier(sum_src, 1, -1), earlier(sum_src, 2, -1)), axis=2)
    sum_k5 = sum_keys.reshape(rows_dev, seg_count, 2 * SUMM, heads_loc, HEAD)
    sum_v5 = sum_values.reshape(rows_dev, seg_count, 2 * SUMM, heads_loc, HEAD)
    first_pos = seq_place * width
    query_docs = lax.dynamic_slice_in_dim(doc_ids, first_pos, width, 2)
    query_pos = first_pos + jnp.arange(width, dtype=jnp.int32)
    query5 = query.reshape(rows_dev, seg_count, width, heads_loc, HEAD)
    sum_allowed = (query_docs[:, :, :, None] == sum_docs[:, :, None, :])[:, :, None]
    sum_scores = jnp.einsum(
        "rsihe,rsjhe->rshij", query5, sum_k5, preferred_element_type=jnp.float32
    )
    sum_scores = jnp.where(sum_allowed, sum_scores, neg_big)
    start_max = jnp.max(sum_scores, axis=-1)
    start_exp = jnp.where(sum_allowed, jnp.exp(sum_scores - start_max[..., None]), 0.0)
    start_sum = jnp.sum(start_exp, axis=-1)
    start_acc = jnp.einsum(
        "rshij,rsjhe->rsihe",
        start_exp.astype(jnp.bfloat16),
        sum_v5,
        preferred_element_type=jnp.float32,
    )
    key_piece = lax.all_gather(keys, "seq", axis=2, tiled=True)
    value_piece = lax.all_gather(values, "seq", axis=2, tiled=True)
    count = key_piece.shape[2]
    key5 = key_piece.reshape(rows_dev, seg_count, count, heads_loc, HEAD)
    value5 = value_piece.reshape(rows_dev, seg_count, count, heads_loc, HEAD)
    key_pos = jnp.arange(count, dtype=jnp.int32)
    causal = (key_pos[None, :] <= query_pos[:, None])[None, None, None]
    allowed = causal & (query_docs[:, :, :, None] == doc_ids[:, :, None, :])[:, :, None]
    scores = jnp.einsum("rsihe,rsjhe->rshij", query5, key5, preferred_element_type=jnp.float32)
    scores = jnp.where(allowed, scores, neg_big)
    new_max = jnp.maximum(start_max, jnp.max(scores, axis=-1))
    factor = jnp.exp(start_max - new_max)
    exponent = jnp.where(allowed, jnp.exp(scores - new_max[..., None]), 0.0)
    new_sum = start_sum * factor + jnp.sum(exponent, axis=-1)
    gained = jnp.einsum(
        "rshij,rsjhe->rsihe",
        exponent.astype(jnp.bfloat16),
        value5,
        preferred_element_type=jnp.float32,
    )
    new_acc = start_acc * jnp.swapaxes(factor, 2, 3)[..., None] + gained
    log_sum = new_max + jnp.log(new_sum)
    mixed_f = new_acc / jnp.swapaxes(new_sum, 2, 3)[..., None]
    mixed = mixed_f.reshape(rows_dev, seg_count, width, half_width).astype(jnp.bfloat16)
    attn_lin = halves(
        jnp.einsum("rsie,ed->rsid", mixed, out_full, preferred_element_type=jnp.float32)
    )
    hidden = states_f + attn_lin + bias_o.astype(jnp.float32)
    ffn_full = (
        lax.all_gather(w_up, ("rows", "seq"), axis=0, tiled=True),
        lax.all_gather(w_down, ("rows", "seq"), axis=1, tiled=True),
        lax.all_gather(bias_up, ("rows", "seq"), axis=1, tiled=True),
        lax.all_gather(gain_two, ("rows", "seq"), axis=0, tiled=True),
        lax.all_gather(shift_two, ("rows", "seq"), axis=0, tiled=True),
        lax.all_gather(bias_down, ("rows", "seq"), axis=0, tiled=True),
    )
    up_full, down_full, bias_u, gain_b, shift_b, bias_d = ffn_full
    normed_two_f, norm_two_back = jax.vjp(
        layer_norm, hidden, gain_b.astype(jnp.float32), shift_b.astype(jnp.float32)
    )
    normed_two = normed_two_f.astype(jnp.bfloat16)
    up_proj = jnp.einsum(
        "rsid,df->rsif", normed_two, up_full, preferred_element_type=jnp.float32
    ) + bias_u.astype(jnp.float32).reshape(-1)
    activated_f, gelu_back = jax.vjp(gelu_exact, up_proj)
    activated = activated_f.astype(jnp.bfloat16)
    down_proj = halves(
        jnp.einsum("rsif,fd->rsid", activated, down_full, preferred_element_type=jnp.float32)
    )
    out_states = (hidden + down_proj + bias_d.astype(jnp.float32)).astype(jnp.bfloat16)
    up_back, down_back = (
        lax.all_gather(w_up, ("rows", "seq"), axis=0, tiled=True),
        lax.all_gather(w_down, ("rows", "seq"), axis=1, tiled=True),
    )
    qkv_back, out_back = (
        lax.all_gather(w_qkv, ("rows", "seq"), axis=1, tiled=True),
        lax.all_gather(w_out, ("rows", "seq"), axis=1, tiled=True),
    )
    grad_out = cotangent.astype(jnp.float32)
    grad_bias_down = jnp.sum(grad_out, axis=(0, 1, 2))
    grad_w_down = jnp.einsum(
        "rsif,rsid->fd", activated, cotangent, preferred_element_type=jnp.float32
    )
    d_act = jnp.einsum("rsid,fd->rsif", cotangent, down_back, preferred_element_type=jnp.float32)
    (d_up,) = gelu_back(d_act)
    d_up_low = d_up.astype(jnp.bfloat16)
    grad_bias_up = jnp.sum(d_up_low, axis=(0, 1, 2), dtype=jnp.float32).reshape(bias_u.shape)
    grad_w_up = jnp.einsum(
        "rsid,rsif->df", normed_two, d_up_low, preferred_element_type=jnp.float32
    )
    d_norm_two = halves(
        jnp.einsum("rsif,df->rsid", d_up_low, up_back, preferred_element_type=jnp.float32)
    )
    d_hidden_ln, grad_gain_two, grad_shift_two = norm_two_back(d_norm_two)
    d_hidden = grad_out + d_hidden_ln
    ffn_grads = (
        lax.psum_scatter(grad_w_up, ("rows", "seq"), scatter_dimension=0, tiled=True),
        lax.psum_scatter(grad_w_down, ("rows", "seq"), scatter_dimension=1, tiled=True),
        lax.psum_scatter(grad_bias_up, ("rows", "seq"), scatter_dimension=1, tiled=True),
        lax.psum_scatter(grad_gain_two, ("rows", "seq"), scatter_dimension=0, tiled=True),
        lax.psum_scatter(grad_shift_two, ("rows", "seq"), scatter_dimension=0, tiled=True),
        lax.psum_scatter(grad_bias_down, ("rows", "seq"), scatter_dimension=0, tiled=True),
    )
    grad_bias_out = jnp.sum(d_hidden, axis=(0, 1, 2))
    d_hidden_low = d_hidden.astype(jnp.bfloat16)
    grad_w_out = jnp.einsum(
        "rsie,rsid->ed", mixed, d_hidden_low, preferred_element_type=jnp.float32
    )
    d_mixed = jnp.einsum(
        "rsid,ed->rsie", d_hidden_low, out_back, preferred_element_type=jnp.float32
    ).astype(jnp.bfloat16)
    d_mixed5 = d_mixed.reshape(rows_dev, seg_count, width, heads_loc, HEAD)
    keys_all, values_all = (
        lax.all_gather(keys, "seq", axis=2, tiled=True),
        lax.all_gather(values, "seq", axis=2, tiled=True),
    )
    key_lead = lead(keys_all.reshape(rows_dev, seg_count, seg_len, heads_loc, HEAD))
    value_lead = lead(values_all.reshape(rows_dev, seg_count, seg_len, heads_loc, HEAD))
    query_lead = lead(query5)
    grad_lead = lead(d_mixed5)
    key_positions = jnp.arange(seg_len, dtype=jnp.int32)

    def segment_back(seg_items):
        q_seg, do_seg, lse_seg, qdoc_seg, k_seg, v_seg, kdoc_seg, sk_seg, sv_seg, sdoc_seg = (
            seg_items
        )
        causal = (key_positions[None, :] <= query_pos[:, None])[None, None]
        allowed = causal & (qdoc_seg[:, :, None] == kdoc_seg[:, None, :])[:, None]
        scores = jnp.einsum("rihe,rjhe->rhij", q_seg, k_seg, preferred_element_type=jnp.float32)
        attn_probs = jnp.where(allowed, jnp.exp(scores - lse_seg[..., None]), 0.0)
        d_probs = jnp.einsum("rihe,rjhe->rhij", do_seg, v_seg, preferred_element_type=jnp.float32)
        summ_allowed = (qdoc_seg[:, :, None] == sdoc_seg[:, None, :])[:, None]
        summ_scores = jnp.einsum(
            "rihe,rjhe->rhij", q_seg, sk_seg, preferred_element_type=jnp.float32
        )
        summ_probs = jnp.where(summ_allowed, jnp.exp(summ_scores - lse_seg[..., None]), 0.0)
        summ_dprobs = jnp.einsum(
            "rihe,rjhe->rhij", do_seg, sv_seg, preferred_element_type=jnp.float32
        )
        delta = jnp.sum(attn_probs * d_probs, axis=-1) + jnp.sum(summ_probs * summ_dprobs, axis=-1)
        d_scores = (attn_probs * (d_probs - delta[..., None])).astype(jnp.bfloat16)
        d_summ = (summ_probs * (summ_dprobs - delta[..., None])).astype(jnp.bfloat16)
        d_query = jnp.einsum("rhij,rjhe->rihe", d_scores, k_seg, preferred_element_type=jnp.float32)
        d_query = d_query + jnp.einsum(
            "rhij,rjhe->rihe", d_summ, sk_seg, preferred_element_type=jnp.float32
        )
        d_sum_keys = jnp.einsum(
            "rhij,rihe->rjhe", d_summ, q_seg, preferred_element_type=jnp.float32
        )
        d_sum_values = jnp.einsum(
            "rhij,rihe->rjhe",
            summ_probs.astype(jnp.bfloat16),
            do_seg,
            preferred_element_type=jnp.float32,
        )
        return (d_query, d_scores, attn_probs.astype(jnp.bfloat16), d_sum_keys, d_sum_values, delta)

    seg_inputs = (
        query_lead,
        grad_lead,
        lead(log_sum),
        lead(query_docs),
        key_lead,
        value_lead,
        lead(doc_ids),
        lead(sum_k5),
        lead(sum_v5),
        lead(sum_docs),
    )
    d_query_lead, d_scores_all, probs_all, d_sk_lead, d_sv_lead, delta_lead = lax.map(
        segment_back, seg_inputs
    )
    d_key_part = jnp.einsum(
        "srhij,srihe->jrshe", d_scores_all, query_lead, preferred_element_type=jnp.float32
    )
    d_value_part = jnp.einsum(
        "srhij,srihe->jrshe", probs_all, grad_lead, preferred_element_type=jnp.float32
    )
    key_grads = lax.psum_scatter(
        jnp.stack((d_key_part, d_value_part), axis=3)
        .reshape(width * lax.axis_size("seq"), rows_dev, seg_count, 2, half_width)
        .astype(jnp.bfloat16),
        "seq",
        scatter_dimension=0,
        tiled=True,
    ).astype(jnp.float32)
    key_grads = jnp.transpose(key_grads, (3, 1, 2, 0, 4))
    d_sk = jnp.moveaxis(d_sk_lead, 0, 1).reshape(rows_dev, seg_count, 2 * SUMM, half_width)
    d_sv = jnp.moveaxis(d_sv_lead, 0, 1).reshape(rows_dev, seg_count, 2 * SUMM, half_width)
    src_keys = later(d_sk[:, :, :SUMM], 1) + later(d_sk[:, :, SUMM:], 2)
    src_values = later(d_sv[:, :, :SUMM], 1) + later(d_sv[:, :, SUMM:], 2)
    summ_grads = lax.psum(jnp.stack((src_keys, src_values)).astype(jnp.bfloat16), "seq").astype(
        jnp.float32
    )
    owner_grads = jnp.where(seq_place == seq_count - 1, summ_grads, 0.0)
    owner_grads = jnp.pad(owner_grads, ((0, 0), (0, 0), (0, 0), (width - SUMM, 0), (0, 0)))
    key_grads = key_grads + owner_grads
    d_keys_low = key_grads[0].astype(jnp.bfloat16)
    d_values_low = key_grads[1].astype(jnp.bfloat16)
    d_query = jnp.moveaxis(d_query_lead, 0, 1).reshape(rows_dev, seg_count, width, half_width)
    d_query_low = d_query.astype(jnp.bfloat16)
    d_pre = (d_query_low.astype(jnp.float32) * score_scale).astype(jnp.bfloat16)
    grad_bias_qv = jnp.stack(
        (
            jnp.sum(d_pre, axis=(0, 1, 2), dtype=jnp.float32),
            jnp.sum(d_values_low, axis=(0, 1, 2), dtype=jnp.float32),
        )
    ).reshape(bqv_full.shape)
    d_qkv = jnp.stack((d_pre, d_keys_low, d_values_low))
    grad_w_qkv = jnp.einsum(
        "rsid,krsie->kde", normed_one, d_qkv, preferred_element_type=jnp.float32
    )
    d_norm_one = halves(
        jnp.einsum("krsie,kde->rsid", d_qkv, qkv_back, preferred_element_type=jnp.float32)
    )
    d_states_ln, grad_gain_one, grad_shift_one = norm_one_back(d_norm_one)
    grad_states = (d_hidden + d_states_ln).astype(jnp.bfloat16)
    attn_grads = (
        lax.psum_scatter(grad_w_qkv, ("rows", "seq"), scatter_dimension=1, tiled=True),
        lax.psum_scatter(grad_w_out, ("rows", "seq"), scatter_dimension=1, tiled=True),
        lax.psum_scatter(grad_bias_qv, ("rows", "seq"), scatter_dimension=2, tiled=True),
        lax.psum_scatter(grad_gain_one, ("rows", "seq"), scatter_dimension=0, tiled=True),
        lax.psum_scatter(grad_shift_one, ("rows", "seq"), scatter_dimension=0, tiled=True),
        lax.psum_scatter(grad_bias_out, ("rows", "seq"), scatter_dimension=0, tiled=True),
    )
    return (
        out_states,
        grad_states,
        attn_grads[0],
        attn_grads[1],
        ffn_grads[0],
        ffn_grads[1],
        attn_grads[2],
        attn_grads[5],
        ffn_grads[2],
        ffn_grads[5],
        attn_grads[3],
        attn_grads[4],
        ffn_grads[3],
        ffn_grads[4],
    )


def opening_kernel(w_ref, s_ref, v_ref, whole_ref, tokens_ref, vectors_ref, z_send, z_recv, x_send, x_recv, y_send, y_recv,
                   fx_send, fx_recv, fy_send, fy_recv, t_send, t_recv, c_send, c_recv, v_send, v_recv, own):
    rows, place, core = lax.axis_index("rows"), lax.axis_index("seq"), lax.axis_index("fsdp")
    count = s_ref.shape[0]
    depth = w_ref.shape[1]
    half = w_ref.shape[2] // 2
    width = s_ref.shape[2] // 2
    steps = count - 1

    def at(row, seq, fsdp=None):
        return (row, seq, core if fsdp is None else fsdp)

    def hail(device):
        pl.semaphore_signal(barrier, inc=1, device_id=device, device_id_type=pl.DeviceIdType.MESH)

    barrier = pltpu.get_barrier_semaphore()
    for away in range(4):
        for along in range(count):
            if away or along:
                hail(at(rows ^ away, lax.rem(place + along, count)))
    hail(at(rows, place, 1 - core))
    pl.semaphore_wait(barrier, 4 * count)

    def shard(ref, row, seq, cut=None):
        first = pl.multiple_of((row * count + seq) * depth, depth)
        if cut is None:
            return ref.at[:, pl.ds(first, depth)]
        return ref.at[:, pl.ds(first, depth), pl.ds(cut * half, half)]

    def remote(src, dst, send, recv, device):
        return pltpu.make_async_remote_copy(
            src_ref=src, dst_ref=dst, send_sem=send, recv_sem=recv, device_id=device,
            device_id_type=pl.DeviceIdType.MESH,
        )

    x_peer, y_peer = rows ^ 1, rows ^ 2

    def spread(t, side, seq, src):
        mine = shard(whole_ref, rows, seq)
        src = mine if src is None else src
        return (
            remote(src, mine, x_send.at[t, side], x_recv.at[t, side], at(x_peer, place)),
            remote(src, mine, y_send.at[t, side], y_recv.at[t, side], at(y_peer, place)),
        )

    def arrived(t, side, seq):
        from_x, from_y = shard(whole_ref, x_peer, seq), shard(whole_ref, y_peer, seq)
        return (
            remote(from_x, from_x, x_send.at[t, side], x_recv.at[t, side], at(x_peer, place)),
            remote(from_y, from_y, y_send.at[t, side], y_recv.at[t, side], at(y_peer, place)),
        )

    def onward(t, side, seq):
        a, b = shard(whole_ref, x_peer, seq, 0), shard(whole_ref, y_peer, seq, 1)
        return (
            remote(a, a, fy_send.at[t, side], fy_recv.at[t, side], at(y_peer, place)),
            remote(b, b, fx_send.at[t, side], fx_recv.at[t, side], at(x_peer, place)),
        )

    def far(t, side, seq):
        a, b = shard(whole_ref, rows ^ 3, seq, 0), shard(whole_ref, rows ^ 3, seq, 1)
        return (
            remote(a, a, fy_send.at[t, side], fy_recv.at[t, side], at(y_peer, place)),
            remote(b, b, fx_send.at[t, side], fx_recv.at[t, side], at(x_peer, place)),
        )

    def along_z(t, side, seq, src):
        mine = shard(whole_ref, rows, seq)
        to = place + 1 if side == 0 else place - 1
        return remote(mine if src is None else src, mine, z_send.at[t, side], z_recv.at[t, side], at(rows, to))

    def origin(t, side):
        return place - t if side == 0 else place + t

    def has(t, side):
        return origin(t, side) >= 0 if side == 0 else origin(t, side) < count

    def has_next(side):
        return place + 1 < count if side == 0 else place >= 1

    for side in range(2):
        @pl.when(has_next(side))
        def _(side=side):
            along_z(1, side, place, w_ref).start()
    for copy in spread(0, 0, place, w_ref):
        copy.start()
    local = pltpu.make_async_copy(w_ref, shard(whole_ref, rows, place), own.at[0])
    local.start()
    vectors = []
    for away in range(4):
        for along in range(count):
            if away or along:
                mine = rows * count + place
                copy = remote(
                    v_ref, vectors_ref.at[mine], v_send.at[away, along], v_recv.at[away, along],
                    at(rows ^ away, lax.rem(place + along, count)),
                )
                copy.start()
                vectors.append(copy)
    local_v = pltpu.make_async_copy(v_ref, vectors_ref.at[rows * count + place], own.at[1])
    local_v.start()

    columns = pl.ds(pl.multiple_of(core * width, width), width)

    def token_copy(along):
        to = lax.rem(place + along, count)
        return remote(
            s_ref.at[to, :, columns], tokens_ref.at[place, :, columns], t_send.at[along], t_recv.at[along], at(rows, to)
        )

    def token_got(along):
        start = lax.rem(place + count - along, count)
        view = tokens_ref.at[start, :, columns]
        return (
            remote(view, view, t_send.at[along], t_recv.at[along], at(rows, start)),
            remote(view, view, c_send.at[along], c_recv.at[along], at(rows, place, 1 - core)),
        )

    def token_far(along):
        start = lax.rem(place + count - along, count)
        view = tokens_ref.at[start, :, pl.ds(pl.multiple_of((1 - core) * width, width), width)]
        return remote(view, view, c_send.at[along], c_recv.at[along], at(rows, place, 1 - core))

    local_t = pltpu.make_async_copy(s_ref.at[place], tokens_ref.at[place], own.at[2])
    local_t.start()

    def pass_on(t, side, seq):
        for got in arrived(t, side, seq):
            got.wait_recv()
        for copy in onward(t, side, seq):
            copy.start()

    for t in range(1, steps + 1):
        for side in range(2):
            @pl.when(has(t, side))
            def _(t=t, side=side):
                seq = origin(t, side)
                along_z(t, side, seq, None).wait_recv()
                if t < steps:
                    @pl.when(has_next(side))
                    def _():
                        along_z(t + 1, side, seq, None).start()
                for copy in spread(t, side, seq, None):
                    copy.start()
        if t == 1:
            for along in range(1, count):
                token_copy(along).start()
            pass_on(0, 0, place)
        else:
            for side in range(2):
                @pl.when(has(t - 1, side))
                def _(t=t, side=side):
                    pass_on(t - 1, side, origin(t - 1, side))
    for side in range(2):
        @pl.when(has(steps, side))
        def _(side=side):
            pass_on(steps, side, origin(steps, side))

    for along in range(1, count):
        got, on = token_got(along)
        got.wait_recv()
        on.start()

    def settle(t, side, seq, src):
        for copy in spread(t, side, seq, src):
            copy.wait_send()
        for copy in onward(t, side, seq):
            copy.wait_send()
        for got in far(t, side, seq):
            got.wait_recv()

    settle(0, 0, place, w_ref)
    for t in range(1, steps + 1):
        for side in range(2):
            @pl.when(has(t, side))
            def _(t=t, side=side):
                settle(t, side, origin(t, side), None)

            @pl.when(has(t - 1, side) & has_next(side))
            def _(t=t, side=side):
                along_z(t, side, origin(t - 1, side), w_ref if t == 1 else None).wait_send()
    for copy in vectors:
        copy.wait_send()
    for away in range(4):
        for along in range(count):
            if away or along:
                start = (rows ^ away) * count + lax.rem(place + count - along, count)
                view = vectors_ref.at[start]
                remote(
                    view, view, v_send.at[away, along], v_recv.at[away, along],
                    at(rows ^ away, lax.rem(place + count - along, count)),
                ).wait_recv()
    for along in range(1, count):
        token_copy(along).wait_send()
        token_got(along)[1].wait_send()
        token_far(along).wait_recv()
    local.wait()
    local_v.wait()
    local_t.wait()


def opening(w, tokens, vector):
    count = tokens.shape[0]
    kinds, depth, half = w.shape
    dma = pltpu.SemaphoreType.DMA
    pair = [dma((count, 2)), dma((count, 2))]
    anywhere = pl.BlockSpec(memory_space=pl.ANY)
    return pl.pallas_call(
        opening_kernel,
        in_specs=[anywhere] * 3,
        out_specs=[anywhere] * 3,
        out_shape=[
            jax.ShapeDtypeStruct((kinds, depth * 4 * count, half), w.dtype),
            jax.ShapeDtypeStruct(tokens.shape, tokens.dtype),
            jax.ShapeDtypeStruct((4 * count,) + vector.shape, vector.dtype),
        ],
        scratch_shapes=pair * 5 + [dma((count,))] * 4 + [dma((4, count))] * 2 + [dma((3,))],
        compiler_params=pltpu.CompilerParams(collective_id=0, has_side_effects=True),
    )(w, tokens, vector)


def closing_kernel(s_ref, v_ref, tokens_ref, sum_ref, held, t_send, t_recv, c_send, c_recv, v_send, v_recv, own):
    rows, place, core = lax.axis_index("rows"), lax.axis_index("seq"), lax.axis_index("fsdp")
    count = s_ref.shape[0]
    width = s_ref.shape[2] // 2

    def at(row, seq, fsdp=None):
        return (row, seq, core if fsdp is None else fsdp)

    def hail(device):
        pl.semaphore_signal(barrier, inc=1, device_id=device, device_id_type=pl.DeviceIdType.MESH)

    barrier = pltpu.get_barrier_semaphore()
    for away in range(4):
        for along in range(count):
            if away or along:
                hail(at(rows ^ away, lax.rem(place + along, count)))
    hail(at(rows, place, 1 - core))
    pl.semaphore_wait(barrier, 4 * count)

    def remote(src, dst, send, recv, device):
        return pltpu.make_async_remote_copy(
            src_ref=src, dst_ref=dst, send_sem=send, recv_sem=recv, device_id=device,
            device_id_type=pl.DeviceIdType.MESH,
        )

    columns = pl.ds(pl.multiple_of(core * width, width), width)
    others = pl.ds(pl.multiple_of((1 - core) * width, width), width)

    def token_copy(along):
        to = lax.rem(place + along, count)
        return remote(
            s_ref.at[to, :, columns], tokens_ref.at[place, :, columns], t_send.at[along], t_recv.at[along], at(rows, to)
        )

    def token_got(along):
        start = lax.rem(place + count - along, count)
        view = tokens_ref.at[start, :, columns]
        return (
            remote(view, view, t_send.at[along], t_recv.at[along], at(rows, start)),
            remote(view, view, c_send.at[along], c_recv.at[along], at(rows, place, 1 - core)),
        )

    def token_far(along):
        view = tokens_ref.at[lax.rem(place + count - along, count), :, others]
        return remote(view, view, c_send.at[along], c_recv.at[along], at(rows, place, 1 - core))

    for along in range(1, count):
        token_copy(along).start()
    local_t = pltpu.make_async_copy(s_ref.at[place], tokens_ref.at[place], own.at[0])
    local_t.start()
    mine = rows * count + place
    vectors = []
    for away in range(4):
        for along in range(count):
            if away or along:
                to_row, to_seq = rows ^ away, lax.rem(place + along, count)
                copy = remote(
                    v_ref.at[to_row * count + to_seq], held.at[away * count + along],
                    v_send.at[away, along], v_recv.at[away, along], at(to_row, to_seq),
                )
                copy.start()
                vectors.append(copy)
    local_v = pltpu.make_async_copy(v_ref.at[mine], held.at[0], own.at[1])
    local_v.start()
    local_v.wait()
    for copy in vectors:
        copy.wait_recv()
    sum_ref[...] = jnp.sum(held[...], axis=0)
    for along in range(1, count):
        got, on = token_got(along)
        got.wait_recv()
        on.start()
    for copy in vectors:
        copy.wait_send()
    for along in range(1, count):
        token_copy(along).wait_send()
        token_got(along)[1].wait_send()
        token_far(along).wait_recv()
    local_t.wait()


def closing(tokens, vectors):
    count = tokens.shape[0]
    dma = pltpu.SemaphoreType.DMA
    anywhere = pl.BlockSpec(memory_space=pl.ANY)
    return pl.pallas_call(
        closing_kernel,
        in_specs=[anywhere] * 2,
        out_specs=[anywhere, pl.BlockSpec(memory_space=pltpu.VMEM)],
        out_shape=[
            jax.ShapeDtypeStruct(tokens.shape, tokens.dtype),
            jax.ShapeDtypeStruct(vectors.shape[1:], F32),
        ],
        scratch_shapes=[pltpu.VMEM(vectors.shape, F32)]
        + [dma((count,))] * 4
        + [dma((4, count))] * 2
        + [dma((2,))],
        compiler_params=pltpu.CompilerParams(collective_id=1, has_side_effects=True),
    )(tokens, vectors)


def product_kernel(mode, finish, n_extra, n_out, *refs):
    a_ref, b_ref = refs[:2]
    extra = refs[2 : 2 + n_extra]
    outs = refs[-1 - n_out : -1]
    total = refs[-1]
    k = pl.program_id(2)
    last = pl.num_programs(2) - 1
    dims = {"nn": ((1,), (0,)), "nt": ((1,), (1,)), "tn": ((0,), (0,))}[mode]
    part = lax.dot_general(a_ref[...], b_ref[...], (dims, ((), ())), preferred_element_type=F32)
    if last == 0:
        finish(part, extra, outs)
        return

    @pl.when(k == 0)
    def _():
        total[...] = part

    @pl.when((k > 0) & (k < last))
    def _():
        total[...] += part

    @pl.when(k == last)
    def _():
        finish(total[...] + part, extra, outs)


def finish_cast(total, extra, outs):
    outs[0][...] = total.astype(outs[0].dtype)


def finish_bias(scale, total, extra, outs):
    outs[0][...] = ((total + extra[0][...]) * scale).astype(BF)


def product(a, b, mode, finish=finish_cast, rows=(), deps=(), blocks=(1024, 1024, 2048)):
    plane = len(b.shape) == 3
    b_shape = b.shape[-2:]
    m, depth = a.shape if mode != "tn" else a.shape[::-1]
    n = b_shape[0] if mode == "nt" else b_shape[1]
    bm, bn, bk = min(blocks[0], m), min(blocks[1], n), min(blocks[2], depth)
    spec = pl.BlockSpec
    a_spec = (
        spec((bk, bm), lambda j, i, k: (k, i)) if mode == "tn" else spec((bm, bk), lambda j, i, k: (i, k))
    )
    if plane:
        b_spec = spec((None, bn, bk), lambda j, i, k: (k % b.shape[0], j, k // b.shape[0]))
    elif mode == "nt":
        b_spec = spec((bn, bk), lambda j, i, k: (j, k))
    else:
        b_spec = spec((bk, bn), lambda j, i, k: (k, j))
    row = spec((1, bn), lambda j, i, k: (0, j))
    field = spec((bm, bn), lambda j, i, k: (i, j))
    return pl.pallas_call(
        functools.partial(product_kernel, mode, finish, len(rows), 1),
        grid=(n // bn, m // bm, depth // bk),
        in_specs=[a_spec, b_spec]
        + [row] * len(rows)
        + [spec(memory_space=pl.ANY)] * len(deps),
        out_specs=field,
        out_shape=jax.ShapeDtypeStruct((m, n), BF),
        scratch_shapes=[pltpu.VMEM((bm, bn), F32)],
        cost_estimate=SMALL_COST,
        compiler_params=pltpu.CompilerParams(vmem_limit_bytes=48 * 2**20),
    )(a, b, *rows, *deps)


def dot_nt(a,b): return lax.dot_general(a,b,(((1,),(1,)),((),())),preferred_element_type=F32)
def dot_nn(a,b): return lax.dot_general(a,b,(((1,),(0,)),((),())),preferred_element_type=F32)

def fwd_kernel(tile, flags, q_ref, k_ref, v_ref, sk_ref, sv_ref, start_ref, doc_ref, sdoc_ref, *rest):
    o_ref, lse_ref, km, vt, acc, top, total = rest[-7:]
    i = pl.program_id(1)
    seg = k_ref.shape[0]
    lanes = lax.broadcasted_iota(jnp.int32, (1, 128), 1)
    masks = [(lanes < HEAD).astype(BF), (lanes >= HEAD).astype(BF)]
    @pl.when(i == 0)
    def _():
        for h in range(2):
            km[h, pl.ds(0, seg)] = k_ref[...] * masks[h]
            km[h, pl.ds(seg, 128)] = sk_ref[...] * masks[h]
        vt[:, pl.ds(0, seg)] = v_ref[...].T
        vt[:, pl.ds(seg, 128)] = sv_ref[...].T
    q = q_ref[...]
    allowed = sdoc_ref[...] == doc_ref[...]
    for h in range(2):
        s = dot_nt(km[h, pl.ds(seg, 128)], q)
        s = jnp.where(allowed, s, neg_big)
        m = jnp.max(s, axis=0, keepdims=True)
        p = jnp.where(allowed, jnp.exp(s - m), 0.0)
        top[h] = m
        total[h] = jnp.sum(p, axis=0, keepdims=True)
        acc[h] = dot_nn(vt[pl.ds(h * HEAD, HEAD), pl.ds(seg, 128)], p.astype(BF))
    def step(j, masked):
        at = pl.multiple_of(j * tile, tile)
        if masked:
            places = at + lax.broadcasted_iota(jnp.int32, (tile, tile), 0)
            mine = i * tile + lax.broadcasted_iota(jnp.int32, (tile, tile), 1)
            okay = (places <= mine) & (places >= start_ref[...])
        ss=[]
        for h in range(2):
            s = dot_nt(km[h, pl.ds(at, tile)], q)
            if masked:
                s = jnp.where(okay, s, neg_big)
            ss.append(s)
        for h in range(2):
            s = ss[h]
            m_old = top[h]
            m = jnp.maximum(m_old, jnp.max(s, axis=0, keepdims=True))
            p = jnp.exp(s - m)
            if masked:
                p = jnp.where(okay, p, 0.0)
            alpha = jnp.exp(m_old - m)
            top[h] = m
            total[h] = total[h] * alpha + jnp.sum(p, axis=0, keepdims=True)
            acc[h] = acc[h] * alpha + dot_nn(vt[pl.ds(h * HEAD, HEAD), pl.ds(at, tile)], p.astype(BF))
    count = pl.num_programs(1)
    def loop(j, _):
        flag = flags[i * count + j]
        @pl.when(flag == 2)
        def _(): step(j, False)
        @pl.when(flag == 1)
        def _(): step(j, True)
        return 0
    lax.fori_loop(0, i + 1, loop, 0)
    out = [acc[h] / total[h] for h in range(2)]
    o_ref[...] = jnp.concatenate(out, axis=0).T.astype(BF)
    for h in range(2):
        lse_ref[0, pl.ds(h, 1)] = top[h] + jnp.log(total[h])

def attn_fwd(q, k, v, sk, sv, start, doc, sdoc, flags, tile, base, pairs, earlier_out=(), deps=()):
    seg, width = q.shape
    count = seg // tile
    spec = pl.BlockSpec
    extra = tuple(earlier_out) + tuple(deps)
    return pl.pallas_call(
        functools.partial(fwd_kernel, tile),
        grid_spec=pltpu.PrefetchScalarGridSpec(
            num_scalar_prefetch=1,
            grid=(pairs, count),
            in_specs=[
                spec((tile, 128), lambda h, i, f: (i, h + base)),
                spec((seg, 128), lambda h, i, f: (0, h + base)),
                spec((seg, 128), lambda h, i, f: (0, h + base)),
                spec((128, 128), lambda h, i, f: (0, h + base)),
                spec((128, 128), lambda h, i, f: (0, h + base)),
                spec((1, tile), lambda h, i, f: (0, i)),
                spec((1, tile), lambda h, i, f: (0, i)),
                spec((128, 1), lambda h, i, f: (0, 0)),
            ]
            + [spec(memory_space=pl.ANY)] * len(extra),
            out_specs=[
                spec((tile, 128), lambda h, i, f: (i, h + base)),
                spec((1, 2, tile), lambda h, i, f: (h + base, 0, i)),
            ],
            scratch_shapes=[
                pltpu.VMEM((2, seg + 128, 128), BF),
                pltpu.VMEM((128, seg + 128), BF),
                pltpu.VMEM((2, HEAD, tile), F32),
                pltpu.VMEM((2, 1, tile), F32),
                pltpu.VMEM((2, 1, tile), F32),
            ],
        ),
        out_shape=[
            jax.ShapeDtypeStruct((seg, width), BF),
            jax.ShapeDtypeStruct((width // 128, 2, seg), F32),
        ],
        input_output_aliases={9: 0, 10: 1} if earlier_out else {},
        cost_estimate=SMALL_COST,
        compiler_params=pltpu.CompilerParams(vmem_limit_bytes=40 * 2**20),
    )(flags, q, k, v, sk, sv, start, doc, sdoc, *extra)


def bwd_kernel(tile, flags, q_ref, k_ref, v_ref, do_ref, o_ref, sk_ref, sv_ref, lse_ref, start_ref, doc_ref, sdoc_ref, *rest):
    dq_ref, dk_ref, dv_ref, dsk_ref, dsv_ref, qm, dom, dqt, delta = rest[-9:]
    j = pl.program_id(1)
    seg = q_ref.shape[0]
    count = seg // tile
    lanes = lax.broadcasted_iota(jnp.int32, (1, 128), 1)
    masks = [(lanes < HEAD).astype(BF), (lanes >= HEAD).astype(BF)]
    @pl.when(j == 0)
    def _():
        dqt[...] = jnp.zeros_like(dqt)
        for h in range(2):
            qm[h] = q_ref[...] * masks[h]
            dom[h] = do_ref[...] * masks[h]
        def one(i, _):
            at = pl.multiple_of(i * tile, tile)
            prod = (do_ref[pl.ds(at, tile)].astype(F32) * o_ref[pl.ds(at, tile)].astype(F32)).T
            for h in range(2):
                delta[h, :, pl.ds(at, tile)] = jnp.sum(prod[h * HEAD:(h + 1) * HEAD], axis=0, keepdims=True)
            return 0
        lax.fori_loop(0, count, one, 0)
    def block(i, kt, k_blk, v_blk, okay):
        at = pl.multiple_of(i * tile, tile)
        gk = gv = None
        for h in range(2):
            qh = qm[h, pl.ds(at, tile)]
            dh = dom[h, pl.ds(at, tile)]
            s = dot_nt(k_blk, qh)
            dp = dot_nt(v_blk, dh)
            p = jnp.exp(s - lse_ref[0, pl.ds(h, 1), pl.ds(at, tile)])
            if okay is not None:
                p = jnp.where(okay, p, 0.0)
            ds = (p * (dp - delta[h, :, pl.ds(at, tile)])).astype(BF)
            a = dot_nn(p.astype(BF), dh)
            b = dot_nn(ds, qh)
            gv = a if gv is None else gv + a
            gk = b if gk is None else gk + b
            dqt[pl.ds(h * HEAD, HEAD), pl.ds(at, tile)] += dot_nn(kt[h * HEAD:(h + 1) * HEAD], ds)
        return gk, gv
    @pl.when(j < count)
    def _():
        at_k = pl.multiple_of(j * tile, tile)
        k_blk = k_ref[...]
        v_blk = v_ref[...]
        kt = k_blk.T
        def masked_of(i):
            places = at_k + lax.broadcasted_iota(jnp.int32, (tile, tile), 0)
            mine = i * tile + lax.broadcasted_iota(jnp.int32, (tile, tile), 1)
            return (places <= mine) & (places >= start_ref[:, pl.ds(pl.multiple_of(i * tile, tile), tile)])
        gk, gv = block(j, kt, k_blk, v_blk, masked_of(j))
        dkacc, dvacc = gk, gv
        def loop(i, carry):
            flag = flags[i * count + j]
            def full(c):
                gk, gv = block(i, kt, k_blk, v_blk, None)
                return c[0] + gk, c[1] + gv
            def part(c):
                gk, gv = block(i, kt, k_blk, v_blk, masked_of(i))
                return c[0] + gk, c[1] + gv
            return lax.switch(flag, [lambda c: c, part, full], carry)
        dkacc, dvacc = lax.fori_loop(j + 1, count, loop, (dkacc, dvacc))
        dk_ref[...] = dkacc.astype(BF)
        dv_ref[...] = dvacc.astype(BF)
    @pl.when(j == count)
    def _():
        kt = sk_ref[...].T
        def loop(i, carry):
            okay = sdoc_ref[...] == doc_ref[:, pl.ds(pl.multiple_of(i * tile, tile), tile)]
            gk, gv = block(i, kt, sk_ref[...], sv_ref[...], okay)
            return carry[0] + gk, carry[1] + gv
        z = jnp.zeros((128, 128), F32)
        a, b = lax.fori_loop(0, count, loop, (z, z))
        dsk_ref[...] = a.astype(BF)
        dsv_ref[...] = b.astype(BF)
        def fin(i, _):
            at = pl.multiple_of(i * tile, tile)
            dq_ref[pl.ds(at, tile)] = (dqt[:, pl.ds(at, tile)].T.astype(BF).astype(F32) * HEAD ** -0.5).astype(BF)
            return 0
        lax.fori_loop(0, count, fin, 0)

def attn_bwd(q, k, v, do, o, sk, sv, lse, start, doc, sdoc, flags, tile, base, pairs, deps=()):
    seg = q.shape[0]
    count = seg // tile
    last = count - 1
    spec = pl.BlockSpec
    return pl.pallas_call(
        functools.partial(bwd_kernel, tile),
        grid_spec=pltpu.PrefetchScalarGridSpec(
            num_scalar_prefetch=1,
            grid=(pairs, count + 1),
            in_specs=[
                spec((seg, 128), lambda h, j, f: (0, h + base)),
                spec((tile, 128), lambda h, j, f: (jnp.minimum(j, last), h + base)),
                spec((tile, 128), lambda h, j, f: (jnp.minimum(j, last), h + base)),
                spec((seg, 128), lambda h, j, f: (0, h + base)),
                spec((seg, 128), lambda h, j, f: (0, h + base)),
                spec((128, 128), lambda h, j, f: (0, h + base)),
                spec((128, 128), lambda h, j, f: (0, h + base)),
                spec((1, 2, seg), lambda h, j, f: (h + base, 0, 0)),
                spec((1, seg), lambda h, j, f: (0, 0)),
                spec((1, seg), lambda h, j, f: (0, 0)),
                spec((128, 1), lambda h, j, f: (0, 0)),
            ]
            + [spec(memory_space=pl.ANY)] * len(deps),
            out_specs=[
                spec((seg, 128), lambda h, j, f: (0, h)),
                spec((tile, 128), lambda h, j, f: (jnp.minimum(j, last), h)),
                spec((tile, 128), lambda h, j, f: (jnp.minimum(j, last), h)),
                spec((128, 128), lambda h, j, f: (0, h)),
                spec((128, 128), lambda h, j, f: (0, h)),
            ],
            scratch_shapes=[
                pltpu.VMEM((2, seg, 128), BF),
                pltpu.VMEM((2, seg, 128), BF),
                pltpu.VMEM((128, seg), F32),
                pltpu.VMEM((2, 1, seg), F32),
            ],
        ),
        out_shape=[jax.ShapeDtypeStruct((seg, pairs * 128), BF)] * 3
        + [jax.ShapeDtypeStruct((128, pairs * 128), BF)] * 2,
        cost_estimate=SMALL_COST,
        compiler_params=pltpu.CompilerParams(vmem_limit_bytes=40 * 2**20),
    )(flags, q, k, v, do, o, sk, sv, lse, start, doc, sdoc, *deps)


def make_meta(doc, tile):
    seg=doc.shape[0]; count=seg//tile
    place=jnp.arange(seg,dtype=jnp.int32)
    new=jnp.concatenate([jnp.ones((1,),bool), doc[1:]!=doc[:-1]])
    start=lax.cummax(jnp.where(new,place,0))
    lo=doc[::tile]; hi=doc[tile-1::tile]
    i=jnp.arange(count)
    full=(lo[None,:]==hi[:,None])&(i[None,:]<i[:,None])
    none=(hi[None,:]<lo[:,None])
    flags=jnp.where(full,2,jnp.where(none,0,1)).astype(jnp.int32).reshape(-1)
    return start.reshape(1,seg), flags


def gate(value, *deps):
    anywhere = pl.BlockSpec(memory_space=pl.ANY)
    return pl.pallas_call(
        lambda *refs: None,
        in_specs=[anywhere] * (1 + len(deps)),
        out_specs=anywhere,
        out_shape=jax.ShapeDtypeStruct(value.shape, value.dtype),
        input_output_aliases={0: 0},
        cost_estimate=SMALL_COST,
    )(value, *deps)


BOTH = ("rows", "seq")


def other_core(block):
    return lax.ppermute(block, "fsdp", ((0, 1), (1, 0)))


def exchange(field):
    count = lax.axis_size("seq")
    me = lax.axis_index("seq")
    core = lax.axis_index("fsdp")
    half = field.shape[2] // 2
    mine = lax.dynamic_slice_in_dim(field, core * half, half, 2)
    got = jnp.zeros_like(mine)
    own = lax.dynamic_slice_in_dim(mine, me, 1, 0)
    got = lax.dynamic_update_slice_in_dim(got, own, me, 0)
    for away in range(1, count):
        block = lax.dynamic_slice_in_dim(mine, lax.rem(me + away, count), 1, 0)
        moved = lax.ppermute(block, "seq", [(n, (n + away) % count) for n in range(count)])
        got = lax.dynamic_update_slice_in_dim(got, moved, lax.rem(me + count - away, count), 0)
    other = other_core(got)
    low_half = jnp.where(core == 0, got, other)
    high_half = jnp.where(core == 0, other, got)
    return jnp.concatenate((low_half, high_half), axis=2)


def shift_by(field, away):
    count = lax.axis_size("seq")
    perm = [(n, n + away) for n in range(count) if 0 <= n + away < count]
    return lax.ppermute(field, "seq", perm)


def both_halves(field):
    low = field.astype(BF)
    return low.astype(F32) + other_core(low).astype(F32)


def norm_forward(field, gain_vec, shift_vec):
    row_mean = jnp.mean(field, axis=-1, keepdims=True)
    centered = field - row_mean
    variance = jnp.mean(centered * centered, axis=-1, keepdims=True)
    scale = lax.rsqrt(variance + norm_eps)
    return (centered * scale * gain_vec + shift_vec).astype(BF), row_mean, scale


def norm_backward(field, row_mean, scale, gain_vec, grad):
    unit = (field - row_mean) * scale
    scaled = grad * gain_vec
    mean_one = jnp.mean(scaled, axis=-1, keepdims=True)
    mean_two = jnp.mean(scaled * unit, axis=-1, keepdims=True)
    d_field = scale * (scaled - mean_one - unit * mean_two)
    return d_field, jnp.sum(grad * unit, axis=0), jnp.sum(grad, axis=0)


def mm(a, b):
    return dot_nn(a, b)


def mm_tn(a, b):
    return lax.dot_general(a, b, (((0,), (0,)), ((), ())), preferred_element_type=F32)


def mm_nt(a, b):
    return dot_nt(a, b)


def layer_by_segment(
    states,
    doc_ids,
    w_qkv,
    w_out,
    w_up,
    w_down,
    bias_qv,
    bias_out,
    bias_up,
    bias_down,
    gain_one,
    shift_one,
    gain_two,
    shift_two,
    cotangent,
):
    segs, width, model = states.shape[1:]
    seg_len = segs * width
    place = lax.axis_index("seq")
    half = w_qkv.shape[2]
    hidden_units = w_up.shape[1]
    tile = 512

    small = (bias_qv, bias_out, bias_up, bias_down, gain_one, shift_one, gain_two, shift_two)
    sizes = [item.size for item in small]
    vector = jnp.concatenate([item.reshape(-1) for item in small])
    room = -(-vector.shape[0] // 2048) * 2048
    vector = jnp.pad(vector, (0, room - vector.shape[0])).reshape(-1, 128)
    qkv_full, tokens, packed = opening(w_qkv, states[0], vector)
    tokens = tokens.reshape(seg_len, model)
    packed = packed.reshape(packed.shape[0], -1)
    cuts = []
    at = 0
    for size in sizes:
        cuts.append(packed[:, at : at + size].astype(F32))
        at += size
    shards = packed.shape[0]

    def spread_last(field, lead):
        return jnp.moveaxis(field.reshape(shards, *lead, -1), 0, len(lead)).reshape(-1)

    bias_pair = jnp.moveaxis(cuts[0].reshape(shards, 2, half // HEAD, -1), 0, 2).reshape(2, half)
    bias_o = cuts[1].reshape(-1)
    bias_u = spread_last(cuts[2], (hidden_units // HEAD,))
    bias_d = cuts[3].reshape(-1)
    gain_a, shift_a, gain_b, shift_b = [item.reshape(-1) for item in cuts[4:]]

    docs = doc_ids[0]
    my_docs = lax.dynamic_index_in_dim(docs, place, 0, keepdims=False)
    start, flags = make_meta(my_docs, tile)
    tails = docs[:, seg_len - SUMM :]
    before_one = lax.dynamic_index_in_dim(tails, jnp.maximum(place - 1, 0), 0, keepdims=False)
    before_two = lax.dynamic_index_in_dim(tails, jnp.maximum(place - 2, 0), 0, keepdims=False)
    sum_docs = jnp.concatenate(
        (
            jnp.where(place >= 1, before_one, -1),
            jnp.where(place >= 2, before_two, -1),
            jnp.full((128 - 2 * SUMM,), -1, jnp.int32),
        )
    ).reshape(128, 1)
    doc_row = my_docs.reshape(1, seg_len)

    tokens_f = tokens.astype(F32)
    normed_one, mean_one, scale_one = norm_forward(tokens_f, gain_a, shift_a)
    query = product(
        normed_one, qkv_full[0], "nn", functools.partial(finish_bias, HEAD**-0.5), (bias_pair[:1],)
    )
    keys = product(normed_one, qkv_full[1], "nn")
    values = product(
        normed_one, qkv_full[2], "nn", functools.partial(finish_bias, 1.0), (bias_pair[1:],)
    )
    out_full = lax.all_gather(gate(w_out.T, normed_one), BOTH, axis=0, tiled=True)
    up_full = lax.all_gather(gate(w_up, values), BOTH, axis=0, tiled=True)
    grad_out = exchange(gate(cotangent[0], query)).reshape(seg_len, model)
    tail = jnp.stack((keys[seg_len - SUMM :], values[seg_len - SUMM :]))
    lent = jnp.concatenate((shift_by(tail, 1), shift_by(tail, 2)), axis=1)
    lent = jnp.pad(lent, ((0, 0), (0, 128 - 2 * SUMM), (0, 0)))
    pairs = half // 128
    each = pairs // 4
    attended = ()
    for n in range(4):
        attended = attn_fwd(
            query, keys, values, lent[0], lent[1], start, doc_row, sum_docs, flags, tile,
            n * each, each, attended, (grad_out,) if n == 3 else (),
        )
        if n == 0:
            down_full = lax.all_gather(gate(w_down.T, attended[0]), BOTH, axis=0, tiled=True)
    mixed, log_sum = attended
    attended = product(mixed, out_full, "nt")
    hidden = tokens_f + both_halves(attended) + bias_o
    normed_two, mean_two, scale_two = norm_forward(hidden, gain_b, shift_b)
    up_proj = mm(normed_two, up_full) + bias_u
    bell = jnp.exp(-0.5 * up_proj * up_proj)
    area = 0.5 * (1.0 + lax.erf(up_proj * (0.5**0.5)))
    activated = (up_proj * area).astype(BF)
    slope = (area + up_proj * bell * 0.3989422804014327).astype(BF)

    def over_rows(partial):
        return lax.psum_scatter(partial, "rows", scatter_dimension=0, tiled=True)

    def over_seq(partial):
        return lax.psum_scatter(partial, "seq", scatter_dimension=0, tiled=True).astype(F32)

    down_sum = product(grad_out, activated, "tn")
    down_rows = over_rows(down_sum)
    slope = gate(slope, down_sum)
    d_up = (mm(grad_out, down_full) * slope.astype(F32)).astype(BF)
    up_sum = product(normed_two, d_up, "tn")
    d_norm_part = product(d_up, up_full, "nt", deps=(up_sum,))
    up_turn = gate(up_sum, down_rows, d_norm_part)
    up_rows = over_rows(up_turn)
    d_norm_two = both_halves(d_norm_part)
    d_hidden_ln, grad_gain_two, grad_shift_two = norm_backward(
        hidden, mean_two, scale_two, gain_b, d_norm_two
    )
    d_hidden = grad_out.astype(F32) + d_hidden_ln
    d_hidden_low = d_hidden.astype(BF)
    d_mixed = product(d_hidden_low, out_full, "nn", deps=(up_turn,))
    out_sum = product(d_hidden_low, mixed, "tn", deps=(d_mixed,))

    def back(n, deps):
        return attn_bwd(
            query, keys, values, d_mixed, mixed, lent[0], lent[1], log_sum, start, doc_row,
            sum_docs, flags, tile, n * each, each, deps,
        )

    def own_half(pieces):
        d_pre, d_keys, d_values, d_lent_k, d_lent_v = [
            jnp.concatenate(pair, axis=1) for pair in zip(*pieces)
        ]
        d_lent = jnp.stack((d_lent_k, d_lent_v))
        back_home = shift_by(d_lent[:, :SUMM], -1).astype(F32) + shift_by(
            d_lent[:, SUMM : 2 * SUMM], -2
        ).astype(F32)
        ends = jnp.stack((d_keys[seg_len - SUMM :], d_values[seg_len - SUMM :])).astype(F32)
        ends = (ends + back_home).astype(BF)
        d_keys = lax.dynamic_update_slice(d_keys, ends[0], (seg_len - SUMM, 0))
        d_values = lax.dynamic_update_slice(d_values, ends[1], (seg_len - SUMM, 0))
        grads = jnp.concatenate((d_pre, d_keys, d_values), axis=1)
        return grads, product(normed_one, grads, "tn", blocks=(1024, grads.shape[1] // 2, 2048))

    piece_0 = back(0, (out_sum,))
    down_turn = gate(down_rows, up_rows, piece_0[0])
    out_rows = over_rows(gate(out_sum, up_rows, down_turn))
    grad_w_down = over_seq(down_turn)
    piece_1 = back(1, (down_turn,))
    first_half, first_sum = own_half((piece_0, piece_1))
    piece_2 = back(2, (first_sum,))
    first_turn = gate(first_sum, out_rows, piece_2[0])
    first_rows = over_rows(first_turn)
    grad_w_up = over_seq(gate(up_rows, first_turn))
    out_partial = product(activated, down_full, "nt", deps=(first_turn,))
    out_tokens = (hidden + both_halves(out_partial) + bias_d).astype(BF)
    out_states = exchange(out_tokens.reshape(segs, width, model))[None]
    piece_3 = back(3, (out_partial,))
    second_half, second_sum = own_half((piece_2, piece_3))
    second_turn = gate(second_sum, first_rows)
    second_rows = over_rows(second_turn)
    d_qkv = jnp.concatenate((first_half, second_half), axis=1)
    d_norm_one = both_halves(product(d_qkv, qkv_full, "nt", deps=(second_turn,), blocks=(1024, 1024, half // 2)))
    grad_w_out = over_seq(gate(out_rows, second_turn))
    qkv_rows = jnp.concatenate((first_rows, second_rows), axis=1)
    grad_w_qkv = over_seq(qkv_rows)
    grad_w_qkv = jnp.transpose(grad_w_qkv.reshape(-1, 2, 3, half // 2), (2, 0, 1, 3)).reshape(3, -1, half)
    grad_w_out = grad_w_out.T
    grad_w_down = grad_w_down.T
    d_tokens_ln, grad_gain_one, grad_shift_one = norm_backward(
        tokens_f, mean_one, scale_one, gain_a, d_norm_one
    )
    grad_tokens = (d_hidden + d_tokens_ln).astype(BF)
    def column_sum(field):
        return jnp.sum(field.astype(F32), axis=0)

    kind_sum = column_sum(d_qkv).reshape(2, 3, half // 2)
    sums = (
        jnp.moveaxis(
            jnp.stack((kind_sum[:, 0], kind_sum[:, 2])).reshape(2, half // HEAD, shards, -1), 2, 0
        ),
        column_sum(d_hidden),
        jnp.moveaxis(column_sum(d_up).reshape(hidden_units // HEAD, shards, -1), 1, 0),
        column_sum(grad_out),
        grad_gain_one,
        grad_shift_one,
        grad_gain_two,
        grad_shift_two,
    )
    vectors = jnp.concatenate([item.reshape(shards, -1) for item in sums], axis=1)
    vectors = jnp.pad(vectors, ((0, 0), (0, room - vectors.shape[1]))).reshape(shards, -1, 128)
    grad_states, vector = closing(grad_tokens.reshape(segs, width, model), gate(vectors, qkv_rows))
    grad_states = grad_states[None]
    vector = vector.reshape(-1)
    small_grads = []
    at = 0
    for item, size in zip(small, sizes):
        small_grads.append(vector[at : at + size].reshape(item.shape))
        at += size
    return (out_states, grad_states, grad_w_qkv, grad_w_out, grad_w_up, grad_w_down, *small_grads)


def solution(mesh):
    whole_segments = mesh.shape["seq"] == SEGS and mesh.shape["rows"] == 4
    return jax.shard_map(
        layer_by_segment if whole_segments else local,
        mesh=mesh,
        in_specs=(
            P("rows", None, "seq", None),
            P("rows", None, None),
            P(None, ("rows", "seq"), "fsdp"),
            P("fsdp", ("rows", "seq")),
            P(("rows", "seq"), "fsdp"),
            P("fsdp", ("rows", "seq")),
            P(None, "fsdp", ("rows", "seq")),
            P(("rows", "seq")),
            P("fsdp", ("rows", "seq")),
            P(("rows", "seq")),
            P(("rows", "seq")),
            P(("rows", "seq")),
            P(("rows", "seq")),
            P(("rows", "seq")),
            P("rows", None, "seq", None),
        ),
        out_specs=(
            P("rows", None, "seq", None),
            P("rows", None, "seq", None),
            P(None, ("rows", "seq"), "fsdp"),
            P("fsdp", ("rows", "seq")),
            P(("rows", "seq"), "fsdp"),
            P("fsdp", ("rows", "seq")),
            P(None, "fsdp", ("rows", "seq")),
            P(("rows", "seq")),
            P("fsdp", ("rows", "seq")),
            P(("rows", "seq")),
            P(("rows", "seq")),
            P(("rows", "seq")),
            P(("rows", "seq")),
            P(("rows", "seq")),
        ),
        check_vma=False,
    )
```

```python
import functools

import jax
import jax.numpy as jnp
from jax import lax
from jax.experimental import pallas as pl
from jax.experimental.pallas import tpu as pltpu
from jax.sharding import PartitionSpec as P

HEAD = 64
SUMM = 50
SEGS = 4
F32 = jnp.float32
BF = jnp.bfloat16
SMALL_COST = pl.CostEstimate(flops=1000, bytes_accessed=1000, transcendentals=0)


def told(microseconds):
    return pl.CostEstimate(flops=int(microseconds * 1e9), bytes_accessed=1000, transcendentals=0)


neg_big = -1e30
norm_eps = 1e-05


def spread(block, axis, source):
    block = jnp.where(lax.axis_index(axis) == source, block, jnp.zeros_like(block))
    return lax.psum(block, axis)


def layer_norm(field, gain_vec, shift_vec):
    row_mean = jnp.mean(field, axis=-1, keepdims=True)
    centered = field - row_mean
    variance = jnp.mean(centered * centered, axis=-1, keepdims=True)
    return centered * lax.rsqrt(variance + norm_eps) * gain_vec + shift_vec


def gelu_exact(field):
    return jax.nn.gelu(field, approximate=False)


def earlier(field, offset, fill_value):
    widths = tuple(((offset, 0) if dim_index == 1 else (0, 0) for dim_index in range(field.ndim)))
    return jnp.pad(field, widths, constant_values=fill_value)[:, : field.shape[1]]


def later(field, offset):
    widths = tuple(((0, offset) if dim_index == 1 else (0, 0) for dim_index in range(field.ndim)))
    return jnp.pad(field, widths)[:, offset:]


def lead(field):
    return jnp.moveaxis(field, 1, 0)


def halves(field):
    return lax.psum(field.astype(jnp.bfloat16), "fsdp").astype(jnp.float32)


def local(
    states,
    doc_ids,
    w_qkv,
    w_out,
    w_up,
    w_down,
    bias_qv,
    bias_out,
    bias_up,
    bias_down,
    gain_one,
    shift_one,
    gain_two,
    shift_two,
    cotangent,
):
    attn_full = (
        lax.all_gather(w_qkv, ("rows", "seq"), axis=1, tiled=True),
        lax.all_gather(w_out, ("rows", "seq"), axis=1, tiled=True),
        lax.all_gather(bias_qv, ("rows", "seq"), axis=2, tiled=True),
        lax.all_gather(gain_one, ("rows", "seq"), axis=0, tiled=True),
        lax.all_gather(shift_one, ("rows", "seq"), axis=0, tiled=True),
        lax.all_gather(bias_out, ("rows", "seq"), axis=0, tiled=True),
    )
    qkv_full, out_full, bqv_full, gain_a, shift_a, bias_o = attn_full
    rows_dev, seg_count, width, model = states.shape
    seq_count = lax.axis_size("seq")
    seq_place = lax.axis_index("seq")
    seg_len = width * seq_count
    half_width = qkv_full.shape[2]
    heads_loc = half_width // HEAD
    score_scale = HEAD ** (-0.5)
    states_f = states.astype(jnp.float32)
    normed_f, norm_one_back = jax.vjp(
        layer_norm, states_f, gain_a.astype(jnp.float32), shift_a.astype(jnp.float32)
    )
    normed_one = normed_f.astype(jnp.bfloat16)
    projected = jnp.einsum(
        "rsid,kde->krsie", normed_one, qkv_full, preferred_element_type=jnp.float32
    )
    bias_pair = bqv_full.astype(jnp.float32).reshape(2, half_width)
    query = ((projected[0] + bias_pair[0]) * score_scale).astype(jnp.bfloat16)
    keys = projected[1].astype(jnp.bfloat16)
    values = (projected[2] + bias_pair[1]).astype(jnp.bfloat16)
    tail = jnp.stack((keys[:, :, width - SUMM :], values[:, :, width - SUMM :]))
    summary = spread(tail, "seq", seq_count - 1)
    sum_keys = jnp.concatenate((earlier(summary[0], 1, 0.0), earlier(summary[0], 2, 0.0)), axis=2)
    sum_values = jnp.concatenate((earlier(summary[1], 1, 0.0), earlier(summary[1], 2, 0.0)), axis=2)
    sum_src = doc_ids[:, :, seg_len - SUMM :]
    sum_docs = jnp.concatenate((earlier(sum_src, 1, -1), earlier(sum_src, 2, -1)), axis=2)
    sum_k5 = sum_keys.reshape(rows_dev, seg_count, 2 * SUMM, heads_loc, HEAD)
    sum_v5 = sum_values.reshape(rows_dev, seg_count, 2 * SUMM, heads_loc, HEAD)
    first_pos = seq_place * width
    query_docs = lax.dynamic_slice_in_dim(doc_ids, first_pos, width, 2)
    query_pos = first_pos + jnp.arange(width, dtype=jnp.int32)
    query5 = query.reshape(rows_dev, seg_count, width, heads_loc, HEAD)
    sum_allowed = (query_docs[:, :, :, None] == sum_docs[:, :, None, :])[:, :, None]
    sum_scores = jnp.einsum(
        "rsihe,rsjhe->rshij", query5, sum_k5, preferred_element_type=jnp.float32
    )
    sum_scores = jnp.where(sum_allowed, sum_scores, neg_big)
    start_max = jnp.max(sum_scores, axis=-1)
    start_exp = jnp.where(sum_allowed, jnp.exp(sum_scores - start_max[..., None]), 0.0)
    start_sum = jnp.sum(start_exp, axis=-1)
    start_acc = jnp.einsum(
        "rshij,rsjhe->rsihe",
        start_exp.astype(jnp.bfloat16),
        sum_v5,
        preferred_element_type=jnp.float32,
    )
    key_piece = lax.all_gather(keys, "seq", axis=2, tiled=True)
    value_piece = lax.all_gather(values, "seq", axis=2, tiled=True)
    count = key_piece.shape[2]
    key5 = key_piece.reshape(rows_dev, seg_count, count, heads_loc, HEAD)
    value5 = value_piece.reshape(rows_dev, seg_count, count, heads_loc, HEAD)
    key_pos = jnp.arange(count, dtype=jnp.int32)
    causal = (key_pos[None, :] <= query_pos[:, None])[None, None, None]
    allowed = causal & (query_docs[:, :, :, None] == doc_ids[:, :, None, :])[:, :, None]
    scores = jnp.einsum("rsihe,rsjhe->rshij", query5, key5, preferred_element_type=jnp.float32)
    scores = jnp.where(allowed, scores, neg_big)
    new_max = jnp.maximum(start_max, jnp.max(scores, axis=-1))
    factor = jnp.exp(start_max - new_max)
    exponent = jnp.where(allowed, jnp.exp(scores - new_max[..., None]), 0.0)
    new_sum = start_sum * factor + jnp.sum(exponent, axis=-1)
    gained = jnp.einsum(
        "rshij,rsjhe->rsihe",
        exponent.astype(jnp.bfloat16),
        value5,
        preferred_element_type=jnp.float32,
    )
    new_acc = start_acc * jnp.swapaxes(factor, 2, 3)[..., None] + gained
    log_sum = new_max + jnp.log(new_sum)
    mixed_f = new_acc / jnp.swapaxes(new_sum, 2, 3)[..., None]
    mixed = mixed_f.reshape(rows_dev, seg_count, width, half_width).astype(jnp.bfloat16)
    attn_lin = halves(
        jnp.einsum("rsie,ed->rsid", mixed, out_full, preferred_element_type=jnp.float32)
    )
    hidden = states_f + attn_lin + bias_o.astype(jnp.float32)
    ffn_full = (
        lax.all_gather(w_up, ("rows", "seq"), axis=0, tiled=True),
        lax.all_gather(w_down, ("rows", "seq"), axis=1, tiled=True),
        lax.all_gather(bias_up, ("rows", "seq"), axis=1, tiled=True),
        lax.all_gather(gain_two, ("rows", "seq"), axis=0, tiled=True),
        lax.all_gather(shift_two, ("rows", "seq"), axis=0, tiled=True),
        lax.all_gather(bias_down, ("rows", "seq"), axis=0, tiled=True),
    )
    up_full, down_full, bias_u, gain_b, shift_b, bias_d = ffn_full
    normed_two_f, norm_two_back = jax.vjp(
        layer_norm, hidden, gain_b.astype(jnp.float32), shift_b.astype(jnp.float32)
    )
    normed_two = normed_two_f.astype(jnp.bfloat16)
    up_proj = jnp.einsum(
        "rsid,df->rsif", normed_two, up_full, preferred_element_type=jnp.float32
    ) + bias_u.astype(jnp.float32).reshape(-1)
    activated_f, gelu_back = jax.vjp(gelu_exact, up_proj)
    activated = activated_f.astype(jnp.bfloat16)
    down_proj = halves(
        jnp.einsum("rsif,fd->rsid", activated, down_full, preferred_element_type=jnp.float32)
    )
    out_states = (hidden + down_proj + bias_d.astype(jnp.float32)).astype(jnp.bfloat16)
    up_back, down_back = (
        lax.all_gather(w_up, ("rows", "seq"), axis=0, tiled=True),
        lax.all_gather(w_down, ("rows", "seq"), axis=1, tiled=True),
    )
    qkv_back, out_back = (
        lax.all_gather(w_qkv, ("rows", "seq"), axis=1, tiled=True),
        lax.all_gather(w_out, ("rows", "seq"), axis=1, tiled=True),
    )
    grad_out = cotangent.astype(jnp.float32)
    grad_bias_down = jnp.sum(grad_out, axis=(0, 1, 2))
    grad_w_down = jnp.einsum(
        "rsif,rsid->fd", activated, cotangent, preferred_element_type=jnp.float32
    )
    d_act = jnp.einsum("rsid,fd->rsif", cotangent, down_back, preferred_element_type=jnp.float32)
    (d_up,) = gelu_back(d_act)
    d_up_low = d_up.astype(jnp.bfloat16)
    grad_bias_up = jnp.sum(d_up_low, axis=(0, 1, 2), dtype=jnp.float32).reshape(bias_u.shape)
    grad_w_up = jnp.einsum(
        "rsid,rsif->df", normed_two, d_up_low, preferred_element_type=jnp.float32
    )
    d_norm_two = halves(
        jnp.einsum("rsif,df->rsid", d_up_low, up_back, preferred_element_type=jnp.float32)
    )
    d_hidden_ln, grad_gain_two, grad_shift_two = norm_two_back(d_norm_two)
    d_hidden = grad_out + d_hidden_ln
    ffn_grads = (
        lax.psum_scatter(grad_w_up, ("rows", "seq"), scatter_dimension=0, tiled=True),
        lax.psum_scatter(grad_w_down, ("rows", "seq"), scatter_dimension=1, tiled=True),
        lax.psum_scatter(grad_bias_up, ("rows", "seq"), scatter_dimension=1, tiled=True),
        lax.psum_scatter(grad_gain_two, ("rows", "seq"), scatter_dimension=0, tiled=True),
        lax.psum_scatter(grad_shift_two, ("rows", "seq"), scatter_dimension=0, tiled=True),
        lax.psum_scatter(grad_bias_down, ("rows", "seq"), scatter_dimension=0, tiled=True),
    )
    grad_bias_out = jnp.sum(d_hidden, axis=(0, 1, 2))
    d_hidden_low = d_hidden.astype(jnp.bfloat16)
    grad_w_out = jnp.einsum(
        "rsie,rsid->ed", mixed, d_hidden_low, preferred_element_type=jnp.float32
    )
    d_mixed = jnp.einsum(
        "rsid,ed->rsie", d_hidden_low, out_back, preferred_element_type=jnp.float32
    ).astype(jnp.bfloat16)
    d_mixed5 = d_mixed.reshape(rows_dev, seg_count, width, heads_loc, HEAD)
    keys_all, values_all = (
        lax.all_gather(keys, "seq", axis=2, tiled=True),
        lax.all_gather(values, "seq", axis=2, tiled=True),
    )
    key_lead = lead(keys_all.reshape(rows_dev, seg_count, seg_len, heads_loc, HEAD))
    value_lead = lead(values_all.reshape(rows_dev, seg_count, seg_len, heads_loc, HEAD))
    query_lead = lead(query5)
    grad_lead = lead(d_mixed5)
    key_positions = jnp.arange(seg_len, dtype=jnp.int32)

    def segment_back(seg_items):
        q_seg, do_seg, lse_seg, qdoc_seg, k_seg, v_seg, kdoc_seg, sk_seg, sv_seg, sdoc_seg = (
            seg_items
        )
        causal = (key_positions[None, :] <= query_pos[:, None])[None, None]
        allowed = causal & (qdoc_seg[:, :, None] == kdoc_seg[:, None, :])[:, None]
        scores = jnp.einsum("rihe,rjhe->rhij", q_seg, k_seg, preferred_element_type=jnp.float32)
        attn_probs = jnp.where(allowed, jnp.exp(scores - lse_seg[..., None]), 0.0)
        d_probs = jnp.einsum("rihe,rjhe->rhij", do_seg, v_seg, preferred_element_type=jnp.float32)
        summ_allowed = (qdoc_seg[:, :, None] == sdoc_seg[:, None, :])[:, None]
        summ_scores = jnp.einsum(
            "rihe,rjhe->rhij", q_seg, sk_seg, preferred_element_type=jnp.float32
        )
        summ_probs = jnp.where(summ_allowed, jnp.exp(summ_scores - lse_seg[..., None]), 0.0)
        summ_dprobs = jnp.einsum(
            "rihe,rjhe->rhij", do_seg, sv_seg, preferred_element_type=jnp.float32
        )
        delta = jnp.sum(attn_probs * d_probs, axis=-1) + jnp.sum(summ_probs * summ_dprobs, axis=-1)
        d_scores = (attn_probs * (d_probs - delta[..., None])).astype(jnp.bfloat16)
        d_summ = (summ_probs * (summ_dprobs - delta[..., None])).astype(jnp.bfloat16)
        d_query = jnp.einsum("rhij,rjhe->rihe", d_scores, k_seg, preferred_element_type=jnp.float32)
        d_query = d_query + jnp.einsum(
            "rhij,rjhe->rihe", d_summ, sk_seg, preferred_element_type=jnp.float32
        )
        d_sum_keys = jnp.einsum(
            "rhij,rihe->rjhe", d_summ, q_seg, preferred_element_type=jnp.float32
        )
        d_sum_values = jnp.einsum(
            "rhij,rihe->rjhe",
            summ_probs.astype(jnp.bfloat16),
            do_seg,
            preferred_element_type=jnp.float32,
        )
        return (d_query, d_scores, attn_probs.astype(jnp.bfloat16), d_sum_keys, d_sum_values, delta)

    seg_inputs = (
        query_lead,
        grad_lead,
        lead(log_sum),
        lead(query_docs),
        key_lead,
        value_lead,
        lead(doc_ids),
        lead(sum_k5),
        lead(sum_v5),
        lead(sum_docs),
    )
    d_query_lead, d_scores_all, probs_all, d_sk_lead, d_sv_lead, delta_lead = lax.map(
        segment_back, seg_inputs
    )
    d_key_part = jnp.einsum(
        "srhij,srihe->jrshe", d_scores_all, query_lead, preferred_element_type=jnp.float32
    )
    d_value_part = jnp.einsum(
        "srhij,srihe->jrshe", probs_all, grad_lead, preferred_element_type=jnp.float32
    )
    key_grads = lax.psum_scatter(
        jnp.stack((d_key_part, d_value_part), axis=3)
        .reshape(width * lax.axis_size("seq"), rows_dev, seg_count, 2, half_width)
        .astype(jnp.bfloat16),
        "seq",
        scatter_dimension=0,
        tiled=True,
    ).astype(jnp.float32)
    key_grads = jnp.transpose(key_grads, (3, 1, 2, 0, 4))
    d_sk = jnp.moveaxis(d_sk_lead, 0, 1).reshape(rows_dev, seg_count, 2 * SUMM, half_width)
    d_sv = jnp.moveaxis(d_sv_lead, 0, 1).reshape(rows_dev, seg_count, 2 * SUMM, half_width)
    src_keys = later(d_sk[:, :, :SUMM], 1) + later(d_sk[:, :, SUMM:], 2)
    src_values = later(d_sv[:, :, :SUMM], 1) + later(d_sv[:, :, SUMM:], 2)
    summ_grads = lax.psum(jnp.stack((src_keys, src_values)).astype(jnp.bfloat16), "seq").astype(
        jnp.float32
    )
    owner_grads = jnp.where(seq_place == seq_count - 1, summ_grads, 0.0)
    owner_grads = jnp.pad(owner_grads, ((0, 0), (0, 0), (0, 0), (width - SUMM, 0), (0, 0)))
    key_grads = key_grads + owner_grads
    d_keys_low = key_grads[0].astype(jnp.bfloat16)
    d_values_low = key_grads[1].astype(jnp.bfloat16)
    d_query = jnp.moveaxis(d_query_lead, 0, 1).reshape(rows_dev, seg_count, width, half_width)
    d_query_low = d_query.astype(jnp.bfloat16)
    d_pre = (d_query_low.astype(jnp.float32) * score_scale).astype(jnp.bfloat16)
    grad_bias_qv = jnp.stack(
        (
            jnp.sum(d_pre, axis=(0, 1, 2), dtype=jnp.float32),
            jnp.sum(d_values_low, axis=(0, 1, 2), dtype=jnp.float32),
        )
    ).reshape(bqv_full.shape)
    d_qkv = jnp.stack((d_pre, d_keys_low, d_values_low))
    grad_w_qkv = jnp.einsum(
        "rsid,krsie->kde", normed_one, d_qkv, preferred_element_type=jnp.float32
    )
    d_norm_one = halves(
        jnp.einsum("krsie,kde->rsid", d_qkv, qkv_back, preferred_element_type=jnp.float32)
    )
    d_states_ln, grad_gain_one, grad_shift_one = norm_one_back(d_norm_one)
    grad_states = (d_hidden + d_states_ln).astype(jnp.bfloat16)
    attn_grads = (
        lax.psum_scatter(grad_w_qkv, ("rows", "seq"), scatter_dimension=1, tiled=True),
        lax.psum_scatter(grad_w_out, ("rows", "seq"), scatter_dimension=1, tiled=True),
        lax.psum_scatter(grad_bias_qv, ("rows", "seq"), scatter_dimension=2, tiled=True),
        lax.psum_scatter(grad_gain_one, ("rows", "seq"), scatter_dimension=0, tiled=True),
        lax.psum_scatter(grad_shift_one, ("rows", "seq"), scatter_dimension=0, tiled=True),
        lax.psum_scatter(grad_bias_out, ("rows", "seq"), scatter_dimension=0, tiled=True),
    )
    return (
        out_states,
        grad_states,
        attn_grads[0],
        attn_grads[1],
        ffn_grads[0],
        ffn_grads[1],
        attn_grads[2],
        attn_grads[5],
        ffn_grads[2],
        ffn_grads[5],
        attn_grads[3],
        attn_grads[4],
        ffn_grads[3],
        ffn_grads[4],
    )


def opening_kernel(w_ref, s_ref, v_ref, whole_ref, tokens_ref, vectors_ref, z_send, z_recv, x_send, x_recv, y_send, y_recv,
                   fx_send, fx_recv, fy_send, fy_recv, t_send, t_recv, c_send, c_recv, v_send, v_recv, own):
    rows, place, core = lax.axis_index("rows"), lax.axis_index("seq"), lax.axis_index("fsdp")
    count = s_ref.shape[0]
    depth = w_ref.shape[1]
    half = w_ref.shape[2] // 2
    width = s_ref.shape[2] // 2
    steps = count - 1

    def at(row, seq, fsdp=None):
        return (row, seq, core if fsdp is None else fsdp)

    def hail(device):
        pl.semaphore_signal(barrier, inc=1, device_id=device, device_id_type=pl.DeviceIdType.MESH)

    barrier = pltpu.get_barrier_semaphore()
    for away in range(4):
        for along in range(count):
            if away or along:
                hail(at(rows ^ away, lax.rem(place + along, count)))
    hail(at(rows, place, 1 - core))
    pl.semaphore_wait(barrier, 4 * count)

    def shard(ref, row, seq, cut=None):
        first = pl.multiple_of((row * count + seq) * depth, depth)
        if cut is None:
            return ref.at[:, pl.ds(first, depth)]
        return ref.at[:, pl.ds(first, depth), pl.ds(cut * half, half)]

    def remote(src, dst, send, recv, device):
        return pltpu.make_async_remote_copy(
            src_ref=src, dst_ref=dst, send_sem=send, recv_sem=recv, device_id=device,
            device_id_type=pl.DeviceIdType.MESH,
        )

    x_peer, y_peer = rows ^ 1, rows ^ 2

    def spread(t, side, seq, src):
        mine = shard(whole_ref, rows, seq)
        src = mine if src is None else src
        return (
            remote(src, mine, x_send.at[t, side], x_recv.at[t, side], at(x_peer, place)),
            remote(src, mine, y_send.at[t, side], y_recv.at[t, side], at(y_peer, place)),
        )

    def arrived(t, side, seq):
        from_x, from_y = shard(whole_ref, x_peer, seq), shard(whole_ref, y_peer, seq)
        return (
            remote(from_x, from_x, x_send.at[t, side], x_recv.at[t, side], at(x_peer, place)),
            remote(from_y, from_y, y_send.at[t, side], y_recv.at[t, side], at(y_peer, place)),
        )

    def onward(t, side, seq):
        a, b = shard(whole_ref, x_peer, seq, 0), shard(whole_ref, y_peer, seq, 1)
        return (
            remote(a, a, fy_send.at[t, side], fy_recv.at[t, side], at(y_peer, place)),
            remote(b, b, fx_send.at[t, side], fx_recv.at[t, side], at(x_peer, place)),
        )

    def far(t, side, seq):
        a, b = shard(whole_ref, rows ^ 3, seq, 0), shard(whole_ref, rows ^ 3, seq, 1)
        return (
            remote(a, a, fy_send.at[t, side], fy_recv.at[t, side], at(y_peer, place)),
            remote(b, b, fx_send.at[t, side], fx_recv.at[t, side], at(x_peer, place)),
        )

    def along_z(t, side, seq, src):
        mine = shard(whole_ref, rows, seq)
        to = place + 1 if side == 0 else place - 1
        return remote(mine if src is None else src, mine, z_send.at[t, side], z_recv.at[t, side], at(rows, to))

    def origin(t, side):
        return place - t if side == 0 else place + t

    def has(t, side):
        return origin(t, side) >= 0 if side == 0 else origin(t, side) < count

    def has_next(side):
        return place + 1 < count if side == 0 else place >= 1

    for side in range(2):
        @pl.when(has_next(side))
        def _(side=side):
            along_z(1, side, place, w_ref).start()
    for copy in spread(0, 0, place, w_ref):
        copy.start()
    local = pltpu.make_async_copy(w_ref, shard(whole_ref, rows, place), own.at[0])
    local.start()
    vectors = []
    for away in range(4):
        for along in range(count):
            if away or along:
                mine = rows * count + place
                copy = remote(
                    v_ref, vectors_ref.at[mine], v_send.at[away, along], v_recv.at[away, along],
                    at(rows ^ away, lax.rem(place + along, count)),
                )
                copy.start()
                vectors.append(copy)
    local_v = pltpu.make_async_copy(v_ref, vectors_ref.at[rows * count + place], own.at[1])
    local_v.start()

    columns = pl.ds(pl.multiple_of(core * width, width), width)

    def token_copy(along):
        to = lax.rem(place + along, count)
        return remote(
            s_ref.at[to, :, columns], tokens_ref.at[place, :, columns], t_send.at[along], t_recv.at[along], at(rows, to)
        )

    def token_got(along):
        start = lax.rem(place + count - along, count)
        view = tokens_ref.at[start, :, columns]
        return remote(view, view, t_send.at[along], t_recv.at[along], at(rows, start))

    def token_on(along):
        view = tokens_ref.at[lax.rem(place + count - along, count), :, columns]
        return remote(view, view, c_send.at[along], c_recv.at[along], at(rows, place, 1 - core))

    def token_far(along):
        start = lax.rem(place + count - along, count)
        view = tokens_ref.at[start, :, pl.ds(pl.multiple_of((1 - core) * width, width), width)]
        return remote(view, view, c_send.at[along], c_recv.at[along], at(rows, place, 1 - core))

    local_t = pltpu.make_async_copy(s_ref.at[place], tokens_ref.at[place], own.at[2])
    local_t.start()

    def pass_on(t, side, seq):
        for got in arrived(t, side, seq):
            got.wait_recv()
        for copy in onward(t, side, seq):
            copy.start()

    for t in range(1, steps + 1):
        for side in range(2):
            @pl.when(has(t, side))
            def _(t=t, side=side):
                seq = origin(t, side)
                along_z(t, side, seq, None).wait_recv()
                if t < steps:
                    @pl.when(has_next(side))
                    def _():
                        along_z(t + 1, side, seq, None).start()
                for copy in spread(t, side, seq, None):
                    copy.start()
        if t == 1:
            for along in range(1, count):
                token_copy(along).start()
            pass_on(0, 0, place)
        else:
            for side in range(2):
                @pl.when(has(t - 1, side))
                def _(t=t, side=side):
                    pass_on(t - 1, side, origin(t - 1, side))
    for side in range(2):
        @pl.when(has(steps, side))
        def _(side=side):
            pass_on(steps, side, origin(steps, side))

    for along in range(1, count):
        token_got(along).wait_recv()
        token_on(along).start()

    def settle(t, side, seq, src):
        for copy in spread(t, side, seq, src):
            copy.wait_send()
        for copy in onward(t, side, seq):
            copy.wait_send()
        for got in far(t, side, seq):
            got.wait_recv()

    settle(0, 0, place, w_ref)
    for t in range(1, steps + 1):
        for side in range(2):
            @pl.when(has(t, side))
            def _(t=t, side=side):
                settle(t, side, origin(t, side), None)

            @pl.when(has(t - 1, side) & has_next(side))
            def _(t=t, side=side):
                along_z(t, side, origin(t - 1, side), w_ref if t == 1 else None).wait_send()
    for copy in vectors:
        copy.wait_send()
    for away in range(4):
        for along in range(count):
            if away or along:
                start = (rows ^ away) * count + lax.rem(place + count - along, count)
                view = vectors_ref.at[start]
                remote(
                    view, view, v_send.at[away, along], v_recv.at[away, along],
                    at(rows ^ away, lax.rem(place + count - along, count)),
                ).wait_recv()
    for along in range(1, count):
        token_copy(along).wait_send()
        token_on(along).wait_send()
        token_far(along).wait_recv()
    local.wait()
    local_v.wait()
    local_t.wait()


def opening(w, tokens, vector):
    count = tokens.shape[0]
    kinds, depth, half = w.shape
    dma = pltpu.SemaphoreType.DMA
    pair = [dma((count, 2)), dma((count, 2))]
    anywhere = pl.BlockSpec(memory_space=pl.ANY)
    return pl.pallas_call(
        opening_kernel,
        in_specs=[anywhere] * 3,
        out_specs=[anywhere] * 3,
        out_shape=[
            jax.ShapeDtypeStruct((kinds, depth * 4 * count, half), w.dtype),
            jax.ShapeDtypeStruct(tokens.shape, tokens.dtype),
            jax.ShapeDtypeStruct((4 * count,) + vector.shape, vector.dtype),
        ],
        scratch_shapes=pair * 5 + [dma((count,))] * 4 + [dma((4, count))] * 2 + [dma((3,))],
        compiler_params=pltpu.CompilerParams(collective_id=0, has_side_effects=True),
    )(w, tokens, vector)


def closing_kernel(s_ref, v_ref, tokens_ref, sum_ref, held, t_send, t_recv, c_send, c_recv, v_send, v_recv, own):
    rows, place, core = lax.axis_index("rows"), lax.axis_index("seq"), lax.axis_index("fsdp")
    count = s_ref.shape[0]
    width = s_ref.shape[2] // 2

    def at(row, seq, fsdp=None):
        return (row, seq, core if fsdp is None else fsdp)

    def hail(device):
        pl.semaphore_signal(barrier, inc=1, device_id=device, device_id_type=pl.DeviceIdType.MESH)

    barrier = pltpu.get_barrier_semaphore()
    for away in range(4):
        for along in range(count):
            if away or along:
                hail(at(rows ^ away, lax.rem(place + along, count)))
    hail(at(rows, place, 1 - core))
    pl.semaphore_wait(barrier, 4 * count)

    def remote(src, dst, send, recv, device):
        return pltpu.make_async_remote_copy(
            src_ref=src, dst_ref=dst, send_sem=send, recv_sem=recv, device_id=device,
            device_id_type=pl.DeviceIdType.MESH,
        )

    columns = pl.ds(pl.multiple_of(core * width, width), width)
    others = pl.ds(pl.multiple_of((1 - core) * width, width), width)

    def token_copy(along):
        to = lax.rem(place + along, count)
        return remote(
            s_ref.at[to, :, columns], tokens_ref.at[place, :, columns], t_send.at[along], t_recv.at[along], at(rows, to)
        )

    def token_got(along):
        start = lax.rem(place + count - along, count)
        view = tokens_ref.at[start, :, columns]
        return remote(view, view, t_send.at[along], t_recv.at[along], at(rows, start))

    def token_on(along):
        view = tokens_ref.at[lax.rem(place + count - along, count), :, columns]
        return remote(view, view, c_send.at[along], c_recv.at[along], at(rows, place, 1 - core))

    def token_far(along):
        view = tokens_ref.at[lax.rem(place + count - along, count), :, others]
        return remote(view, view, c_send.at[along], c_recv.at[along], at(rows, place, 1 - core))

    for along in range(1, count):
        token_copy(along).start()
    local_t = pltpu.make_async_copy(s_ref.at[place], tokens_ref.at[place], own.at[0])
    local_t.start()
    mine = rows * count + place
    vectors = []
    for away in range(4):
        for along in range(count):
            if away or along:
                to_row, to_seq = rows ^ away, lax.rem(place + along, count)
                copy = remote(
                    v_ref.at[to_row * count + to_seq], held.at[away * count + along],
                    v_send.at[away, along], v_recv.at[away, along], at(to_row, to_seq),
                )
                copy.start()
                vectors.append(copy)
    local_v = pltpu.make_async_copy(v_ref.at[mine], held.at[0], own.at[1])
    local_v.start()
    local_v.wait()
    for copy in vectors:
        copy.wait_recv()
    sum_ref[...] = jnp.sum(held[...], axis=0)
    for along in range(1, count):
        token_got(along).wait_recv()
        token_on(along).start()
    for copy in vectors:
        copy.wait_send()
    for along in range(1, count):
        token_copy(along).wait_send()
        token_on(along).wait_send()
        token_far(along).wait_recv()
    local_t.wait()


def closing(tokens, vectors):
    count = tokens.shape[0]
    dma = pltpu.SemaphoreType.DMA
    anywhere = pl.BlockSpec(memory_space=pl.ANY)
    return pl.pallas_call(
        closing_kernel,
        in_specs=[anywhere] * 2,
        out_specs=[anywhere, pl.BlockSpec(memory_space=pltpu.VMEM)],
        out_shape=[
            jax.ShapeDtypeStruct(tokens.shape, tokens.dtype),
            jax.ShapeDtypeStruct(vectors.shape[1:], F32),
        ],
        scratch_shapes=[pltpu.VMEM(vectors.shape, F32)]
        + [dma((count,))] * 4
        + [dma((4, count))] * 2
        + [dma((2,))],
        compiler_params=pltpu.CompilerParams(collective_id=1, has_side_effects=True),
    )(tokens, vectors)


class Move:
    def __init__(self, alongs, src_ref, out_ref, sems):
        self.alongs, self.src, self.out = alongs, src_ref, out_ref
        self.t_send, self.t_recv, self.c_send, self.c_recv = sems
        self.rows, self.place, self.core = [lax.axis_index(name) for name in ("rows", "seq", "fsdp")]
        self.count = src_ref.shape[0]
        self.width = src_ref.shape[2] // 2

    def columns(self, core):
        return pl.ds(pl.multiple_of(core * self.width, self.width), self.width)

    def remote(self, src, dst, send, recv, seq, core):
        return pltpu.make_async_remote_copy(
            src_ref=src, dst_ref=dst, send_sem=send, recv_sem=recv, device_id=(self.rows, seq, core),
            device_id_type=pl.DeviceIdType.MESH,
        )

    def origin(self, along):
        return lax.rem(self.place + self.count - along, self.count)

    def sent(self, n, along):
        to = lax.rem(self.place + along, self.count)
        src, dst = self.src.at[to, :, self.columns(self.core)], self.out.at[self.place, :, self.columns(self.core)]
        return self.remote(src, dst, self.t_send.at[n], self.t_recv.at[n], to, self.core)

    def got(self, n, along):
        start = self.origin(along)
        view = self.out.at[start, :, self.columns(self.core)]
        return self.remote(view, view, self.t_send.at[n], self.t_recv.at[n], start, self.core)

    def passed(self, n, along, mine):
        view = self.out.at[self.origin(along), :, self.columns(self.core if mine else 1 - self.core)]
        return self.remote(view, view, self.c_send.at[n], self.c_recv.at[n], self.place, 1 - self.core)

    def begin(self):
        barrier = pltpu.get_barrier_semaphore()
        peers = sorted(set(self.alongs) | {self.count - along for along in self.alongs})
        for along in peers:
            device = (self.rows, lax.rem(self.place + along, self.count), self.core)
            pl.semaphore_signal(barrier, inc=1, device_id=device, device_id_type=pl.DeviceIdType.MESH)
        device = (self.rows, self.place, 1 - self.core)
        pl.semaphore_signal(barrier, inc=1, device_id=device, device_id_type=pl.DeviceIdType.MESH)
        pl.semaphore_wait(barrier, len(peers) + 1)
        for n, along in enumerate(self.alongs):
            self.sent(n, along).start()

    def end(self):
        for n, along in enumerate(self.alongs):
            self.got(n, along).wait_recv()
            self.passed(n, along, True).start()
        for n, along in enumerate(self.alongs):
            self.sent(n, along).wait_send()
            self.passed(n, along, True).wait_send()
            self.passed(n, along, False).wait_recv()


def product_kernel(mode, finish, n_extra, n_in, move, *refs):
    if move is None:
        return product_step(mode, finish, n_extra, refs[: 2 + n_extra], refs[n_in:-1], refs[-1])
    moving = Move(move, refs[2 + n_extra], refs[n_in + 1], refs[-4:])
    ids = [pl.program_id(n) for n in range(3)]
    ends = [pl.num_programs(n) - 1 for n in range(3)]

    @pl.when((ids[0] == 0) & (ids[1] == 0) & (ids[2] == 0))
    def _():
        moving.begin()

    product_step(mode, finish, n_extra, refs[: 2 + n_extra], refs[n_in : n_in + 1], refs[n_in + 2])

    @pl.when((ids[0] == ends[0]) & (ids[1] == ends[1]) & (ids[2] == ends[2]))
    def _():
        moving.end()


def product_step(mode, finish, n_extra, refs, outs, total):
    a_ref, b_ref = refs[:2]
    extra = refs[2:]
    k = pl.program_id(2)
    last = pl.num_programs(2) - 1
    dims = {"nn": ((1,), (0,)), "nt": ((1,), (1,)), "tn": ((0,), (0,))}[mode]
    part = lax.dot_general(a_ref[...], b_ref[...], (dims, ((), ())), preferred_element_type=F32)
    if last == 0:
        finish(part, extra, outs)
        return

    @pl.when(k == 0)
    def _():
        total[...] = part

    @pl.when((k > 0) & (k < last))
    def _():
        total[...] += part

    @pl.when(k == last)
    def _():
        finish(total[...] + part, extra, outs)


def finish_cast(total, extra, outs):
    outs[0][...] = total.astype(outs[0].dtype)


def finish_bias(scale, total, extra, outs):
    outs[0][...] = ((total + extra[0][...]) * scale).astype(BF)


def product(a, b, mode, finish=finish_cast, rows=(), deps=(), planes=(0,), blocks=(1024, 1024, 2048), move=None):
    plane = len(b.shape) == 3
    b_shape = b.shape[-2:]
    m, depth = a.shape if mode != "tn" else a.shape[::-1]
    n = b_shape[0] if mode == "nt" else b_shape[1]
    bm, bn, bk = min(blocks[0], m), min(blocks[1], n), min(blocks[2], depth)
    spec = pl.BlockSpec
    a_spec = (
        spec((bk, bm), lambda j, i, k: (k, i)) if mode == "tn" else spec((bm, bk), lambda j, i, k: (i, k))
    )
    first, turns = planes[0], len(planes)
    if plane and mode == "nt":
        b_spec = spec((None, bn, bk), lambda j, i, k: (first + k % turns, j, k // turns))
    elif plane:
        b_spec = spec((None, bk, bn), lambda j, i, k: (first, k, j))
    elif mode == "nt":
        b_spec = spec((bn, bk), lambda j, i, k: (j, k))
    else:
        b_spec = spec((bk, bn), lambda j, i, k: (k, j))
    row = spec((1, bn), lambda j, i, k: (0, j))
    field = spec((bm, bn), lambda j, i, k: (i, j))
    out_specs, out_shape = field, jax.ShapeDtypeStruct((m, n), BF)
    scratch, aliases, inputs = [pltpu.VMEM((bm, bn), F32)], {}, (a, b, *rows)
    params = dict(vmem_limit_bytes=48 * 2**20)
    if move is not None:
        src, target, alongs, ident = move
        out_specs, out_shape = (
            [field, spec(memory_space=pl.ANY)],
            [out_shape, jax.ShapeDtypeStruct(src.shape, src.dtype)],
        )
        dma = pltpu.SemaphoreType.DMA
        scratch += [dma((len(alongs),))] * 4
        aliases = {len(inputs) + 1: 1}
        inputs += (src, target)
        params.update(collective_id=ident, has_side_effects=True)
        move = alongs
    n_in = len(inputs) + len(deps)
    return pl.pallas_call(
        functools.partial(product_kernel, mode, finish, len(rows), n_in, move),
        grid=(n // bn, m // bm, depth // bk),
        in_specs=[a_spec, b_spec]
        + [row] * len(rows)
        + [spec(memory_space=pl.ANY)] * (n_in - 2 - len(rows)),
        out_specs=out_specs,
        out_shape=out_shape,
        scratch_shapes=scratch,
        input_output_aliases=aliases,
        cost_estimate=told(2.0 * m * n * depth / 8e8),
        compiler_params=pltpu.CompilerParams(**params),
    )(*inputs, *deps)


def dot_nt(a,b): return lax.dot_general(a,b,(((1,),(1,)),((),())),preferred_element_type=F32)
def dot_nn(a,b): return lax.dot_general(a,b,(((1,),(0,)),((),())),preferred_element_type=F32)

def fwd_kernel(tile, flags, q_ref, k_ref, v_ref, sk_ref, sv_ref, start_ref, doc_ref, sdoc_ref, *rest):
    o_ref, lse_ref, km, vt, acc, top, total = rest[-7:]
    i = pl.program_id(1)
    seg = k_ref.shape[0]
    lanes = lax.broadcasted_iota(jnp.int32, (1, 128), 1)
    masks = [(lanes < HEAD).astype(BF), (lanes >= HEAD).astype(BF)]
    @pl.when(i == 0)
    def _():
        for h in range(2):
            km[h, pl.ds(0, seg)] = k_ref[...] * masks[h]
            km[h, pl.ds(seg, 128)] = sk_ref[...] * masks[h]
        vt[:, pl.ds(0, seg)] = v_ref[...].T
        vt[:, pl.ds(seg, 128)] = sv_ref[...].T
    q = q_ref[...]
    allowed = sdoc_ref[...] == doc_ref[...]
    for h in range(2):
        s = dot_nt(km[h, pl.ds(seg, 128)], q)
        s = jnp.where(allowed, s, neg_big)
        m = jnp.max(s, axis=0, keepdims=True)
        p = jnp.where(allowed, jnp.exp(s - m), 0.0)
        top[h] = m
        total[h] = jnp.sum(p, axis=0, keepdims=True)
        acc[h] = dot_nn(vt[pl.ds(h * HEAD, HEAD), pl.ds(seg, 128)], p.astype(BF))
    def step(j, masked):
        at = pl.multiple_of(j * tile, tile)
        if masked:
            places = at + lax.broadcasted_iota(jnp.int32, (tile, tile), 0)
            mine = i * tile + lax.broadcasted_iota(jnp.int32, (tile, tile), 1)
            okay = (places <= mine) & (places >= start_ref[...])
        ss=[]
        for h in range(2):
            s = dot_nt(km[h, pl.ds(at, tile)], q)
            if masked:
                s = jnp.where(okay, s, neg_big)
            ss.append(s)
        for h in range(2):
            s = ss[h]
            m_old = top[h]
            m = jnp.maximum(m_old, jnp.max(s, axis=0, keepdims=True))
            p = jnp.exp(s - m)
            if masked:
                p = jnp.where(okay, p, 0.0)
            alpha = jnp.exp(m_old - m)
            top[h] = m
            total[h] = total[h] * alpha + jnp.sum(p, axis=0, keepdims=True)
            acc[h] = acc[h] * alpha + dot_nn(vt[pl.ds(h * HEAD, HEAD), pl.ds(at, tile)], p.astype(BF))
    count = pl.num_programs(1)
    def loop(j, _):
        flag = flags[i * count + j]
        @pl.when(flag == 2)
        def _(): step(j, False)
        @pl.when(flag == 1)
        def _(): step(j, True)
        return 0
    lax.fori_loop(0, i + 1, loop, 0)
    out = [acc[h] / total[h] for h in range(2)]
    o_ref[...] = jnp.concatenate(out, axis=0).T.astype(BF)
    for h in range(2):
        lse_ref[0, pl.ds(h, 1)] = top[h] + jnp.log(total[h])

def attn_fwd(q, k, v, sk, sv, start, doc, sdoc, flags, tile, base, pairs, earlier_out=(), deps=()):
    seg, width = q.shape
    count = seg // tile
    spec = pl.BlockSpec
    extra = tuple(earlier_out) + tuple(deps)
    return pl.pallas_call(
        functools.partial(fwd_kernel, tile),
        grid_spec=pltpu.PrefetchScalarGridSpec(
            num_scalar_prefetch=1,
            grid=(pairs, count),
            in_specs=[
                spec((tile, 128), lambda h, i, f: (i, h + base)),
                spec((seg, 128), lambda h, i, f: (0, h + base)),
                spec((seg, 128), lambda h, i, f: (0, h + base)),
                spec((128, 128), lambda h, i, f: (0, h + base)),
                spec((128, 128), lambda h, i, f: (0, h + base)),
                spec((1, tile), lambda h, i, f: (0, i)),
                spec((1, tile), lambda h, i, f: (0, i)),
                spec((128, 1), lambda h, i, f: (0, 0)),
            ]
            + [spec(memory_space=pl.ANY)] * len(extra),
            out_specs=[
                spec((tile, 128), lambda h, i, f: (i, h + base)),
                spec((1, 2, tile), lambda h, i, f: (h + base, 0, i)),
            ],
            scratch_shapes=[
                pltpu.VMEM((2, seg + 128, 128), BF),
                pltpu.VMEM((128, seg + 128), BF),
                pltpu.VMEM((2, HEAD, tile), F32),
                pltpu.VMEM((2, 1, tile), F32),
                pltpu.VMEM((2, 1, tile), F32),
            ],
        ),
        out_shape=[
            jax.ShapeDtypeStruct((seg, width), BF),
            jax.ShapeDtypeStruct((width // 128, 2, seg), F32),
        ],
        input_output_aliases={9: 0, 10: 1} if earlier_out else {},
        cost_estimate=told(4.2 * pairs * 4),
        compiler_params=pltpu.CompilerParams(vmem_limit_bytes=40 * 2**20),
    )(flags, q, k, v, sk, sv, start, doc, sdoc, *extra)


def bwd_kernel(tile, flags, q_ref, k_ref, v_ref, do_ref, o_ref, sk_ref, sv_ref, lse_ref, start_ref, doc_ref, sdoc_ref, *rest):
    dq_ref, dk_ref, dv_ref, dsk_ref, dsv_ref, qm, dom, dqt, delta = rest[-9:]
    j = pl.program_id(1)
    seg = q_ref.shape[0]
    count = seg // tile
    lanes = lax.broadcasted_iota(jnp.int32, (1, 128), 1)
    masks = [(lanes < HEAD).astype(BF), (lanes >= HEAD).astype(BF)]
    @pl.when(j == 0)
    def _():
        dqt[...] = jnp.zeros_like(dqt)
        for h in range(2):
            qm[h] = q_ref[...] * masks[h]
            dom[h] = do_ref[...] * masks[h]
        def one(i, _):
            at = pl.multiple_of(i * tile, tile)
            prod = (do_ref[pl.ds(at, tile)].astype(F32) * o_ref[pl.ds(at, tile)].astype(F32)).T
            for h in range(2):
                delta[h, :, pl.ds(at, tile)] = jnp.sum(prod[h * HEAD:(h + 1) * HEAD], axis=0, keepdims=True)
            return 0
        lax.fori_loop(0, count, one, 0)
    def block(i, kt, k_blk, v_blk, okay):
        at = pl.multiple_of(i * tile, tile)
        gk = gv = None
        for h in range(2):
            qh = qm[h, pl.ds(at, tile)]
            dh = dom[h, pl.ds(at, tile)]
            s = dot_nt(k_blk, qh)
            dp = dot_nt(v_blk, dh)
            p = jnp.exp(s - lse_ref[0, pl.ds(h, 1), pl.ds(at, tile)])
            if okay is not None:
                p = jnp.where(okay, p, 0.0)
            ds = (p * (dp - delta[h, :, pl.ds(at, tile)])).astype(BF)
            a = dot_nn(p.astype(BF), dh)
            b = dot_nn(ds, qh)
            gv = a if gv is None else gv + a
            gk = b if gk is None else gk + b
            dqt[pl.ds(h * HEAD, HEAD), pl.ds(at, tile)] += dot_nn(kt[h * HEAD:(h + 1) * HEAD], ds)
        return gk, gv
    @pl.when(j < count)
    def _():
        at_k = pl.multiple_of(j * tile, tile)
        k_blk = k_ref[...]
        v_blk = v_ref[...]
        kt = k_blk.T
        def masked_of(i):
            places = at_k + lax.broadcasted_iota(jnp.int32, (tile, tile), 0)
            mine = i * tile + lax.broadcasted_iota(jnp.int32, (tile, tile), 1)
            return (places <= mine) & (places >= start_ref[:, pl.ds(pl.multiple_of(i * tile, tile), tile)])
        gk, gv = block(j, kt, k_blk, v_blk, masked_of(j))
        dkacc, dvacc = gk, gv
        def loop(i, carry):
            flag = flags[i * count + j]
            def full(c):
                gk, gv = block(i, kt, k_blk, v_blk, None)
                return c[0] + gk, c[1] + gv
            def part(c):
                gk, gv = block(i, kt, k_blk, v_blk, masked_of(i))
                return c[0] + gk, c[1] + gv
            return lax.switch(flag, [lambda c: c, part, full], carry)
        dkacc, dvacc = lax.fori_loop(j + 1, count, loop, (dkacc, dvacc))
        dk_ref[...] = dkacc.astype(BF)
        dv_ref[...] = dvacc.astype(BF)
    @pl.when(j == count)
    def _():
        kt = sk_ref[...].T
        def loop(i, carry):
            okay = sdoc_ref[...] == doc_ref[:, pl.ds(pl.multiple_of(i * tile, tile), tile)]
            gk, gv = block(i, kt, sk_ref[...], sv_ref[...], okay)
            return carry[0] + gk, carry[1] + gv
        z = jnp.zeros((128, 128), F32)
        a, b = lax.fori_loop(0, count, loop, (z, z))
        dsk_ref[...] = a.astype(BF)
        dsv_ref[...] = b.astype(BF)
        def fin(i, _):
            at = pl.multiple_of(i * tile, tile)
            dq_ref[pl.ds(at, tile)] = (dqt[:, pl.ds(at, tile)].T.astype(BF).astype(F32) * HEAD ** -0.5).astype(BF)
            return 0
        lax.fori_loop(0, count, fin, 0)

def attn_bwd(q, k, v, do, o, sk, sv, lse, start, doc, sdoc, flags, tile, base, pairs, deps=()):
    seg = q.shape[0]
    count = seg // tile
    last = count - 1
    spec = pl.BlockSpec
    return pl.pallas_call(
        functools.partial(bwd_kernel, tile),
        grid_spec=pltpu.PrefetchScalarGridSpec(
            num_scalar_prefetch=1,
            grid=(pairs, count + 1),
            in_specs=[
                spec((seg, 128), lambda h, j, f: (0, h + base)),
                spec((tile, 128), lambda h, j, f: (jnp.minimum(j, last), h + base)),
                spec((tile, 128), lambda h, j, f: (jnp.minimum(j, last), h + base)),
                spec((seg, 128), lambda h, j, f: (0, h + base)),
                spec((seg, 128), lambda h, j, f: (0, h + base)),
                spec((128, 128), lambda h, j, f: (0, h + base)),
                spec((128, 128), lambda h, j, f: (0, h + base)),
                spec((1, 2, seg), lambda h, j, f: (h + base, 0, 0)),
                spec((1, seg), lambda h, j, f: (0, 0)),
                spec((1, seg), lambda h, j, f: (0, 0)),
                spec((128, 1), lambda h, j, f: (0, 0)),
            ]
            + [spec(memory_space=pl.ANY)] * len(deps),
            out_specs=[
                spec((seg, 128), lambda h, j, f: (0, h)),
                spec((tile, 128), lambda h, j, f: (jnp.minimum(j, last), h)),
                spec((tile, 128), lambda h, j, f: (jnp.minimum(j, last), h)),
                spec((128, 128), lambda h, j, f: (0, h)),
                spec((128, 128), lambda h, j, f: (0, h)),
            ],
            scratch_shapes=[
                pltpu.VMEM((2, seg, 128), BF),
                pltpu.VMEM((2, seg, 128), BF),
                pltpu.VMEM((128, seg), F32),
                pltpu.VMEM((2, 1, seg), F32),
            ],
        ),
        out_shape=[jax.ShapeDtypeStruct((seg, pairs * 128), BF)] * 3
        + [jax.ShapeDtypeStruct((128, pairs * 128), BF)] * 2,
        cost_estimate=told(5.5 * pairs * 4),
        compiler_params=pltpu.CompilerParams(vmem_limit_bytes=40 * 2**20),
    )(flags, q, k, v, do, o, sk, sv, lse, start, doc, sdoc, *deps)


def make_meta(doc, tile):
    seg=doc.shape[0]; count=seg//tile
    place=jnp.arange(seg,dtype=jnp.int32)
    new=jnp.concatenate([jnp.ones((1,),bool), doc[1:]!=doc[:-1]])
    start=lax.cummax(jnp.where(new,place,0))
    lo=doc[::tile]; hi=doc[tile-1::tile]
    i=jnp.arange(count)
    full=(lo[None,:]==hi[:,None])&(i[None,:]<i[:,None])
    none=(hi[None,:]<lo[:,None])
    flags=jnp.where(full,2,jnp.where(none,0,1)).astype(jnp.int32).reshape(-1)
    return start.reshape(1,seg), flags


def gate(value, *deps):
    anywhere = pl.BlockSpec(memory_space=pl.ANY)
    return pl.pallas_call(
        lambda *refs: None,
        in_specs=[anywhere] * (1 + len(deps)),
        out_specs=anywhere,
        out_shape=jax.ShapeDtypeStruct(value.shape, value.dtype),
        input_output_aliases={0: 0},
        cost_estimate=SMALL_COST,
    )(value, *deps)


def blank(shape, dtype):
    return pl.pallas_call(
        lambda ref: None,
        out_specs=pl.BlockSpec(memory_space=pl.ANY),
        out_shape=jax.ShapeDtypeStruct(shape, dtype),
        cost_estimate=SMALL_COST,
    )()


BOTH = ("rows", "seq")


def other_core(block):
    return lax.ppermute(block, "fsdp", ((0, 1), (1, 0)))


def along_line(field, hold=()):
    count = lax.axis_size("seq")
    me = lax.axis_index("seq")
    core = lax.axis_index("fsdp")
    half = field.shape[2] // 2
    mine = lax.dynamic_slice_in_dim(field, core * half, half, 2)
    got = jnp.zeros_like(mine)
    own = lax.dynamic_slice_in_dim(mine, me, 1, 0)
    got = lax.dynamic_update_slice_in_dim(got, own, me, 0)
    for away in range(1, count):
        block = lax.dynamic_slice_in_dim(mine, lax.rem(me + away, count), 1, 0)
        moved = lax.ppermute(block, "seq", [(n, (n + away) % count) for n in range(count)])
        moved = gate(moved, *hold) if hold else moved
        got = lax.dynamic_update_slice_in_dim(got, moved, lax.rem(me + count - away, count), 0)
    return got


def between_cores(got, hold=()):
    core = lax.axis_index("fsdp")
    other = other_core(got)
    other = gate(other, *hold) if hold else other
    low_half = jnp.where(core == 0, got, other)
    high_half = jnp.where(core == 0, other, got)
    return jnp.concatenate((low_half, high_half), axis=2)


def shift_by(field, away):
    count = lax.axis_size("seq")
    perm = [(n, n + away) for n in range(count) if 0 <= n + away < count]
    return lax.ppermute(field, "seq", perm)


def both_halves(field):
    low = field.astype(BF)
    return low.astype(F32) + other_core(low).astype(F32)


def norm_forward(field, gain_vec, shift_vec):
    row_mean = jnp.mean(field, axis=-1, keepdims=True)
    centered = field - row_mean
    variance = jnp.mean(centered * centered, axis=-1, keepdims=True)
    scale = lax.rsqrt(variance + norm_eps)
    return (centered * scale * gain_vec + shift_vec).astype(BF), row_mean, scale


def norm_backward(field, row_mean, scale, gain_vec, grad):
    unit = (field - row_mean) * scale
    scaled = grad * gain_vec
    mean_one = jnp.mean(scaled, axis=-1, keepdims=True)
    mean_two = jnp.mean(scaled * unit, axis=-1, keepdims=True)
    d_field = scale * (scaled - mean_one - unit * mean_two)
    return d_field, jnp.sum(grad * unit, axis=0), jnp.sum(grad, axis=0)


def mm(a, b):
    return dot_nn(a, b)


def mm_tn(a, b):
    return lax.dot_general(a, b, (((0,), (0,)), ((), ())), preferred_element_type=F32)


def mm_nt(a, b):
    return dot_nt(a, b)


def layer_by_segment(
    states,
    doc_ids,
    w_qkv,
    w_out,
    w_up,
    w_down,
    bias_qv,
    bias_out,
    bias_up,
    bias_down,
    gain_one,
    shift_one,
    gain_two,
    shift_two,
    cotangent,
):
    segs, width, model = states.shape[1:]
    seg_len = segs * width
    place = lax.axis_index("seq")
    half = w_qkv.shape[2]
    hidden_units = w_up.shape[1]
    tile = 512

    small = (bias_qv, bias_out, bias_up, bias_down, gain_one, shift_one, gain_two, shift_two)
    sizes = [item.size for item in small]
    vector = jnp.concatenate([item.reshape(-1) for item in small])
    room = -(-vector.shape[0] // 2048) * 2048
    vector = jnp.pad(vector, (0, room - vector.shape[0])).reshape(-1, 128)
    attn_weights = jnp.concatenate((w_qkv, w_out.T[None]), axis=0)
    attn_full, tokens, packed = opening(attn_weights, states[0], vector)
    tokens = tokens.reshape(seg_len, model)
    packed = packed.reshape(packed.shape[0], -1)
    cuts = []
    at = 0
    for size in sizes:
        cuts.append(packed[:, at : at + size].astype(F32))
        at += size
    shards = packed.shape[0]

    def spread_last(field, lead):
        return jnp.moveaxis(field.reshape(shards, *lead, -1), 0, len(lead)).reshape(-1)

    bias_pair = jnp.moveaxis(cuts[0].reshape(shards, 2, half // HEAD, -1), 0, 2).reshape(2, half)
    bias_o = cuts[1].reshape(-1)
    bias_u = spread_last(cuts[2], (hidden_units // HEAD,))
    bias_d = cuts[3].reshape(-1)
    gain_a, shift_a, gain_b, shift_b = [item.reshape(-1) for item in cuts[4:]]

    docs = doc_ids[0]
    my_docs = lax.dynamic_index_in_dim(docs, place, 0, keepdims=False)
    start, flags = make_meta(my_docs, tile)
    tails = docs[:, seg_len - SUMM :]
    before_one = lax.dynamic_index_in_dim(tails, jnp.maximum(place - 1, 0), 0, keepdims=False)
    before_two = lax.dynamic_index_in_dim(tails, jnp.maximum(place - 2, 0), 0, keepdims=False)
    sum_docs = jnp.concatenate(
        (
            jnp.where(place >= 1, before_one, -1),
            jnp.where(place >= 2, before_two, -1),
            jnp.full((128 - 2 * SUMM,), -1, jnp.int32),
        )
    ).reshape(128, 1)
    doc_row = my_docs.reshape(1, seg_len)

    tokens_f = tokens.astype(F32)
    normed_one, mean_one, scale_one = norm_forward(tokens_f, gain_a, shift_a)
    query = product(
        normed_one, attn_full, "nn", functools.partial(finish_bias, HEAD**-0.5), (bias_pair[:1],), planes=(0,)
    )
    keys = product(normed_one, attn_full, "nn", planes=(1,))
    values = product(
        normed_one, attn_full, "nn", functools.partial(finish_bias, 1.0), (bias_pair[1:],), planes=(2,)
    )
    up_full = lax.all_gather(gate(w_up, normed_one), BOTH, axis=0, tiled=True)
    tail = jnp.stack((keys[seg_len - SUMM :], values[seg_len - SUMM :]))
    lent = jnp.concatenate((shift_by(tail, 1), shift_by(tail, 2)), axis=1)
    lent = jnp.pad(lent, ((0, 0), (0, 128 - 2 * SUMM), (0, 0)))
    pairs = half // 128
    each = pairs // 4
    attended = ()
    done = []
    for n in range(4):
        attended = attn_fwd(
            query, keys, values, lent[0], lent[1], start, doc_row, sum_docs, flags, tile,
            n * each, each, attended,
        )
        done.append(attended[1])
    down_full = lax.all_gather(gate(w_down.T, values), BOTH, axis=0, tiled=True)
    mixed, log_sum = attended
    attended = product(mixed, attn_full, "nt", planes=(3,))
    grad_out = along_line(gate(cotangent[0], query), (done[2],))
    grad_out = between_cores(grad_out, (attended,)).reshape(seg_len, model)
    hidden = tokens_f + both_halves(attended) + bias_o
    normed_two, mean_two, scale_two = norm_forward(hidden, gain_b, shift_b)
    up_proj = mm(normed_two, up_full) + bias_u
    bell = jnp.exp(-0.5 * up_proj * up_proj)
    area = 0.5 * (1.0 + lax.erf(up_proj * (0.5**0.5)))
    activated = (up_proj * area).astype(BF)
    slope = (area + up_proj * bell * 0.3989422804014327).astype(BF)

    def over_rows(partial):
        return lax.psum_scatter(partial, "rows", scatter_dimension=0, tiled=True)

    def over_seq(partial):
        return lax.psum_scatter(partial, "seq", scatter_dimension=0, tiled=True)

    down_sum = product(grad_out, activated, "tn")
    down_rows = over_rows(down_sum)
    slope = gate(slope, down_sum)
    d_up = (mm(grad_out, down_full) * slope.astype(F32)).astype(BF)
    up_sum = product(normed_two, d_up, "tn")
    d_norm_part = product(d_up, up_full, "nt", deps=(up_sum,))
    d_norm_other = other_core(d_norm_part)
    up_turn = gate(up_sum, down_rows, d_norm_other)
    up_rows = over_rows(up_turn)
    d_norm_two = d_norm_part.astype(F32) + d_norm_other.astype(F32)
    d_hidden_ln, grad_gain_two, grad_shift_two = norm_backward(
        hidden, mean_two, scale_two, gain_b, d_norm_two
    )
    d_hidden = grad_out.astype(F32) + d_hidden_ln
    d_hidden_low = d_hidden.astype(BF)
    d_mixed = product(d_hidden_low, attn_full, "nn", deps=(up_turn,), planes=(3,))
    out_sum = product(d_hidden_low, mixed, "tn", deps=(d_mixed,))

    def back(n, count, deps):
        return attn_bwd(
            query, keys, values, d_mixed, mixed, lent[0], lent[1], log_sum, start, doc_row,
            sum_docs, flags, tile, n * each, count * each, deps,
        )

    def own_half(pieces, move, deps=()):
        d_pre, d_keys, d_values, d_lent_k, d_lent_v = [
            jnp.concatenate(pair, axis=1) if len(pair) > 1 else pair[0] for pair in zip(*pieces)
        ]
        d_lent = jnp.stack((d_lent_k, d_lent_v))
        back_home = shift_by(d_lent[:, :SUMM], -1).astype(F32) + shift_by(
            d_lent[:, SUMM : 2 * SUMM], -2
        ).astype(F32)
        ends = jnp.stack((d_keys[seg_len - SUMM :], d_values[seg_len - SUMM :])).astype(F32)
        ends = (ends + back_home).astype(BF)
        d_keys = lax.dynamic_update_slice(d_keys, ends[0], (seg_len - SUMM, 0))
        d_values = lax.dynamic_update_slice(d_values, ends[1], (seg_len - SUMM, 0))
        grads = jnp.concatenate((d_pre, d_keys, d_values), axis=1)
        return grads, product(
            normed_one, grads, "tn", blocks=(1024, grads.shape[1] // 2, 2048), move=move, deps=deps
        )

    piece_0 = back(0, 1, (out_sum,))
    out_partial = product(activated, down_full, "nt", deps=(piece_0[0],))
    down_turn = gate(down_rows, up_rows, out_partial)
    down_seq = over_seq(down_turn)
    grad_w_down = down_seq.astype(F32)
    out_tokens = (hidden + both_halves(out_partial) + bias_d).astype(BF).reshape(segs, width, model)
    out_own = lax.dynamic_slice_in_dim(out_tokens, place, 1, 0)
    out_begun = lax.dynamic_update_slice_in_dim(blank(out_tokens.shape, BF), out_own, place, 0)
    piece_1 = back(1, 1, (down_turn, out_begun))
    out_turn = gate(out_sum, down_seq, piece_1[0])
    out_rows = over_rows(out_turn)
    first_half, (first_sum, out_moved) = own_half((piece_0, piece_1), (out_tokens, out_begun, (1,), 2), (out_turn,))
    up_turn_two = gate(up_rows, out_rows, first_sum)
    up_seq = over_seq(up_turn_two)
    grad_w_up = up_seq.astype(F32)
    first_turn = gate(first_sum, up_turn_two)
    first_rows = over_rows(first_turn)
    piece_2 = back(2, 2, (first_turn,))
    second_half, (second_sum, out_moved) = own_half((piece_2,), (out_tokens, out_moved, (segs - 1,), 3))
    second_turn = gate(second_sum, first_rows, up_seq)
    second_rows = over_rows(second_turn)
    d_qkv = jnp.concatenate((first_half, second_half), axis=1)
    d_norm_part, out_moved = product(
        d_qkv, attn_full, "nt", deps=(second_turn,), blocks=(1024, 1024, half // 2), planes=(0, 1, 2),
        move=(out_tokens, out_moved, tuple(range(2, segs - 1)), 4),
    )
    out_states = out_moved[None]
    d_norm_other = other_core(d_norm_part)
    d_norm_one = d_norm_part.astype(F32) + d_norm_other.astype(F32)
    out_seq = over_seq(gate(out_rows, second_turn))
    grad_w_down = grad_w_down.T
    d_tokens_ln, grad_gain_one, grad_shift_one = norm_backward(
        tokens_f, mean_one, scale_one, gain_a, d_norm_one
    )
    grad_tokens = (d_hidden + d_tokens_ln).astype(BF)
    qkv_rows = gate(jnp.concatenate((first_rows, gate(second_rows, d_norm_other)), axis=1), d_norm_other)
    grad_w_qkv = over_seq(qkv_rows).astype(F32)
    grad_w_out = gate(out_seq, grad_tokens).astype(F32)
    grad_w_qkv = jnp.transpose(grad_w_qkv.reshape(-1, 2, 3, half // 2), (2, 0, 1, 3)).reshape(3, -1, half)
    grad_w_out = grad_w_out.T
    def column_sum(field):
        return jnp.sum(field.astype(F32), axis=0)

    kind_sum = column_sum(d_qkv).reshape(2, 3, half // 2)
    sums = (
        jnp.moveaxis(
            jnp.stack((kind_sum[:, 0], kind_sum[:, 2])).reshape(2, half // HEAD, shards, -1), 2, 0
        ),
        column_sum(d_hidden),
        jnp.moveaxis(column_sum(d_up).reshape(hidden_units // HEAD, shards, -1), 1, 0),
        column_sum(grad_out),
        grad_gain_one,
        grad_shift_one,
        grad_gain_two,
        grad_shift_two,
    )
    vectors = jnp.concatenate([item.reshape(shards, -1) for item in sums], axis=1)
    vectors = jnp.pad(vectors, ((0, 0), (0, room - vectors.shape[1]))).reshape(shards, -1, 128)
    grad_states, vector = closing(grad_tokens.reshape(segs, width, model), gate(vectors, qkv_rows))
    grad_states = grad_states[None]
    vector = vector.reshape(-1)
    small_grads = []
    at = 0
    for item, size in zip(small, sizes):
        small_grads.append(vector[at : at + size].reshape(item.shape))
        at += size
    return (out_states, grad_states, grad_w_qkv, grad_w_out, grad_w_up, grad_w_down, *small_grads)


def solution(mesh):
    whole_segments = mesh.shape["seq"] == SEGS and mesh.shape["rows"] == 4
    return jax.shard_map(
        layer_by_segment if whole_segments else local,
        mesh=mesh,
        in_specs=(
            P("rows", None, "seq", None),
            P("rows", None, None),
            P(None, ("rows", "seq"), "fsdp"),
            P("fsdp", ("rows", "seq")),
            P(("rows", "seq"), "fsdp"),
            P("fsdp", ("rows", "seq")),
            P(None, "fsdp", ("rows", "seq")),
            P(("rows", "seq")),
            P("fsdp", ("rows", "seq")),
            P(("rows", "seq")),
            P(("rows", "seq")),
            P(("rows", "seq")),
            P(("rows", "seq")),
            P(("rows", "seq")),
            P("rows", None, "seq", None),
        ),
        out_specs=(
            P("rows", None, "seq", None),
            P("rows", None, "seq", None),
            P(None, ("rows", "seq"), "fsdp"),
            P("fsdp", ("rows", "seq")),
            P(("rows", "seq"), "fsdp"),
            P("fsdp", ("rows", "seq")),
            P(None, "fsdp", ("rows", "seq")),
            P(("rows", "seq")),
            P("fsdp", ("rows", "seq")),
            P(("rows", "seq")),
            P(("rows", "seq")),
            P(("rows", "seq")),
            P(("rows", "seq")),
            P(("rows", "seq")),
        ),
        check_vma=False,
    )
```

```python
import functools

import jax
import jax.numpy as jnp
from jax import lax
from jax.experimental import pallas as pl
from jax.experimental.pallas import tpu as pltpu
from jax.sharding import PartitionSpec as P

HEAD = 64
SUMM = 50
SEGS = 4
F32 = jnp.float32
BF = jnp.bfloat16
SMALL_COST = pl.CostEstimate(flops=1000, bytes_accessed=1000, transcendentals=0)


def told(microseconds):
    return pl.CostEstimate(flops=int(microseconds * 1e9), bytes_accessed=1000, transcendentals=0)


neg_big = -1e30
norm_eps = 1e-05


def spread(block, axis, source):
    block = jnp.where(lax.axis_index(axis) == source, block, jnp.zeros_like(block))
    return lax.psum(block, axis)


def layer_norm(field, gain_vec, shift_vec):
    row_mean = jnp.mean(field, axis=-1, keepdims=True)
    centered = field - row_mean
    variance = jnp.mean(centered * centered, axis=-1, keepdims=True)
    return centered * lax.rsqrt(variance + norm_eps) * gain_vec + shift_vec


def gelu_exact(field):
    return jax.nn.gelu(field, approximate=False)


def earlier(field, offset, fill_value):
    widths = tuple(((offset, 0) if dim_index == 1 else (0, 0) for dim_index in range(field.ndim)))
    return jnp.pad(field, widths, constant_values=fill_value)[:, : field.shape[1]]


def later(field, offset):
    widths = tuple(((0, offset) if dim_index == 1 else (0, 0) for dim_index in range(field.ndim)))
    return jnp.pad(field, widths)[:, offset:]


def lead(field):
    return jnp.moveaxis(field, 1, 0)


def halves(field):
    return lax.psum(field.astype(jnp.bfloat16), "fsdp").astype(jnp.float32)


def local(
    states,
    doc_ids,
    w_qkv,
    w_out,
    w_up,
    w_down,
    bias_qv,
    bias_out,
    bias_up,
    bias_down,
    gain_one,
    shift_one,
    gain_two,
    shift_two,
    cotangent,
):
    attn_full = (
        lax.all_gather(w_qkv, ("rows", "seq"), axis=1, tiled=True),
        lax.all_gather(w_out, ("rows", "seq"), axis=1, tiled=True),
        lax.all_gather(bias_qv, ("rows", "seq"), axis=2, tiled=True),
        lax.all_gather(gain_one, ("rows", "seq"), axis=0, tiled=True),
        lax.all_gather(shift_one, ("rows", "seq"), axis=0, tiled=True),
        lax.all_gather(bias_out, ("rows", "seq"), axis=0, tiled=True),
    )
    qkv_full, out_full, bqv_full, gain_a, shift_a, bias_o = attn_full
    rows_dev, seg_count, width, model = states.shape
    seq_count = lax.axis_size("seq")
    seq_place = lax.axis_index("seq")
    seg_len = width * seq_count
    half_width = qkv_full.shape[2]
    heads_loc = half_width // HEAD
    score_scale = HEAD ** (-0.5)
    states_f = states.astype(jnp.float32)
    normed_f, norm_one_back = jax.vjp(
        layer_norm, states_f, gain_a.astype(jnp.float32), shift_a.astype(jnp.float32)
    )
    normed_one = normed_f.astype(jnp.bfloat16)
    projected = jnp.einsum(
        "rsid,kde->krsie", normed_one, qkv_full, preferred_element_type=jnp.float32
    )
    bias_pair = bqv_full.astype(jnp.float32).reshape(2, half_width)
    query = ((projected[0] + bias_pair[0]) * score_scale).astype(jnp.bfloat16)
    keys = projected[1].astype(jnp.bfloat16)
    values = (projected[2] + bias_pair[1]).astype(jnp.bfloat16)
    tail = jnp.stack((keys[:, :, width - SUMM :], values[:, :, width - SUMM :]))
    summary = spread(tail, "seq", seq_count - 1)
    sum_keys = jnp.concatenate((earlier(summary[0], 1, 0.0), earlier(summary[0], 2, 0.0)), axis=2)
    sum_values = jnp.concatenate((earlier(summary[1], 1, 0.0), earlier(summary[1], 2, 0.0)), axis=2)
    sum_src = doc_ids[:, :, seg_len - SUMM :]
    sum_docs = jnp.concatenate((earlier(sum_src, 1, -1), earlier(sum_src, 2, -1)), axis=2)
    sum_k5 = sum_keys.reshape(rows_dev, seg_count, 2 * SUMM, heads_loc, HEAD)
    sum_v5 = sum_values.reshape(rows_dev, seg_count, 2 * SUMM, heads_loc, HEAD)
    first_pos = seq_place * width
    query_docs = lax.dynamic_slice_in_dim(doc_ids, first_pos, width, 2)
    query_pos = first_pos + jnp.arange(width, dtype=jnp.int32)
    query5 = query.reshape(rows_dev, seg_count, width, heads_loc, HEAD)
    sum_allowed = (query_docs[:, :, :, None] == sum_docs[:, :, None, :])[:, :, None]
    sum_scores = jnp.einsum(
        "rsihe,rsjhe->rshij", query5, sum_k5, preferred_element_type=jnp.float32
    )
    sum_scores = jnp.where(sum_allowed, sum_scores, neg_big)
    start_max = jnp.max(sum_scores, axis=-1)
    start_exp = jnp.where(sum_allowed, jnp.exp(sum_scores - start_max[..., None]), 0.0)
    start_sum = jnp.sum(start_exp, axis=-1)
    start_acc = jnp.einsum(
        "rshij,rsjhe->rsihe",
        start_exp.astype(jnp.bfloat16),
        sum_v5,
        preferred_element_type=jnp.float32,
    )
    key_piece = lax.all_gather(keys, "seq", axis=2, tiled=True)
    value_piece = lax.all_gather(values, "seq", axis=2, tiled=True)
    count = key_piece.shape[2]
    key5 = key_piece.reshape(rows_dev, seg_count, count, heads_loc, HEAD)
    value5 = value_piece.reshape(rows_dev, seg_count, count, heads_loc, HEAD)
    key_pos = jnp.arange(count, dtype=jnp.int32)
    causal = (key_pos[None, :] <= query_pos[:, None])[None, None, None]
    allowed = causal & (query_docs[:, :, :, None] == doc_ids[:, :, None, :])[:, :, None]
    scores = jnp.einsum("rsihe,rsjhe->rshij", query5, key5, preferred_element_type=jnp.float32)
    scores = jnp.where(allowed, scores, neg_big)
    new_max = jnp.maximum(start_max, jnp.max(scores, axis=-1))
    factor = jnp.exp(start_max - new_max)
    exponent = jnp.where(allowed, jnp.exp(scores - new_max[..., None]), 0.0)
    new_sum = start_sum * factor + jnp.sum(exponent, axis=-1)
    gained = jnp.einsum(
        "rshij,rsjhe->rsihe",
        exponent.astype(jnp.bfloat16),
        value5,
        preferred_element_type=jnp.float32,
    )
    new_acc = start_acc * jnp.swapaxes(factor, 2, 3)[..., None] + gained
    log_sum = new_max + jnp.log(new_sum)
    mixed_f = new_acc / jnp.swapaxes(new_sum, 2, 3)[..., None]
    mixed = mixed_f.reshape(rows_dev, seg_count, width, half_width).astype(jnp.bfloat16)
    attn_lin = halves(
        jnp.einsum("rsie,ed->rsid", mixed, out_full, preferred_element_type=jnp.float32)
    )
    hidden = states_f + attn_lin + bias_o.astype(jnp.float32)
    ffn_full = (
        lax.all_gather(w_up, ("rows", "seq"), axis=0, tiled=True),
        lax.all_gather(w_down, ("rows", "seq"), axis=1, tiled=True),
        lax.all_gather(bias_up, ("rows", "seq"), axis=1, tiled=True),
        lax.all_gather(gain_two, ("rows", "seq"), axis=0, tiled=True),
        lax.all_gather(shift_two, ("rows", "seq"), axis=0, tiled=True),
        lax.all_gather(bias_down, ("rows", "seq"), axis=0, tiled=True),
    )
    up_full, down_full, bias_u, gain_b, shift_b, bias_d = ffn_full
    normed_two_f, norm_two_back = jax.vjp(
        layer_norm, hidden, gain_b.astype(jnp.float32), shift_b.astype(jnp.float32)
    )
    normed_two = normed_two_f.astype(jnp.bfloat16)
    up_proj = jnp.einsum(
        "rsid,df->rsif", normed_two, up_full, preferred_element_type=jnp.float32
    ) + bias_u.astype(jnp.float32).reshape(-1)
    activated_f, gelu_back = jax.vjp(gelu_exact, up_proj)
    activated = activated_f.astype(jnp.bfloat16)
    down_proj = halves(
        jnp.einsum("rsif,fd->rsid", activated, down_full, preferred_element_type=jnp.float32)
    )
    out_states = (hidden + down_proj + bias_d.astype(jnp.float32)).astype(jnp.bfloat16)
    up_back, down_back = (
        lax.all_gather(w_up, ("rows", "seq"), axis=0, tiled=True),
        lax.all_gather(w_down, ("rows", "seq"), axis=1, tiled=True),
    )
    qkv_back, out_back = (
        lax.all_gather(w_qkv, ("rows", "seq"), axis=1, tiled=True),
        lax.all_gather(w_out, ("rows", "seq"), axis=1, tiled=True),
    )
    grad_out = cotangent.astype(jnp.float32)
    grad_bias_down = jnp.sum(grad_out, axis=(0, 1, 2))
    grad_w_down = jnp.einsum(
        "rsif,rsid->fd", activated, cotangent, preferred_element_type=jnp.float32
    )
    d_act = jnp.einsum("rsid,fd->rsif", cotangent, down_back, preferred_element_type=jnp.float32)
    (d_up,) = gelu_back(d_act)
    d_up_low = d_up.astype(jnp.bfloat16)
    grad_bias_up = jnp.sum(d_up_low, axis=(0, 1, 2), dtype=jnp.float32).reshape(bias_u.shape)
    grad_w_up = jnp.einsum(
        "rsid,rsif->df", normed_two, d_up_low, preferred_element_type=jnp.float32
    )
    d_norm_two = halves(
        jnp.einsum("rsif,df->rsid", d_up_low, up_back, preferred_element_type=jnp.float32)
    )
    d_hidden_ln, grad_gain_two, grad_shift_two = norm_two_back(d_norm_two)
    d_hidden = grad_out + d_hidden_ln
    ffn_grads = (
        lax.psum_scatter(grad_w_up, ("rows", "seq"), scatter_dimension=0, tiled=True),
        lax.psum_scatter(grad_w_down, ("rows", "seq"), scatter_dimension=1, tiled=True),
        lax.psum_scatter(grad_bias_up, ("rows", "seq"), scatter_dimension=1, tiled=True),
        lax.psum_scatter(grad_gain_two, ("rows", "seq"), scatter_dimension=0, tiled=True),
        lax.psum_scatter(grad_shift_two, ("rows", "seq"), scatter_dimension=0, tiled=True),
        lax.psum_scatter(grad_bias_down, ("rows", "seq"), scatter_dimension=0, tiled=True),
    )
    grad_bias_out = jnp.sum(d_hidden, axis=(0, 1, 2))
    d_hidden_low = d_hidden.astype(jnp.bfloat16)
    grad_w_out = jnp.einsum(
        "rsie,rsid->ed", mixed, d_hidden_low, preferred_element_type=jnp.float32
    )
    d_mixed = jnp.einsum(
        "rsid,ed->rsie", d_hidden_low, out_back, preferred_element_type=jnp.float32
    ).astype(jnp.bfloat16)
    d_mixed5 = d_mixed.reshape(rows_dev, seg_count, width, heads_loc, HEAD)
    keys_all, values_all = (
        lax.all_gather(keys, "seq", axis=2, tiled=True),
        lax.all_gather(values, "seq", axis=2, tiled=True),
    )
    key_lead = lead(keys_all.reshape(rows_dev, seg_count, seg_len, heads_loc, HEAD))
    value_lead = lead(values_all.reshape(rows_dev, seg_count, seg_len, heads_loc, HEAD))
    query_lead = lead(query5)
    grad_lead = lead(d_mixed5)
    key_positions = jnp.arange(seg_len, dtype=jnp.int32)

    def segment_back(seg_items):
        q_seg, do_seg, lse_seg, qdoc_seg, k_seg, v_seg, kdoc_seg, sk_seg, sv_seg, sdoc_seg = (
            seg_items
        )
        causal = (key_positions[None, :] <= query_pos[:, None])[None, None]
        allowed = causal & (qdoc_seg[:, :, None] == kdoc_seg[:, None, :])[:, None]
        scores = jnp.einsum("rihe,rjhe->rhij", q_seg, k_seg, preferred_element_type=jnp.float32)
        attn_probs = jnp.where(allowed, jnp.exp(scores - lse_seg[..., None]), 0.0)
        d_probs = jnp.einsum("rihe,rjhe->rhij", do_seg, v_seg, preferred_element_type=jnp.float32)
        summ_allowed = (qdoc_seg[:, :, None] == sdoc_seg[:, None, :])[:, None]
        summ_scores = jnp.einsum(
            "rihe,rjhe->rhij", q_seg, sk_seg, preferred_element_type=jnp.float32
        )
        summ_probs = jnp.where(summ_allowed, jnp.exp(summ_scores - lse_seg[..., None]), 0.0)
        summ_dprobs = jnp.einsum(
            "rihe,rjhe->rhij", do_seg, sv_seg, preferred_element_type=jnp.float32
        )
        delta = jnp.sum(attn_probs * d_probs, axis=-1) + jnp.sum(summ_probs * summ_dprobs, axis=-1)
        d_scores = (attn_probs * (d_probs - delta[..., None])).astype(jnp.bfloat16)
        d_summ = (summ_probs * (summ_dprobs - delta[..., None])).astype(jnp.bfloat16)
        d_query = jnp.einsum("rhij,rjhe->rihe", d_scores, k_seg, preferred_element_type=jnp.float32)
        d_query = d_query + jnp.einsum(
            "rhij,rjhe->rihe", d_summ, sk_seg, preferred_element_type=jnp.float32
        )
        d_sum_keys = jnp.einsum(
            "rhij,rihe->rjhe", d_summ, q_seg, preferred_element_type=jnp.float32
        )
        d_sum_values = jnp.einsum(
            "rhij,rihe->rjhe",
            summ_probs.astype(jnp.bfloat16),
            do_seg,
            preferred_element_type=jnp.float32,
        )
        return (d_query, d_scores, attn_probs.astype(jnp.bfloat16), d_sum_keys, d_sum_values, delta)

    seg_inputs = (
        query_lead,
        grad_lead,
        lead(log_sum),
        lead(query_docs),
        key_lead,
        value_lead,
        lead(doc_ids),
        lead(sum_k5),
        lead(sum_v5),
        lead(sum_docs),
    )
    d_query_lead, d_scores_all, probs_all, d_sk_lead, d_sv_lead, delta_lead = lax.map(
        segment_back, seg_inputs
    )
    d_key_part = jnp.einsum(
        "srhij,srihe->jrshe", d_scores_all, query_lead, preferred_element_type=jnp.float32
    )
    d_value_part = jnp.einsum(
        "srhij,srihe->jrshe", probs_all, grad_lead, preferred_element_type=jnp.float32
    )
    key_grads = lax.psum_scatter(
        jnp.stack((d_key_part, d_value_part), axis=3)
        .reshape(width * lax.axis_size("seq"), rows_dev, seg_count, 2, half_width)
        .astype(jnp.bfloat16),
        "seq",
        scatter_dimension=0,
        tiled=True,
    ).astype(jnp.float32)
    key_grads = jnp.transpose(key_grads, (3, 1, 2, 0, 4))
    d_sk = jnp.moveaxis(d_sk_lead, 0, 1).reshape(rows_dev, seg_count, 2 * SUMM, half_width)
    d_sv = jnp.moveaxis(d_sv_lead, 0, 1).reshape(rows_dev, seg_count, 2 * SUMM, half_width)
    src_keys = later(d_sk[:, :, :SUMM], 1) + later(d_sk[:, :, SUMM:], 2)
    src_values = later(d_sv[:, :, :SUMM], 1) + later(d_sv[:, :, SUMM:], 2)
    summ_grads = lax.psum(jnp.stack((src_keys, src_values)).astype(jnp.bfloat16), "seq").astype(
        jnp.float32
    )
    owner_grads = jnp.where(seq_place == seq_count - 1, summ_grads, 0.0)
    owner_grads = jnp.pad(owner_grads, ((0, 0), (0, 0), (0, 0), (width - SUMM, 0), (0, 0)))
    key_grads = key_grads + owner_grads
    d_keys_low = key_grads[0].astype(jnp.bfloat16)
    d_values_low = key_grads[1].astype(jnp.bfloat16)
    d_query = jnp.moveaxis(d_query_lead, 0, 1).reshape(rows_dev, seg_count, width, half_width)
    d_query_low = d_query.astype(jnp.bfloat16)
    d_pre = (d_query_low.astype(jnp.float32) * score_scale).astype(jnp.bfloat16)
    grad_bias_qv = jnp.stack(
        (
            jnp.sum(d_pre, axis=(0, 1, 2), dtype=jnp.float32),
            jnp.sum(d_values_low, axis=(0, 1, 2), dtype=jnp.float32),
        )
    ).reshape(bqv_full.shape)
    d_qkv = jnp.stack((d_pre, d_keys_low, d_values_low))
    grad_w_qkv = jnp.einsum(
        "rsid,krsie->kde", normed_one, d_qkv, preferred_element_type=jnp.float32
    )
    d_norm_one = halves(
        jnp.einsum("krsie,kde->rsid", d_qkv, qkv_back, preferred_element_type=jnp.float32)
    )
    d_states_ln, grad_gain_one, grad_shift_one = norm_one_back(d_norm_one)
    grad_states = (d_hidden + d_states_ln).astype(jnp.bfloat16)
    attn_grads = (
        lax.psum_scatter(grad_w_qkv, ("rows", "seq"), scatter_dimension=1, tiled=True),
        lax.psum_scatter(grad_w_out, ("rows", "seq"), scatter_dimension=1, tiled=True),
        lax.psum_scatter(grad_bias_qv, ("rows", "seq"), scatter_dimension=2, tiled=True),
        lax.psum_scatter(grad_gain_one, ("rows", "seq"), scatter_dimension=0, tiled=True),
        lax.psum_scatter(grad_shift_one, ("rows", "seq"), scatter_dimension=0, tiled=True),
        lax.psum_scatter(grad_bias_out, ("rows", "seq"), scatter_dimension=0, tiled=True),
    )
    return (
        out_states,
        grad_states,
        attn_grads[0],
        attn_grads[1],
        ffn_grads[0],
        ffn_grads[1],
        attn_grads[2],
        attn_grads[5],
        ffn_grads[2],
        ffn_grads[5],
        attn_grads[3],
        attn_grads[4],
        ffn_grads[3],
        ffn_grads[4],
    )


def opening_kernel(w_ref, s_ref, v_ref, whole_ref, tokens_ref, vectors_ref, z_send, z_recv, x_send, x_recv, y_send, y_recv,
                   fx_send, fx_recv, fy_send, fy_recv, t_send, t_recv, c_send, c_recv, v_send, v_recv, own):
    rows, place, core = lax.axis_index("rows"), lax.axis_index("seq"), lax.axis_index("fsdp")
    count = s_ref.shape[0]
    depth = w_ref.shape[1]
    half = w_ref.shape[2] // 2
    width = s_ref.shape[2] // 2
    steps = count - 1

    def at(row, seq, fsdp=None):
        return (row, seq, core if fsdp is None else fsdp)

    def hail(device):
        pl.semaphore_signal(barrier, inc=1, device_id=device, device_id_type=pl.DeviceIdType.MESH)

    barrier = pltpu.get_barrier_semaphore()
    for away in range(4):
        for along in range(count):
            if away or along:
                hail(at(rows ^ away, lax.rem(place + along, count)))
    hail(at(rows, place, 1 - core))
    pl.semaphore_wait(barrier, 4 * count)

    def shard(ref, row, seq, cut=None):
        first = pl.multiple_of((row * count + seq) * depth, depth)
        if cut is None:
            return ref.at[:, pl.ds(first, depth)]
        return ref.at[:, pl.ds(first, depth), pl.ds(cut * half, half)]

    def remote(src, dst, send, recv, device):
        return pltpu.make_async_remote_copy(
            src_ref=src, dst_ref=dst, send_sem=send, recv_sem=recv, device_id=device,
            device_id_type=pl.DeviceIdType.MESH,
        )

    x_peer, y_peer = rows ^ 1, rows ^ 2

    def spread(t, side, seq, src):
        mine = shard(whole_ref, rows, seq)
        src = mine if src is None else src
        return (
            remote(src, mine, x_send.at[t, side], x_recv.at[t, side], at(x_peer, place)),
            remote(src, mine, y_send.at[t, side], y_recv.at[t, side], at(y_peer, place)),
        )

    def arrived(t, side, seq):
        from_x, from_y = shard(whole_ref, x_peer, seq), shard(whole_ref, y_peer, seq)
        return (
            remote(from_x, from_x, x_send.at[t, side], x_recv.at[t, side], at(x_peer, place)),
            remote(from_y, from_y, y_send.at[t, side], y_recv.at[t, side], at(y_peer, place)),
        )

    def onward(t, side, seq):
        a, b = shard(whole_ref, x_peer, seq, 0), shard(whole_ref, y_peer, seq, 1)
        return (
            remote(a, a, fy_send.at[t, side], fy_recv.at[t, side], at(y_peer, place)),
            remote(b, b, fx_send.at[t, side], fx_recv.at[t, side], at(x_peer, place)),
        )

    def far(t, side, seq):
        a, b = shard(whole_ref, rows ^ 3, seq, 0), shard(whole_ref, rows ^ 3, seq, 1)
        return (
            remote(a, a, fy_send.at[t, side], fy_recv.at[t, side], at(y_peer, place)),
            remote(b, b, fx_send.at[t, side], fx_recv.at[t, side], at(x_peer, place)),
        )

    def along_z(t, side, seq, src):
        mine = shard(whole_ref, rows, seq)
        to = place + 1 if side == 0 else place - 1
        return remote(mine if src is None else src, mine, z_send.at[t, side], z_recv.at[t, side], at(rows, to))

    def origin(t, side):
        return place - t if side == 0 else place + t

    def has(t, side):
        return origin(t, side) >= 0 if side == 0 else origin(t, side) < count

    def has_next(side):
        return place + 1 < count if side == 0 else place >= 1

    for side in range(2):
        @pl.when(has_next(side))
        def _(side=side):
            along_z(1, side, place, w_ref).start()
    for copy in spread(0, 0, place, w_ref):
        copy.start()
    local = pltpu.make_async_copy(w_ref, shard(whole_ref, rows, place), own.at[0])
    local.start()
    vectors = []
    for away in range(4):
        for along in range(count):
            if away or along:
                mine = rows * count + place
                copy = remote(
                    v_ref, vectors_ref.at[mine], v_send.at[away, along], v_recv.at[away, along],
                    at(rows ^ away, lax.rem(place + along, count)),
                )
                copy.start()
                vectors.append(copy)
    local_v = pltpu.make_async_copy(v_ref, vectors_ref.at[rows * count + place], own.at[1])
    local_v.start()

    columns = pl.ds(pl.multiple_of(core * width, width), width)

    def token_copy(along):
        to = lax.rem(place + along, count)
        return remote(
            s_ref.at[to, :, columns], tokens_ref.at[place, :, columns], t_send.at[along], t_recv.at[along], at(rows, to)
        )

    def token_got(along):
        start = lax.rem(place + count - along, count)
        view = tokens_ref.at[start, :, columns]
        return remote(view, view, t_send.at[along], t_recv.at[along], at(rows, start))

    def token_on(along):
        view = tokens_ref.at[lax.rem(place + count - along, count), :, columns]
        return remote(view, view, c_send.at[along], c_recv.at[along], at(rows, place, 1 - core))

    def token_far(along):
        start = lax.rem(place + count - along, count)
        view = tokens_ref.at[start, :, pl.ds(pl.multiple_of((1 - core) * width, width), width)]
        return remote(view, view, c_send.at[along], c_recv.at[along], at(rows, place, 1 - core))

    local_t = pltpu.make_async_copy(s_ref.at[place], tokens_ref.at[place], own.at[2])
    local_t.start()

    def pass_on(t, side, seq):
        for got in arrived(t, side, seq):
            got.wait_recv()
        for copy in onward(t, side, seq):
            copy.start()

    for t in range(1, steps + 1):
        for side in range(2):
            @pl.when(has(t, side))
            def _(t=t, side=side):
                seq = origin(t, side)
                along_z(t, side, seq, None).wait_recv()
                if t < steps:
                    @pl.when(has_next(side))
                    def _():
                        along_z(t + 1, side, seq, None).start()
                for copy in spread(t, side, seq, None):
                    copy.start()
        if t == 1:
            for along in range(1, count):
                token_copy(along).start()
            pass_on(0, 0, place)
        else:
            for side in range(2):
                @pl.when(has(t - 1, side))
                def _(t=t, side=side):
                    pass_on(t - 1, side, origin(t - 1, side))
    for side in range(2):
        @pl.when(has(steps, side))
        def _(side=side):
            pass_on(steps, side, origin(steps, side))

    for along in range(1, count):
        token_got(along).wait_recv()
        token_on(along).start()

    def settle(t, side, seq, src):
        for copy in spread(t, side, seq, src):
            copy.wait_send()
        for copy in onward(t, side, seq):
            copy.wait_send()
        for got in far(t, side, seq):
            got.wait_recv()

    settle(0, 0, place, w_ref)
    for t in range(1, steps + 1):
        for side in range(2):
            @pl.when(has(t, side))
            def _(t=t, side=side):
                settle(t, side, origin(t, side), None)

            @pl.when(has(t - 1, side) & has_next(side))
            def _(t=t, side=side):
                along_z(t, side, origin(t - 1, side), w_ref if t == 1 else None).wait_send()
    for copy in vectors:
        copy.wait_send()
    for away in range(4):
        for along in range(count):
            if away or along:
                start = (rows ^ away) * count + lax.rem(place + count - along, count)
                view = vectors_ref.at[start]
                remote(
                    view, view, v_send.at[away, along], v_recv.at[away, along],
                    at(rows ^ away, lax.rem(place + count - along, count)),
                ).wait_recv()
    for along in range(1, count):
        token_copy(along).wait_send()
        token_on(along).wait_send()
        token_far(along).wait_recv()
    local.wait()
    local_v.wait()
    local_t.wait()


def opening(w, tokens, vector):
    count = tokens.shape[0]
    kinds, depth, half = w.shape
    dma = pltpu.SemaphoreType.DMA
    pair = [dma((count, 2)), dma((count, 2))]
    anywhere = pl.BlockSpec(memory_space=pl.ANY)
    return pl.pallas_call(
        opening_kernel,
        in_specs=[anywhere] * 3,
        out_specs=[anywhere] * 3,
        out_shape=[
            jax.ShapeDtypeStruct((kinds, depth * 4 * count, half), w.dtype),
            jax.ShapeDtypeStruct(tokens.shape, tokens.dtype),
            jax.ShapeDtypeStruct((4 * count,) + vector.shape, vector.dtype),
        ],
        scratch_shapes=pair * 5 + [dma((count,))] * 4 + [dma((4, count))] * 2 + [dma((3,))],
        compiler_params=pltpu.CompilerParams(collective_id=0, has_side_effects=True),
    )(w, tokens, vector)


def closing_kernel(s_ref, v_ref, tokens_ref, sum_ref, held, t_send, t_recv, c_send, c_recv, v_send, v_recv, own):
    rows, place, core = lax.axis_index("rows"), lax.axis_index("seq"), lax.axis_index("fsdp")
    count = s_ref.shape[0]
    width = s_ref.shape[2] // 2

    def at(row, seq, fsdp=None):
        return (row, seq, core if fsdp is None else fsdp)

    def hail(device):
        pl.semaphore_signal(barrier, inc=1, device_id=device, device_id_type=pl.DeviceIdType.MESH)

    barrier = pltpu.get_barrier_semaphore()
    for away in range(4):
        for along in range(count):
            if away or along:
                hail(at(rows ^ away, lax.rem(place + along, count)))
    hail(at(rows, place, 1 - core))
    pl.semaphore_wait(barrier, 4 * count)

    def remote(src, dst, send, recv, device):
        return pltpu.make_async_remote_copy(
            src_ref=src, dst_ref=dst, send_sem=send, recv_sem=recv, device_id=device,
            device_id_type=pl.DeviceIdType.MESH,
        )

    columns = pl.ds(pl.multiple_of(core * width, width), width)
    others = pl.ds(pl.multiple_of((1 - core) * width, width), width)

    def token_copy(along):
        to = lax.rem(place + along, count)
        return remote(
            s_ref.at[to, :, columns], tokens_ref.at[place, :, columns], t_send.at[along], t_recv.at[along], at(rows, to)
        )

    def token_got(along):
        start = lax.rem(place + count - along, count)
        view = tokens_ref.at[start, :, columns]
        return remote(view, view, t_send.at[along], t_recv.at[along], at(rows, start))

    def token_on(along):
        view = tokens_ref.at[lax.rem(place + count - along, count), :, columns]
        return remote(view, view, c_send.at[along], c_recv.at[along], at(rows, place, 1 - core))

    def token_far(along):
        view = tokens_ref.at[lax.rem(place + count - along, count), :, others]
        return remote(view, view, c_send.at[along], c_recv.at[along], at(rows, place, 1 - core))

    for along in range(1, count):
        token_copy(along).start()
    local_t = pltpu.make_async_copy(s_ref.at[place], tokens_ref.at[place], own.at[0])
    local_t.start()
    mine = rows * count + place
    vectors = []
    for away in range(4):
        for along in range(count):
            if away or along:
                to_row, to_seq = rows ^ away, lax.rem(place + along, count)
                copy = remote(
                    v_ref.at[to_row * count + to_seq], held.at[away * count + along],
                    v_send.at[away, along], v_recv.at[away, along], at(to_row, to_seq),
                )
                copy.start()
                vectors.append(copy)
    local_v = pltpu.make_async_copy(v_ref.at[mine], held.at[0], own.at[1])
    local_v.start()
    local_v.wait()
    for copy in vectors:
        copy.wait_recv()
    sum_ref[...] = jnp.sum(held[...], axis=0)
    for along in range(1, count):
        token_got(along).wait_recv()
        token_on(along).start()
    for copy in vectors:
        copy.wait_send()
    for along in range(1, count):
        token_copy(along).wait_send()
        token_on(along).wait_send()
        token_far(along).wait_recv()
    local_t.wait()


def closing(tokens, vectors):
    count = tokens.shape[0]
    dma = pltpu.SemaphoreType.DMA
    anywhere = pl.BlockSpec(memory_space=pl.ANY)
    return pl.pallas_call(
        closing_kernel,
        in_specs=[anywhere] * 2,
        out_specs=[anywhere, pl.BlockSpec(memory_space=pltpu.VMEM)],
        out_shape=[
            jax.ShapeDtypeStruct(tokens.shape, tokens.dtype),
            jax.ShapeDtypeStruct(vectors.shape[1:], F32),
        ],
        scratch_shapes=[pltpu.VMEM(vectors.shape, F32)]
        + [dma((count,))] * 4
        + [dma((4, count))] * 2
        + [dma((2,))],
        compiler_params=pltpu.CompilerParams(collective_id=1, has_side_effects=True),
    )(tokens, vectors)


def norm_back_kernel(field_ref, own_ref, other_ref, rest_ref, gain_ref, *outs):
    field = field_ref[...].astype(F32)
    width = field.shape[1]
    grad = own_ref[...].astype(F32) + other_ref[...].astype(F32)
    centered = field - jnp.sum(field, axis=1, keepdims=True) * (1.0 / width)
    variance = jnp.sum(centered * centered, axis=1, keepdims=True) * (1.0 / width)
    scale = lax.rsqrt(variance + norm_eps)
    unit = centered * scale
    scaled = grad * gain_ref[...]
    mean_one = jnp.sum(scaled, axis=1, keepdims=True) * (1.0 / width)
    mean_two = jnp.sum(scaled * unit, axis=1, keepdims=True) * (1.0 / width)
    total = rest_ref[...].astype(F32) + scale * (scaled - mean_one - unit * mean_two)
    sums_ref = outs[-1]
    for ref in outs[:-1]:
        ref[...] = total.astype(ref.dtype)

    @pl.when(pl.program_id(0) == 0)
    def _():
        sums_ref[...] = jnp.zeros_like(sums_ref)

    for n, item in enumerate((grad * unit, grad, total)):
        sums_ref[pl.ds(n, 1)] += jnp.sum(item, axis=0, keepdims=True)


def norm_back(field, own, other, rest, gain, kinds):
    tokens, width = field.shape
    rows = min(256, tokens)
    block = pl.BlockSpec((rows, width), lambda i: (i, 0))
    flat = lambda n: pl.BlockSpec((n, width), lambda i: (0, 0))
    return pl.pallas_call(
        norm_back_kernel,
        grid=(tokens // rows,),
        in_specs=[block] * 4 + [flat(1)],
        out_specs=[block] * len(kinds) + [flat(8)],
        out_shape=[jax.ShapeDtypeStruct(field.shape, kind) for kind in kinds]
        + [jax.ShapeDtypeStruct((8, width), F32)],
        cost_estimate=told(15.0),
        compiler_params=pltpu.CompilerParams(vmem_limit_bytes=48 * 2**20),
    )(field, own, other, rest, gain.reshape(1, width))


class Move:
    def __init__(self, alongs, src_ref, out_ref, sems):
        self.alongs, self.src, self.out = alongs, src_ref, out_ref
        self.t_send, self.t_recv, self.c_send, self.c_recv = sems
        self.rows, self.place, self.core = [lax.axis_index(name) for name in ("rows", "seq", "fsdp")]
        self.count = src_ref.shape[0]
        self.width = src_ref.shape[2] // 2

    def columns(self, core):
        return pl.ds(pl.multiple_of(core * self.width, self.width), self.width)

    def remote(self, src, dst, send, recv, seq, core):
        return pltpu.make_async_remote_copy(
            src_ref=src, dst_ref=dst, send_sem=send, recv_sem=recv, device_id=(self.rows, seq, core),
            device_id_type=pl.DeviceIdType.MESH,
        )

    def origin(self, along):
        return lax.rem(self.place + self.count - along, self.count)

    def sent(self, n, along):
        to = lax.rem(self.place + along, self.count)
        src, dst = self.src.at[to, :, self.columns(self.core)], self.out.at[self.place, :, self.columns(self.core)]
        return self.remote(src, dst, self.t_send.at[n], self.t_recv.at[n], to, self.core)

    def got(self, n, along):
        start = self.origin(along)
        view = self.out.at[start, :, self.columns(self.core)]
        return self.remote(view, view, self.t_send.at[n], self.t_recv.at[n], start, self.core)

    def passed(self, n, along, mine):
        view = self.out.at[self.origin(along), :, self.columns(self.core if mine else 1 - self.core)]
        return self.remote(view, view, self.c_send.at[n], self.c_recv.at[n], self.place, 1 - self.core)

    def begin(self):
        barrier = pltpu.get_barrier_semaphore()
        peers = sorted(set(self.alongs) | {self.count - along for along in self.alongs})
        for along in peers:
            device = (self.rows, lax.rem(self.place + along, self.count), self.core)
            pl.semaphore_signal(barrier, inc=1, device_id=device, device_id_type=pl.DeviceIdType.MESH)
        device = (self.rows, self.place, 1 - self.core)
        pl.semaphore_signal(barrier, inc=1, device_id=device, device_id_type=pl.DeviceIdType.MESH)
        pl.semaphore_wait(barrier, len(peers) + 1)
        for n, along in enumerate(self.alongs):
            self.sent(n, along).start()

    def end(self):
        for n, along in enumerate(self.alongs):
            self.got(n, along).wait_recv()
            self.passed(n, along, True).start()
        for n, along in enumerate(self.alongs):
            self.sent(n, along).wait_send()
            self.passed(n, along, True).wait_send()
            self.passed(n, along, False).wait_recv()


def product_kernel(mode, finish, n_extra, n_in, move, *refs):
    if move is None:
        return product_step(mode, finish, n_extra, refs[: 2 + n_extra], refs[n_in:-1], refs[-1])
    moving = Move(move, refs[2 + n_extra], refs[n_in + 1], refs[-4:])
    ids = [pl.program_id(n) for n in range(3)]
    ends = [pl.num_programs(n) - 1 for n in range(3)]

    @pl.when((ids[0] == 0) & (ids[1] == 0) & (ids[2] == 0))
    def _():
        moving.begin()

    product_step(mode, finish, n_extra, refs[: 2 + n_extra], refs[n_in : n_in + 1], refs[n_in + 2])

    @pl.when((ids[0] == ends[0]) & (ids[1] == ends[1]) & (ids[2] == ends[2]))
    def _():
        moving.end()


def product_step(mode, finish, n_extra, refs, outs, total):
    a_ref, b_ref = refs[:2]
    extra = refs[2:]
    k = pl.program_id(2)
    last = pl.num_programs(2) - 1
    dims = {"nn": ((1,), (0,)), "nt": ((1,), (1,)), "tn": ((0,), (0,))}[mode]
    part = lax.dot_general(a_ref[...], b_ref[...], (dims, ((), ())), preferred_element_type=F32)
    if last == 0:
        finish(part, extra, outs)
        return

    @pl.when(k == 0)
    def _():
        total[...] = part

    @pl.when((k > 0) & (k < last))
    def _():
        total[...] += part

    @pl.when(k == last)
    def _():
        finish(total[...] + part, extra, outs)


def finish_cast(total, extra, outs):
    outs[0][...] = total.astype(outs[0].dtype)


def finish_bias(scale, total, extra, outs):
    outs[0][...] = ((total + extra[0][...]) * scale).astype(BF)


def product(a, b, mode, finish=finish_cast, rows=(), deps=(), planes=(0,), blocks=(1024, 1024, 2048), move=None):
    plane = len(b.shape) == 3
    b_shape = b.shape[-2:]
    m, depth = a.shape if mode != "tn" else a.shape[::-1]
    n = b_shape[0] if mode == "nt" else b_shape[1]
    bm, bn, bk = min(blocks[0], m), min(blocks[1], n), min(blocks[2], depth)
    spec = pl.BlockSpec
    a_spec = (
        spec((bk, bm), lambda j, i, k: (k, i)) if mode == "tn" else spec((bm, bk), lambda j, i, k: (i, k))
    )
    first, turns = planes[0], len(planes)
    if plane and mode == "nt":
        b_spec = spec((None, bn, bk), lambda j, i, k: (first + k % turns, j, k // turns))
    elif plane:
        b_spec = spec((None, bk, bn), lambda j, i, k: (first, k, j))
    elif mode == "nt":
        b_spec = spec((bn, bk), lambda j, i, k: (j, k))
    else:
        b_spec = spec((bk, bn), lambda j, i, k: (k, j))
    row = spec((1, bn), lambda j, i, k: (0, j))
    field = spec((bm, bn), lambda j, i, k: (i, j))
    out_specs, out_shape = field, jax.ShapeDtypeStruct((m, n), BF)
    scratch, aliases, inputs = [pltpu.VMEM((bm, bn), F32)], {}, (a, b, *rows)
    params = dict(vmem_limit_bytes=48 * 2**20)
    if move is not None:
        src, target, alongs, ident = move
        out_specs, out_shape = (
            [field, spec(memory_space=pl.ANY)],
            [out_shape, jax.ShapeDtypeStruct(src.shape, src.dtype)],
        )
        dma = pltpu.SemaphoreType.DMA
        scratch += [dma((len(alongs),))] * 4
        aliases = {len(inputs) + 1: 1}
        inputs += (src, target)
        params.update(collective_id=ident, has_side_effects=True)
        move = alongs
    n_in = len(inputs) + len(deps)
    return pl.pallas_call(
        functools.partial(product_kernel, mode, finish, len(rows), n_in, move),
        grid=(n // bn, m // bm, depth // bk),
        in_specs=[a_spec, b_spec]
        + [row] * len(rows)
        + [spec(memory_space=pl.ANY)] * (n_in - 2 - len(rows)),
        out_specs=out_specs,
        out_shape=out_shape,
        scratch_shapes=scratch,
        input_output_aliases=aliases,
        cost_estimate=told(2.0 * m * n * depth / 8e8),
        compiler_params=pltpu.CompilerParams(**params),
    )(*inputs, *deps)


def dot_nt(a,b): return lax.dot_general(a,b,(((1,),(1,)),((),())),preferred_element_type=F32)
def dot_nn(a,b): return lax.dot_general(a,b,(((1,),(0,)),((),())),preferred_element_type=F32)

def fwd_kernel(tile, flags, q_ref, k_ref, v_ref, sk_ref, sv_ref, start_ref, doc_ref, sdoc_ref, *rest):
    o_ref, lse_ref, km, vt, acc, top, total = rest[-7:]
    i = pl.program_id(1)
    seg = k_ref.shape[0]
    lanes = lax.broadcasted_iota(jnp.int32, (1, 128), 1)
    masks = [(lanes < HEAD).astype(BF), (lanes >= HEAD).astype(BF)]
    @pl.when(i == 0)
    def _():
        for h in range(2):
            km[h, pl.ds(0, seg)] = k_ref[...] * masks[h]
            km[h, pl.ds(seg, 128)] = sk_ref[...] * masks[h]
        vt[:, pl.ds(0, seg)] = v_ref[...].T
        vt[:, pl.ds(seg, 128)] = sv_ref[...].T
    q = q_ref[...]
    allowed = sdoc_ref[...] == doc_ref[...]
    for h in range(2):
        s = dot_nt(km[h, pl.ds(seg, 128)], q)
        s = jnp.where(allowed, s, neg_big)
        m = jnp.max(s, axis=0, keepdims=True)
        p = jnp.where(allowed, jnp.exp(s - m), 0.0)
        top[h] = m
        total[h] = jnp.sum(p, axis=0, keepdims=True)
        acc[h] = dot_nn(vt[pl.ds(h * HEAD, HEAD), pl.ds(seg, 128)], p.astype(BF))
    def step(j, masked):
        at = pl.multiple_of(j * tile, tile)
        if masked:
            places = at + lax.broadcasted_iota(jnp.int32, (tile, tile), 0)
            mine = i * tile + lax.broadcasted_iota(jnp.int32, (tile, tile), 1)
            okay = (places <= mine) & (places >= start_ref[...])
        ss=[]
        for h in range(2):
            s = dot_nt(km[h, pl.ds(at, tile)], q)
            if masked:
                s = jnp.where(okay, s, neg_big)
            ss.append(s)
        for h in range(2):
            s = ss[h]
            m_old = top[h]
            m = jnp.maximum(m_old, jnp.max(s, axis=0, keepdims=True))
            p = jnp.exp(s - m)
            if masked:
                p = jnp.where(okay, p, 0.0)
            alpha = jnp.exp(m_old - m)
            top[h] = m
            total[h] = total[h] * alpha + jnp.sum(p, axis=0, keepdims=True)
            acc[h] = acc[h] * alpha + dot_nn(vt[pl.ds(h * HEAD, HEAD), pl.ds(at, tile)], p.astype(BF))
    count = pl.num_programs(1)
    def loop(j, _):
        flag = flags[i * count + j]
        @pl.when(flag == 2)
        def _(): step(j, False)
        @pl.when(flag == 1)
        def _(): step(j, True)
        return 0
    lax.fori_loop(0, i + 1, loop, 0)
    out = [acc[h] / total[h] for h in range(2)]
    o_ref[...] = jnp.concatenate(out, axis=0).T.astype(BF)
    for h in range(2):
        lse_ref[0, pl.ds(h, 1)] = top[h] + jnp.log(total[h])

def attn_fwd(q, k, v, sk, sv, start, doc, sdoc, flags, tile, base, pairs, earlier_out=(), deps=()):
    seg, width = q.shape
    count = seg // tile
    spec = pl.BlockSpec
    extra = tuple(earlier_out) + tuple(deps)
    return pl.pallas_call(
        functools.partial(fwd_kernel, tile),
        grid_spec=pltpu.PrefetchScalarGridSpec(
            num_scalar_prefetch=1,
            grid=(pairs, count),
            in_specs=[
                spec((tile, 128), lambda h, i, f: (i, h + base)),
                spec((seg, 128), lambda h, i, f: (0, h + base)),
                spec((seg, 128), lambda h, i, f: (0, h + base)),
                spec((128, 128), lambda h, i, f: (0, h + base)),
                spec((128, 128), lambda h, i, f: (0, h + base)),
                spec((1, tile), lambda h, i, f: (0, i)),
                spec((1, tile), lambda h, i, f: (0, i)),
                spec((128, 1), lambda h, i, f: (0, 0)),
            ]
            + [spec(memory_space=pl.ANY)] * len(extra),
            out_specs=[
                spec((tile, 128), lambda h, i, f: (i, h + base)),
                spec((1, 2, tile), lambda h, i, f: (h + base, 0, i)),
            ],
            scratch_shapes=[
                pltpu.VMEM((2, seg + 128, 128), BF),
                pltpu.VMEM((128, seg + 128), BF),
                pltpu.VMEM((2, HEAD, tile), F32),
                pltpu.VMEM((2, 1, tile), F32),
                pltpu.VMEM((2, 1, tile), F32),
            ],
        ),
        out_shape=[
            jax.ShapeDtypeStruct((seg, width), BF),
            jax.ShapeDtypeStruct((width // 128, 2, seg), F32),
        ],
        input_output_aliases={9: 0, 10: 1} if earlier_out else {},
        cost_estimate=told(4.2 * pairs * 4),
        compiler_params=pltpu.CompilerParams(vmem_limit_bytes=40 * 2**20),
    )(flags, q, k, v, sk, sv, start, doc, sdoc, *extra)


def bwd_kernel(tile, flags, q_ref, k_ref, v_ref, do_ref, o_ref, sk_ref, sv_ref, lse_ref, start_ref, doc_ref, sdoc_ref, *rest):
    dq_ref, dk_ref, dv_ref, dsk_ref, dsv_ref, qm, dom, dqt, delta = rest[-9:]
    j = pl.program_id(1)
    seg = q_ref.shape[0]
    count = seg // tile
    lanes = lax.broadcasted_iota(jnp.int32, (1, 128), 1)
    masks = [(lanes < HEAD).astype(BF), (lanes >= HEAD).astype(BF)]
    @pl.when(j == 0)
    def _():
        dqt[...] = jnp.zeros_like(dqt)
        for h in range(2):
            qm[h] = q_ref[...] * masks[h]
            dom[h] = do_ref[...] * masks[h]
        def one(i, _):
            at = pl.multiple_of(i * tile, tile)
            prod = (do_ref[pl.ds(at, tile)].astype(F32) * o_ref[pl.ds(at, tile)].astype(F32)).T
            for h in range(2):
                delta[h, :, pl.ds(at, tile)] = jnp.sum(prod[h * HEAD:(h + 1) * HEAD], axis=0, keepdims=True)
            return 0
        lax.fori_loop(0, count, one, 0)
    def block(i, kt, k_blk, v_blk, okay):
        at = pl.multiple_of(i * tile, tile)
        gk = gv = None
        for h in range(2):
            qh = qm[h, pl.ds(at, tile)]
            dh = dom[h, pl.ds(at, tile)]
            s = dot_nt(k_blk, qh)
            dp = dot_nt(v_blk, dh)
            p = jnp.exp(s - lse_ref[0, pl.ds(h, 1), pl.ds(at, tile)])
            if okay is not None:
                p = jnp.where(okay, p, 0.0)
            ds = (p * (dp - delta[h, :, pl.ds(at, tile)])).astype(BF)
            a = dot_nn(p.astype(BF), dh)
            b = dot_nn(ds, qh)
            gv = a if gv is None else gv + a
            gk = b if gk is None else gk + b
            dqt[pl.ds(h * HEAD, HEAD), pl.ds(at, tile)] += dot_nn(kt[h * HEAD:(h + 1) * HEAD], ds)
        return gk, gv
    @pl.when(j < count)
    def _():
        at_k = pl.multiple_of(j * tile, tile)
        k_blk = k_ref[...]
        v_blk = v_ref[...]
        kt = k_blk.T
        def masked_of(i):
            places = at_k + lax.broadcasted_iota(jnp.int32, (tile, tile), 0)
            mine = i * tile + lax.broadcasted_iota(jnp.int32, (tile, tile), 1)
            return (places <= mine) & (places >= start_ref[:, pl.ds(pl.multiple_of(i * tile, tile), tile)])
        gk, gv = block(j, kt, k_blk, v_blk, masked_of(j))
        dkacc, dvacc = gk, gv
        def loop(i, carry):
            flag = flags[i * count + j]
            def full(c):
                gk, gv = block(i, kt, k_blk, v_blk, None)
                return c[0] + gk, c[1] + gv
            def part(c):
                gk, gv = block(i, kt, k_blk, v_blk, masked_of(i))
                return c[0] + gk, c[1] + gv
            return lax.switch(flag, [lambda c: c, part, full], carry)
        dkacc, dvacc = lax.fori_loop(j + 1, count, loop, (dkacc, dvacc))
        dk_ref[...] = dkacc.astype(BF)
        dv_ref[...] = dvacc.astype(BF)
    @pl.when(j == count)
    def _():
        kt = sk_ref[...].T
        def loop(i, carry):
            okay = sdoc_ref[...] == doc_ref[:, pl.ds(pl.multiple_of(i * tile, tile), tile)]
            gk, gv = block(i, kt, sk_ref[...], sv_ref[...], okay)
            return carry[0] + gk, carry[1] + gv
        z = jnp.zeros((128, 128), F32)
        a, b = lax.fori_loop(0, count, loop, (z, z))
        dsk_ref[...] = a.astype(BF)
        dsv_ref[...] = b.astype(BF)
        def fin(i, _):
            at = pl.multiple_of(i * tile, tile)
            dq_ref[pl.ds(at, tile)] = (dqt[:, pl.ds(at, tile)].T.astype(BF).astype(F32) * HEAD ** -0.5).astype(BF)
            return 0
        lax.fori_loop(0, count, fin, 0)

def attn_bwd(q, k, v, do, o, sk, sv, lse, start, doc, sdoc, flags, tile, base, pairs, deps=()):
    seg = q.shape[0]
    count = seg // tile
    last = count - 1
    spec = pl.BlockSpec
    return pl.pallas_call(
        functools.partial(bwd_kernel, tile),
        grid_spec=pltpu.PrefetchScalarGridSpec(
            num_scalar_prefetch=1,
            grid=(pairs, count + 1),
            in_specs=[
                spec((seg, 128), lambda h, j, f: (0, h + base)),
                spec((tile, 128), lambda h, j, f: (jnp.minimum(j, last), h + base)),
                spec((tile, 128), lambda h, j, f: (jnp.minimum(j, last), h + base)),
                spec((seg, 128), lambda h, j, f: (0, h + base)),
                spec((seg, 128), lambda h, j, f: (0, h + base)),
                spec((128, 128), lambda h, j, f: (0, h + base)),
                spec((128, 128), lambda h, j, f: (0, h + base)),
                spec((1, 2, seg), lambda h, j, f: (h + base, 0, 0)),
                spec((1, seg), lambda h, j, f: (0, 0)),
                spec((1, seg), lambda h, j, f: (0, 0)),
                spec((128, 1), lambda h, j, f: (0, 0)),
            ]
            + [spec(memory_space=pl.ANY)] * len(deps),
            out_specs=[
                spec((seg, 128), lambda h, j, f: (0, h)),
                spec((tile, 128), lambda h, j, f: (jnp.minimum(j, last), h)),
                spec((tile, 128), lambda h, j, f: (jnp.minimum(j, last), h)),
                spec((128, 128), lambda h, j, f: (0, h)),
                spec((128, 128), lambda h, j, f: (0, h)),
            ],
            scratch_shapes=[
                pltpu.VMEM((2, seg, 128), BF),
                pltpu.VMEM((2, seg, 128), BF),
                pltpu.VMEM((128, seg), F32),
                pltpu.VMEM((2, 1, seg), F32),
            ],
        ),
        out_shape=[jax.ShapeDtypeStruct((seg, pairs * 128), BF)] * 3
        + [jax.ShapeDtypeStruct((128, pairs * 128), BF)] * 2,
        cost_estimate=told(5.5 * pairs * 4),
        compiler_params=pltpu.CompilerParams(vmem_limit_bytes=40 * 2**20),
    )(flags, q, k, v, do, o, sk, sv, lse, start, doc, sdoc, *deps)


def make_meta(doc, tile):
    seg=doc.shape[0]; count=seg//tile
    place=jnp.arange(seg,dtype=jnp.int32)
    new=jnp.concatenate([jnp.ones((1,),bool), doc[1:]!=doc[:-1]])
    start=lax.cummax(jnp.where(new,place,0))
    lo=doc[::tile]; hi=doc[tile-1::tile]
    i=jnp.arange(count)
    full=(lo[None,:]==hi[:,None])&(i[None,:]<i[:,None])
    none=(hi[None,:]<lo[:,None])
    flags=jnp.where(full,2,jnp.where(none,0,1)).astype(jnp.int32).reshape(-1)
    return start.reshape(1,seg), flags


def gate(value, *deps):
    anywhere = pl.BlockSpec(memory_space=pl.ANY)
    return pl.pallas_call(
        lambda *refs: None,
        in_specs=[anywhere] * (1 + len(deps)),
        out_specs=anywhere,
        out_shape=jax.ShapeDtypeStruct(value.shape, value.dtype),
        input_output_aliases={0: 0},
        cost_estimate=SMALL_COST,
    )(value, *deps)


def blank(shape, dtype):
    return pl.pallas_call(
        lambda ref: None,
        out_specs=pl.BlockSpec(memory_space=pl.ANY),
        out_shape=jax.ShapeDtypeStruct(shape, dtype),
        cost_estimate=SMALL_COST,
    )()


def copied(blocks):
    block = pl.BlockSpec((1,) + blocks.shape[1:], lambda i: (i, 0, 0))

    def kernel(source, target):
        target[...] = source[...]

    return pl.pallas_call(
        kernel,
        grid=blocks.shape[:1],
        in_specs=[block],
        out_specs=block,
        out_shape=jax.ShapeDtypeStruct(blocks.shape, blocks.dtype),
        cost_estimate=told(6.0),
        compiler_params=pltpu.CompilerParams(vmem_limit_bytes=24 * 2**20),
    )(blocks)


BOTH = ("rows", "seq")


def other_core(block):
    return lax.ppermute(block, "fsdp", ((0, 1), (1, 0)))


def along_line(field, begin, hold):
    count = lax.axis_size("seq")
    me = lax.axis_index("seq")
    core = lax.axis_index("fsdp")
    half = field.shape[2] // 2
    mine = gate(lax.dynamic_slice_in_dim(field, core * half, half, 2), begin)
    got = jnp.zeros_like(mine)
    own = lax.dynamic_slice_in_dim(mine, me, 1, 0)
    got = lax.dynamic_update_slice_in_dim(got, own, me, 0)
    for away in range(1, count):
        block = lax.dynamic_slice_in_dim(mine, lax.rem(me + away, count), 1, 0)
        moved = lax.ppermute(block, "seq", [(n, (n + away) % count) for n in range(count)])
        moved = gate(moved, *hold)
        got = lax.dynamic_update_slice_in_dim(got, moved, lax.rem(me + count - away, count), 0)
    return got


def between_cores(got, hold=()):
    core = lax.axis_index("fsdp")
    other = other_core(got)
    other = gate(other, *hold) if hold else other
    low_half = jnp.where(core == 0, got, other)
    high_half = jnp.where(core == 0, other, got)
    return jnp.concatenate((low_half, high_half), axis=2)


def shift_by(field, away):
    count = lax.axis_size("seq")
    perm = [(n, n + away) for n in range(count) if 0 <= n + away < count]
    return lax.ppermute(field, "seq", perm)


def both_halves(field):
    low = field.astype(BF)
    return low.astype(F32) + other_core(low).astype(F32)


def norm_forward(field, gain_vec, shift_vec):
    row_mean = jnp.mean(field, axis=-1, keepdims=True)
    centered = field - row_mean
    variance = jnp.mean(centered * centered, axis=-1, keepdims=True)
    scale = lax.rsqrt(variance + norm_eps)
    return (centered * scale * gain_vec + shift_vec).astype(BF)


def mm(a, b):
    return dot_nn(a, b)


def mm_tn(a, b):
    return lax.dot_general(a, b, (((0,), (0,)), ((), ())), preferred_element_type=F32)


def mm_nt(a, b):
    return dot_nt(a, b)


def layer_by_segment(
    states,
    doc_ids,
    w_qkv,
    w_out,
    w_up,
    w_down,
    bias_qv,
    bias_out,
    bias_up,
    bias_down,
    gain_one,
    shift_one,
    gain_two,
    shift_two,
    cotangent,
):
    segs, width, model = states.shape[1:]
    seg_len = segs * width
    place = lax.axis_index("seq")
    half = w_qkv.shape[2]
    hidden_units = w_up.shape[1]
    tile = 512

    small = (bias_qv, bias_out, bias_up, bias_down, gain_one, shift_one, gain_two, shift_two)
    sizes = [item.size for item in small]
    vector = jnp.concatenate([item.reshape(-1) for item in small])
    room = -(-vector.shape[0] // 2048) * 2048
    vector = jnp.pad(vector, (0, room - vector.shape[0])).reshape(-1, 128)
    attn_weights = jnp.concatenate((w_qkv, w_out.T[None]), axis=0)
    attn_full, tokens, packed = opening(attn_weights, states[0], vector)
    tokens = tokens.reshape(seg_len, model)
    packed = packed.reshape(packed.shape[0], -1)
    cuts = []
    at = 0
    for size in sizes:
        cuts.append(packed[:, at : at + size].astype(F32))
        at += size
    shards = packed.shape[0]

    def spread_last(field, lead):
        return jnp.moveaxis(field.reshape(shards, *lead, -1), 0, len(lead)).reshape(-1)

    bias_pair = jnp.moveaxis(cuts[0].reshape(shards, 2, half // HEAD, -1), 0, 2).reshape(2, half)
    bias_o = cuts[1].reshape(-1)
    bias_u = spread_last(cuts[2], (hidden_units // HEAD,))
    bias_d = cuts[3].reshape(-1)
    gain_a, shift_a, gain_b, shift_b = [item.reshape(-1) for item in cuts[4:]]

    docs = doc_ids[0]
    my_docs = lax.dynamic_index_in_dim(docs, place, 0, keepdims=False)
    start, flags = make_meta(my_docs, tile)
    tails = docs[:, seg_len - SUMM :]
    before_one = lax.dynamic_index_in_dim(tails, jnp.maximum(place - 1, 0), 0, keepdims=False)
    before_two = lax.dynamic_index_in_dim(tails, jnp.maximum(place - 2, 0), 0, keepdims=False)
    sum_docs = jnp.concatenate(
        (
            jnp.where(place >= 1, before_one, -1),
            jnp.where(place >= 2, before_two, -1),
            jnp.full((128 - 2 * SUMM,), -1, jnp.int32),
        )
    ).reshape(128, 1)
    doc_row = my_docs.reshape(1, seg_len)

    tokens_f = tokens.astype(F32)
    normed_one = norm_forward(tokens_f, gain_a, shift_a)
    query = product(
        normed_one, attn_full, "nn", functools.partial(finish_bias, HEAD**-0.5), (bias_pair[:1],), planes=(0,)
    )
    keys = product(normed_one, attn_full, "nn", planes=(1,))
    values = product(
        normed_one, attn_full, "nn", functools.partial(finish_bias, 1.0), (bias_pair[1:],), planes=(2,)
    )
    up_full = lax.all_gather(gate(w_up, tokens), BOTH, axis=0, tiled=True)
    tail = jnp.stack((keys[seg_len - SUMM :], values[seg_len - SUMM :]))
    lent = jnp.concatenate((shift_by(tail, 1), shift_by(tail, 2)), axis=1)
    lent = jnp.pad(lent, ((0, 0), (0, 128 - 2 * SUMM), (0, 0)))
    pairs = half // 128
    each = pairs // 4
    attended = ()
    done = []
    for n in range(4):
        attended = attn_fwd(
            query, keys, values, lent[0], lent[1], start, doc_row, sum_docs, flags, tile,
            n * each, each, attended,
        )
        done.append(attended[1])
    down_full = lax.all_gather(gate(w_down.T, values), BOTH, axis=0, tiled=True)
    mixed, log_sum = attended
    attended = product(mixed, attn_full, "nt", planes=(3,))
    grad_out = along_line(cotangent[0], query, (done[2],))
    grad_out = between_cores(grad_out, (attended,)).reshape(seg_len, model)
    hidden = tokens_f + both_halves(attended) + bias_o
    normed_two = norm_forward(hidden, gain_b, shift_b)
    up_proj = mm(normed_two, up_full) + bias_u
    bell = jnp.exp(-0.5 * up_proj * up_proj)
    area = 0.5 * (1.0 + lax.erf(up_proj * (0.5**0.5)))
    activated = (up_proj * area).astype(BF)
    slope = (area + up_proj * bell * 0.3989422804014327).astype(BF)

    def over_rows(partial):
        return lax.psum_scatter(partial, "rows", scatter_dimension=0, tiled=True)

    def over_seq(partial):
        return lax.psum_scatter(partial, "seq", scatter_dimension=0, tiled=True)

    down_sum = product(grad_out, activated, "tn")
    down_rows = over_rows(down_sum)
    slope = gate(slope, down_sum)
    d_up = (mm(grad_out, down_full) * slope.astype(F32)).astype(BF)
    up_sum = product(normed_two, d_up, "tn")
    def column_sum(field):
        return jnp.sum(field.astype(F32), axis=0)

    d_norm_part = product(d_up, up_full, "nt", deps=(up_sum,))
    sum_grad_out = column_sum(grad_out)
    d_norm_other = gate(other_core(d_norm_part), sum_grad_out)
    up_turn = gate(up_sum, down_rows, d_norm_other)
    up_rows = over_rows(up_turn)
    d_hidden, d_hidden_low, sums_two = norm_back(
        hidden, d_norm_part, d_norm_other, grad_out, gain_b, (F32, BF)
    )
    d_mixed = product(d_hidden_low, attn_full, "nn", deps=(up_turn,), planes=(3,))
    out_sum = product(d_hidden_low, mixed, "tn", deps=(d_mixed,))

    def back(n, count, deps):
        return attn_bwd(
            query, keys, values, d_mixed, mixed, lent[0], lent[1], log_sum, start, doc_row,
            sum_docs, flags, tile, n * each, count * each, deps,
        )

    def own_half(pieces, move, deps=()):
        d_pre, d_keys, d_values, d_lent_k, d_lent_v = [
            jnp.concatenate(pair, axis=1) if len(pair) > 1 else pair[0] for pair in zip(*pieces)
        ]
        d_lent = jnp.stack((d_lent_k, d_lent_v))
        back_home = shift_by(d_lent[:, :SUMM], -1).astype(F32) + shift_by(
            d_lent[:, SUMM : 2 * SUMM], -2
        ).astype(F32)
        ends = jnp.stack((d_keys[seg_len - SUMM :], d_values[seg_len - SUMM :])).astype(F32)
        ends = (ends + back_home).astype(BF)
        d_keys = lax.dynamic_update_slice(d_keys, ends[0], (seg_len - SUMM, 0))
        d_values = lax.dynamic_update_slice(d_values, ends[1], (seg_len - SUMM, 0))
        grads = jnp.concatenate((d_pre, d_keys, d_values), axis=1)
        return grads, product(
            normed_one, grads, "tn", blocks=(1024, grads.shape[1] // 2, 2048), move=move, deps=deps
        )

    piece_0 = back(0, 1, (out_sum,))
    out_partial = product(activated, down_full, "nt", deps=(piece_0[0],))
    down_turn = gate(down_rows, up_rows, out_partial)
    down_seq = over_seq(down_turn)
    grad_w_down = down_seq.astype(F32)
    out_tokens = (hidden + both_halves(out_partial) + bias_d).astype(BF).reshape(segs, width, model)
    out_own = lax.dynamic_slice_in_dim(out_tokens, place, 1, 0)
    out_begun = lax.dynamic_update_slice_in_dim(blank(out_tokens.shape, BF), out_own, place, 0)
    piece_1 = back(1, 1, (down_turn, out_begun))
    out_turn = gate(out_sum, down_seq, piece_1[0])
    out_rows = over_rows(out_turn)
    first_half, (first_sum, out_moved) = own_half((piece_0, piece_1), (out_tokens, out_begun, (1,), 2), (out_turn,))
    up_turn_two = gate(up_rows, out_rows, first_sum)
    up_seq = over_seq(up_turn_two)
    grad_w_up = up_seq.astype(F32)
    first_turn = gate(first_sum, up_turn_two)
    first_rows = over_rows(first_turn)
    piece_2 = back(2, 2, (first_turn,))
    second_half, (second_sum, out_moved) = own_half((piece_2,), (out_tokens, out_moved, (segs - 1,), 3))
    second_turn = gate(second_sum, first_rows, up_seq)
    second_rows = over_rows(second_turn)
    d_qkv = jnp.concatenate((first_half, second_half), axis=1)
    d_norm_part, out_moved = product(
        d_qkv, attn_full, "nt", deps=(second_turn,), blocks=(1024, 1024, half // 2), planes=(0, 1, 2),
        move=(out_tokens, out_moved, tuple(range(2, segs - 1)), 4),
    )
    out_states = copied(out_moved)[None]
    kind_sum = column_sum(d_qkv).reshape(2, 3, half // 2)
    d_norm_other = gate(other_core(d_norm_part), kind_sum, out_states)
    grad_tokens, sums_one = norm_back(
        tokens, d_norm_part, d_norm_other, d_hidden, gain_a, (BF,)
    )
    grad_w_down = grad_w_down.T
    qkv_rows = jnp.concatenate((out_rows, first_rows, gate(second_rows, d_norm_other)), axis=1)
    attn_seq = over_seq(qkv_rows).astype(F32)
    grad_w_out, grad_w_qkv = attn_seq[:, :half].T, attn_seq[:, half:]
    grad_w_qkv = jnp.transpose(grad_w_qkv.reshape(-1, 2, 3, half // 2), (2, 0, 1, 3)).reshape(3, -1, half)

    sums = (
        jnp.moveaxis(
            jnp.stack((kind_sum[:, 0], kind_sum[:, 2])).reshape(2, half // HEAD, shards, -1), 2, 0
        ),
        sums_two[2],
        jnp.moveaxis(column_sum(d_up).reshape(hidden_units // HEAD, shards, -1), 1, 0),
        sum_grad_out,
        sums_one[0],
        sums_one[1],
        sums_two[0],
        sums_two[1],
    )
    vectors = jnp.concatenate([item.reshape(shards, -1) for item in sums], axis=1)
    vectors = jnp.pad(vectors, ((0, 0), (0, room - vectors.shape[1]))).reshape(shards, -1, 128)
    grad_states, vector = closing(grad_tokens.reshape(segs, width, model), gate(vectors, qkv_rows))
    grad_states = grad_states[None]
    vector = vector.reshape(-1)
    small_grads = []
    at = 0
    for item, size in zip(small, sizes):
        small_grads.append(vector[at : at + size].reshape(item.shape))
        at += size
    return (out_states, grad_states, grad_w_qkv, grad_w_out, grad_w_up, grad_w_down, *small_grads)


def solution(mesh):
    whole_segments = mesh.shape["seq"] == SEGS and mesh.shape["rows"] == 4
    return jax.shard_map(
        layer_by_segment if whole_segments else local,
        mesh=mesh,
        in_specs=(
            P("rows", None, "seq", None),
            P("rows", None, None),
            P(None, ("rows", "seq"), "fsdp"),
            P("fsdp", ("rows", "seq")),
            P(("rows", "seq"), "fsdp"),
            P("fsdp", ("rows", "seq")),
            P(None, "fsdp", ("rows", "seq")),
            P(("rows", "seq")),
            P("fsdp", ("rows", "seq")),
            P(("rows", "seq")),
            P(("rows", "seq")),
            P(("rows", "seq")),
            P(("rows", "seq")),
            P(("rows", "seq")),
            P("rows", None, "seq", None),
        ),
        out_specs=(
            P("rows", None, "seq", None),
            P("rows", None, "seq", None),
            P(None, ("rows", "seq"), "fsdp"),
            P("fsdp", ("rows", "seq")),
            P(("rows", "seq"), "fsdp"),
            P("fsdp", ("rows", "seq")),
            P(None, "fsdp", ("rows", "seq")),
            P(("rows", "seq")),
            P("fsdp", ("rows", "seq")),
            P(("rows", "seq")),
            P(("rows", "seq")),
            P(("rows", "seq")),
            P(("rows", "seq")),
            P(("rows", "seq")),
        ),
        check_vma=False,
    )
```

```python
import functools

import jax
import jax.numpy as jnp
from jax import lax
from jax.experimental import pallas as pl
from jax.experimental.pallas import tpu as pltpu
from jax.sharding import PartitionSpec as P

HEAD = 64
SUMM = 50
SEGS = 4
F32 = jnp.float32
BF = jnp.bfloat16
SMALL_COST = pl.CostEstimate(flops=1000, bytes_accessed=1000, transcendentals=0)


def told(microseconds):
    return pl.CostEstimate(flops=int(microseconds * 1e9), bytes_accessed=1000, transcendentals=0)


neg_big = -1e30
norm_eps = 1e-05


def spread(block, axis, source):
    block = jnp.where(lax.axis_index(axis) == source, block, jnp.zeros_like(block))
    return lax.psum(block, axis)


def layer_norm(field, gain_vec, shift_vec):
    row_mean = jnp.mean(field, axis=-1, keepdims=True)
    centered = field - row_mean
    variance = jnp.mean(centered * centered, axis=-1, keepdims=True)
    return centered * lax.rsqrt(variance + norm_eps) * gain_vec + shift_vec


def gelu_exact(field):
    return jax.nn.gelu(field, approximate=False)


def earlier(field, offset, fill_value):
    widths = tuple(((offset, 0) if dim_index == 1 else (0, 0) for dim_index in range(field.ndim)))
    return jnp.pad(field, widths, constant_values=fill_value)[:, : field.shape[1]]


def later(field, offset):
    widths = tuple(((0, offset) if dim_index == 1 else (0, 0) for dim_index in range(field.ndim)))
    return jnp.pad(field, widths)[:, offset:]


def lead(field):
    return jnp.moveaxis(field, 1, 0)


def halves(field):
    return lax.psum(field.astype(jnp.bfloat16), "fsdp").astype(jnp.float32)


def local(
    states,
    doc_ids,
    w_qkv,
    w_out,
    w_up,
    w_down,
    bias_qv,
    bias_out,
    bias_up,
    bias_down,
    gain_one,
    shift_one,
    gain_two,
    shift_two,
    cotangent,
):
    attn_full = (
        lax.all_gather(w_qkv, ("rows", "seq"), axis=1, tiled=True),
        lax.all_gather(w_out, ("rows", "seq"), axis=1, tiled=True),
        lax.all_gather(bias_qv, ("rows", "seq"), axis=2, tiled=True),
        lax.all_gather(gain_one, ("rows", "seq"), axis=0, tiled=True),
        lax.all_gather(shift_one, ("rows", "seq"), axis=0, tiled=True),
        lax.all_gather(bias_out, ("rows", "seq"), axis=0, tiled=True),
    )
    qkv_full, out_full, bqv_full, gain_a, shift_a, bias_o = attn_full
    rows_dev, seg_count, width, model = states.shape
    seq_count = lax.axis_size("seq")
    seq_place = lax.axis_index("seq")
    seg_len = width * seq_count
    half_width = qkv_full.shape[2]
    heads_loc = half_width // HEAD
    score_scale = HEAD ** (-0.5)
    states_f = states.astype(jnp.float32)
    normed_f, norm_one_back = jax.vjp(
        layer_norm, states_f, gain_a.astype(jnp.float32), shift_a.astype(jnp.float32)
    )
    normed_one = normed_f.astype(jnp.bfloat16)
    projected = jnp.einsum(
        "rsid,kde->krsie", normed_one, qkv_full, preferred_element_type=jnp.float32
    )
    bias_pair = bqv_full.astype(jnp.float32).reshape(2, half_width)
    query = ((projected[0] + bias_pair[0]) * score_scale).astype(jnp.bfloat16)
    keys = projected[1].astype(jnp.bfloat16)
    values = (projected[2] + bias_pair[1]).astype(jnp.bfloat16)
    tail = jnp.stack((keys[:, :, width - SUMM :], values[:, :, width - SUMM :]))
    summary = spread(tail, "seq", seq_count - 1)
    sum_keys = jnp.concatenate((earlier(summary[0], 1, 0.0), earlier(summary[0], 2, 0.0)), axis=2)
    sum_values = jnp.concatenate((earlier(summary[1], 1, 0.0), earlier(summary[1], 2, 0.0)), axis=2)
    sum_src = doc_ids[:, :, seg_len - SUMM :]
    sum_docs = jnp.concatenate((earlier(sum_src, 1, -1), earlier(sum_src, 2, -1)), axis=2)
    sum_k5 = sum_keys.reshape(rows_dev, seg_count, 2 * SUMM, heads_loc, HEAD)
    sum_v5 = sum_values.reshape(rows_dev, seg_count, 2 * SUMM, heads_loc, HEAD)
    first_pos = seq_place * width
    query_docs = lax.dynamic_slice_in_dim(doc_ids, first_pos, width, 2)
    query_pos = first_pos + jnp.arange(width, dtype=jnp.int32)
    query5 = query.reshape(rows_dev, seg_count, width, heads_loc, HEAD)
    sum_allowed = (query_docs[:, :, :, None] == sum_docs[:, :, None, :])[:, :, None]
    sum_scores = jnp.einsum(
        "rsihe,rsjhe->rshij", query5, sum_k5, preferred_element_type=jnp.float32
    )
    sum_scores = jnp.where(sum_allowed, sum_scores, neg_big)
    start_max = jnp.max(sum_scores, axis=-1)
    start_exp = jnp.where(sum_allowed, jnp.exp(sum_scores - start_max[..., None]), 0.0)
    start_sum = jnp.sum(start_exp, axis=-1)
    start_acc = jnp.einsum(
        "rshij,rsjhe->rsihe",
        start_exp.astype(jnp.bfloat16),
        sum_v5,
        preferred_element_type=jnp.float32,
    )
    key_piece = lax.all_gather(keys, "seq", axis=2, tiled=True)
    value_piece = lax.all_gather(values, "seq", axis=2, tiled=True)
    count = key_piece.shape[2]
    key5 = key_piece.reshape(rows_dev, seg_count, count, heads_loc, HEAD)
    value5 = value_piece.reshape(rows_dev, seg_count, count, heads_loc, HEAD)
    key_pos = jnp.arange(count, dtype=jnp.int32)
    causal = (key_pos[None, :] <= query_pos[:, None])[None, None, None]
    allowed = causal & (query_docs[:, :, :, None] == doc_ids[:, :, None, :])[:, :, None]
    scores = jnp.einsum("rsihe,rsjhe->rshij", query5, key5, preferred_element_type=jnp.float32)
    scores = jnp.where(allowed, scores, neg_big)
    new_max = jnp.maximum(start_max, jnp.max(scores, axis=-1))
    factor = jnp.exp(start_max - new_max)
    exponent = jnp.where(allowed, jnp.exp(scores - new_max[..., None]), 0.0)
    new_sum = start_sum * factor + jnp.sum(exponent, axis=-1)
    gained = jnp.einsum(
        "rshij,rsjhe->rsihe",
        exponent.astype(jnp.bfloat16),
        value5,
        preferred_element_type=jnp.float32,
    )
    new_acc = start_acc * jnp.swapaxes(factor, 2, 3)[..., None] + gained
    log_sum = new_max + jnp.log(new_sum)
    mixed_f = new_acc / jnp.swapaxes(new_sum, 2, 3)[..., None]
    mixed = mixed_f.reshape(rows_dev, seg_count, width, half_width).astype(jnp.bfloat16)
    attn_lin = halves(
        jnp.einsum("rsie,ed->rsid", mixed, out_full, preferred_element_type=jnp.float32)
    )
    hidden = states_f + attn_lin + bias_o.astype(jnp.float32)
    ffn_full = (
        lax.all_gather(w_up, ("rows", "seq"), axis=0, tiled=True),
        lax.all_gather(w_down, ("rows", "seq"), axis=1, tiled=True),
        lax.all_gather(bias_up, ("rows", "seq"), axis=1, tiled=True),
        lax.all_gather(gain_two, ("rows", "seq"), axis=0, tiled=True),
        lax.all_gather(shift_two, ("rows", "seq"), axis=0, tiled=True),
        lax.all_gather(bias_down, ("rows", "seq"), axis=0, tiled=True),
    )
    up_full, down_full, bias_u, gain_b, shift_b, bias_d = ffn_full
    normed_two_f, norm_two_back = jax.vjp(
        layer_norm, hidden, gain_b.astype(jnp.float32), shift_b.astype(jnp.float32)
    )
    normed_two = normed_two_f.astype(jnp.bfloat16)
    up_proj = jnp.einsum(
        "rsid,df->rsif", normed_two, up_full, preferred_element_type=jnp.float32
    ) + bias_u.astype(jnp.float32).reshape(-1)
    activated_f, gelu_back = jax.vjp(gelu_exact, up_proj)
    activated = activated_f.astype(jnp.bfloat16)
    down_proj = halves(
        jnp.einsum("rsif,fd->rsid", activated, down_full, preferred_element_type=jnp.float32)
    )
    out_states = (hidden + down_proj + bias_d.astype(jnp.float32)).astype(jnp.bfloat16)
    up_back, down_back = (
        lax.all_gather(w_up, ("rows", "seq"), axis=0, tiled=True),
        lax.all_gather(w_down, ("rows", "seq"), axis=1, tiled=True),
    )
    qkv_back, out_back = (
        lax.all_gather(w_qkv, ("rows", "seq"), axis=1, tiled=True),
        lax.all_gather(w_out, ("rows", "seq"), axis=1, tiled=True),
    )
    grad_out = cotangent.astype(jnp.float32)
    grad_bias_down = jnp.sum(grad_out, axis=(0, 1, 2))
    grad_w_down = jnp.einsum(
        "rsif,rsid->fd", activated, cotangent, preferred_element_type=jnp.float32
    )
    d_act = jnp.einsum("rsid,fd->rsif", cotangent, down_back, preferred_element_type=jnp.float32)
    (d_up,) = gelu_back(d_act)
    d_up_low = d_up.astype(jnp.bfloat16)
    grad_bias_up = jnp.sum(d_up_low, axis=(0, 1, 2), dtype=jnp.float32).reshape(bias_u.shape)
    grad_w_up = jnp.einsum(
        "rsid,rsif->df", normed_two, d_up_low, preferred_element_type=jnp.float32
    )
    d_norm_two = halves(
        jnp.einsum("rsif,df->rsid", d_up_low, up_back, preferred_element_type=jnp.float32)
    )
    d_hidden_ln, grad_gain_two, grad_shift_two = norm_two_back(d_norm_two)
    d_hidden = grad_out + d_hidden_ln
    ffn_grads = (
        lax.psum_scatter(grad_w_up, ("rows", "seq"), scatter_dimension=0, tiled=True),
        lax.psum_scatter(grad_w_down, ("rows", "seq"), scatter_dimension=1, tiled=True),
        lax.psum_scatter(grad_bias_up, ("rows", "seq"), scatter_dimension=1, tiled=True),
        lax.psum_scatter(grad_gain_two, ("rows", "seq"), scatter_dimension=0, tiled=True),
        lax.psum_scatter(grad_shift_two, ("rows", "seq"), scatter_dimension=0, tiled=True),
        lax.psum_scatter(grad_bias_down, ("rows", "seq"), scatter_dimension=0, tiled=True),
    )
    grad_bias_out = jnp.sum(d_hidden, axis=(0, 1, 2))
    d_hidden_low = d_hidden.astype(jnp.bfloat16)
    grad_w_out = jnp.einsum(
        "rsie,rsid->ed", mixed, d_hidden_low, preferred_element_type=jnp.float32
    )
    d_mixed = jnp.einsum(
        "rsid,ed->rsie", d_hidden_low, out_back, preferred_element_type=jnp.float32
    ).astype(jnp.bfloat16)
    d_mixed5 = d_mixed.reshape(rows_dev, seg_count, width, heads_loc, HEAD)
    keys_all, values_all = (
        lax.all_gather(keys, "seq", axis=2, tiled=True),
        lax.all_gather(values, "seq", axis=2, tiled=True),
    )
    key_lead = lead(keys_all.reshape(rows_dev, seg_count, seg_len, heads_loc, HEAD))
    value_lead = lead(values_all.reshape(rows_dev, seg_count, seg_len, heads_loc, HEAD))
    query_lead = lead(query5)
    grad_lead = lead(d_mixed5)
    key_positions = jnp.arange(seg_len, dtype=jnp.int32)

    def segment_back(seg_items):
        q_seg, do_seg, lse_seg, qdoc_seg, k_seg, v_seg, kdoc_seg, sk_seg, sv_seg, sdoc_seg = (
            seg_items
        )
        causal = (key_positions[None, :] <= query_pos[:, None])[None, None]
        allowed = causal & (qdoc_seg[:, :, None] == kdoc_seg[:, None, :])[:, None]
        scores = jnp.einsum("rihe,rjhe->rhij", q_seg, k_seg, preferred_element_type=jnp.float32)
        attn_probs = jnp.where(allowed, jnp.exp(scores - lse_seg[..., None]), 0.0)
        d_probs = jnp.einsum("rihe,rjhe->rhij", do_seg, v_seg, preferred_element_type=jnp.float32)
        summ_allowed = (qdoc_seg[:, :, None] == sdoc_seg[:, None, :])[:, None]
        summ_scores = jnp.einsum(
            "rihe,rjhe->rhij", q_seg, sk_seg, preferred_element_type=jnp.float32
        )
        summ_probs = jnp.where(summ_allowed, jnp.exp(summ_scores - lse_seg[..., None]), 0.0)
        summ_dprobs = jnp.einsum(
            "rihe,rjhe->rhij", do_seg, sv_seg, preferred_element_type=jnp.float32
        )
        delta = jnp.sum(attn_probs * d_probs, axis=-1) + jnp.sum(summ_probs * summ_dprobs, axis=-1)
        d_scores = (attn_probs * (d_probs - delta[..., None])).astype(jnp.bfloat16)
        d_summ = (summ_probs * (summ_dprobs - delta[..., None])).astype(jnp.bfloat16)
        d_query = jnp.einsum("rhij,rjhe->rihe", d_scores, k_seg, preferred_element_type=jnp.float32)
        d_query = d_query + jnp.einsum(
            "rhij,rjhe->rihe", d_summ, sk_seg, preferred_element_type=jnp.float32
        )
        d_sum_keys = jnp.einsum(
            "rhij,rihe->rjhe", d_summ, q_seg, preferred_element_type=jnp.float32
        )
        d_sum_values = jnp.einsum(
            "rhij,rihe->rjhe",
            summ_probs.astype(jnp.bfloat16),
            do_seg,
            preferred_element_type=jnp.float32,
        )
        return (d_query, d_scores, attn_probs.astype(jnp.bfloat16), d_sum_keys, d_sum_values, delta)

    seg_inputs = (
        query_lead,
        grad_lead,
        lead(log_sum),
        lead(query_docs),
        key_lead,
        value_lead,
        lead(doc_ids),
        lead(sum_k5),
        lead(sum_v5),
        lead(sum_docs),
    )
    d_query_lead, d_scores_all, probs_all, d_sk_lead, d_sv_lead, delta_lead = lax.map(
        segment_back, seg_inputs
    )
    d_key_part = jnp.einsum(
        "srhij,srihe->jrshe", d_scores_all, query_lead, preferred_element_type=jnp.float32
    )
    d_value_part = jnp.einsum(
        "srhij,srihe->jrshe", probs_all, grad_lead, preferred_element_type=jnp.float32
    )
    key_grads = lax.psum_scatter(
        jnp.stack((d_key_part, d_value_part), axis=3)
        .reshape(width * lax.axis_size("seq"), rows_dev, seg_count, 2, half_width)
        .astype(jnp.bfloat16),
        "seq",
        scatter_dimension=0,
        tiled=True,
    ).astype(jnp.float32)
    key_grads = jnp.transpose(key_grads, (3, 1, 2, 0, 4))
    d_sk = jnp.moveaxis(d_sk_lead, 0, 1).reshape(rows_dev, seg_count, 2 * SUMM, half_width)
    d_sv = jnp.moveaxis(d_sv_lead, 0, 1).reshape(rows_dev, seg_count, 2 * SUMM, half_width)
    src_keys = later(d_sk[:, :, :SUMM], 1) + later(d_sk[:, :, SUMM:], 2)
    src_values = later(d_sv[:, :, :SUMM], 1) + later(d_sv[:, :, SUMM:], 2)
    summ_grads = lax.psum(jnp.stack((src_keys, src_values)).astype(jnp.bfloat16), "seq").astype(
        jnp.float32
    )
    owner_grads = jnp.where(seq_place == seq_count - 1, summ_grads, 0.0)
    owner_grads = jnp.pad(owner_grads, ((0, 0), (0, 0), (0, 0), (width - SUMM, 0), (0, 0)))
    key_grads = key_grads + owner_grads
    d_keys_low = key_grads[0].astype(jnp.bfloat16)
    d_values_low = key_grads[1].astype(jnp.bfloat16)
    d_query = jnp.moveaxis(d_query_lead, 0, 1).reshape(rows_dev, seg_count, width, half_width)
    d_query_low = d_query.astype(jnp.bfloat16)
    d_pre = (d_query_low.astype(jnp.float32) * score_scale).astype(jnp.bfloat16)
    grad_bias_qv = jnp.stack(
        (
            jnp.sum(d_pre, axis=(0, 1, 2), dtype=jnp.float32),
            jnp.sum(d_values_low, axis=(0, 1, 2), dtype=jnp.float32),
        )
    ).reshape(bqv_full.shape)
    d_qkv = jnp.stack((d_pre, d_keys_low, d_values_low))
    grad_w_qkv = jnp.einsum(
        "rsid,krsie->kde", normed_one, d_qkv, preferred_element_type=jnp.float32
    )
    d_norm_one = halves(
        jnp.einsum("krsie,kde->rsid", d_qkv, qkv_back, preferred_element_type=jnp.float32)
    )
    d_states_ln, grad_gain_one, grad_shift_one = norm_one_back(d_norm_one)
    grad_states = (d_hidden + d_states_ln).astype(jnp.bfloat16)
    attn_grads = (
        lax.psum_scatter(grad_w_qkv, ("rows", "seq"), scatter_dimension=1, tiled=True),
        lax.psum_scatter(grad_w_out, ("rows", "seq"), scatter_dimension=1, tiled=True),
        lax.psum_scatter(grad_bias_qv, ("rows", "seq"), scatter_dimension=2, tiled=True),
        lax.psum_scatter(grad_gain_one, ("rows", "seq"), scatter_dimension=0, tiled=True),
        lax.psum_scatter(grad_shift_one, ("rows", "seq"), scatter_dimension=0, tiled=True),
        lax.psum_scatter(grad_bias_out, ("rows", "seq"), scatter_dimension=0, tiled=True),
    )
    return (
        out_states,
        grad_states,
        attn_grads[0],
        attn_grads[1],
        ffn_grads[0],
        ffn_grads[1],
        attn_grads[2],
        attn_grads[5],
        ffn_grads[2],
        ffn_grads[5],
        attn_grads[3],
        attn_grads[4],
        ffn_grads[3],
        ffn_grads[4],
    )


def opening_kernel(w_ref, s_ref, v_ref, whole_ref, tokens_ref, vectors_ref, z_send, z_recv, x_send, x_recv, y_send, y_recv,
                   fx_send, fx_recv, fy_send, fy_recv, t_send, t_recv, c_send, c_recv, v_send, v_recv, own):
    rows, place, core = lax.axis_index("rows"), lax.axis_index("seq"), lax.axis_index("fsdp")
    count = s_ref.shape[0]
    depth = w_ref.shape[1]
    half = w_ref.shape[2] // 2
    width = s_ref.shape[2] // 2
    steps = count - 1

    def at(row, seq, fsdp=None):
        return (row, seq, core if fsdp is None else fsdp)

    def hail(device):
        pl.semaphore_signal(barrier, inc=1, device_id=device, device_id_type=pl.DeviceIdType.MESH)

    barrier = pltpu.get_barrier_semaphore()
    for away in range(4):
        for along in range(count):
            if away or along:
                hail(at(rows ^ away, lax.rem(place + along, count)))
    hail(at(rows, place, 1 - core))
    pl.semaphore_wait(barrier, 4 * count)

    def shard(ref, row, seq, cut=None):
        first = pl.multiple_of((row * count + seq) * depth, depth)
        if cut is None:
            return ref.at[:, pl.ds(first, depth)]
        return ref.at[:, pl.ds(first, depth), pl.ds(cut * half, half)]

    def remote(src, dst, send, recv, device):
        return pltpu.make_async_remote_copy(
            src_ref=src, dst_ref=dst, send_sem=send, recv_sem=recv, device_id=device,
            device_id_type=pl.DeviceIdType.MESH,
        )

    x_peer, y_peer = rows ^ 1, rows ^ 2

    def spread(t, side, seq, src):
        mine = shard(whole_ref, rows, seq)
        src = mine if src is None else src
        return (
            remote(src, mine, x_send.at[t, side], x_recv.at[t, side], at(x_peer, place)),
            remote(src, mine, y_send.at[t, side], y_recv.at[t, side], at(y_peer, place)),
        )

    def arrived(t, side, seq):
        from_x, from_y = shard(whole_ref, x_peer, seq), shard(whole_ref, y_peer, seq)
        return (
            remote(from_x, from_x, x_send.at[t, side], x_recv.at[t, side], at(x_peer, place)),
            remote(from_y, from_y, y_send.at[t, side], y_recv.at[t, side], at(y_peer, place)),
        )

    def onward(t, side, seq):
        a, b = shard(whole_ref, x_peer, seq, 0), shard(whole_ref, y_peer, seq, 1)
        return (
            remote(a, a, fy_send.at[t, side], fy_recv.at[t, side], at(y_peer, place)),
            remote(b, b, fx_send.at[t, side], fx_recv.at[t, side], at(x_peer, place)),
        )

    def far(t, side, seq):
        a, b = shard(whole_ref, rows ^ 3, seq, 0), shard(whole_ref, rows ^ 3, seq, 1)
        return (
            remote(a, a, fy_send.at[t, side], fy_recv.at[t, side], at(y_peer, place)),
            remote(b, b, fx_send.at[t, side], fx_recv.at[t, side], at(x_peer, place)),
        )

    def along_z(t, side, seq, src):
        mine = shard(whole_ref, rows, seq)
        to = place + 1 if side == 0 else place - 1
        return remote(mine if src is None else src, mine, z_send.at[t, side], z_recv.at[t, side], at(rows, to))

    def origin(t, side):
        return place - t if side == 0 else place + t

    def has(t, side):
        return origin(t, side) >= 0 if side == 0 else origin(t, side) < count

    def has_next(side):
        return place + 1 < count if side == 0 else place >= 1

    for side in range(2):
        @pl.when(has_next(side))
        def _(side=side):
            along_z(1, side, place, w_ref).start()
    for copy in spread(0, 0, place, w_ref):
        copy.start()
    local = pltpu.make_async_copy(w_ref, shard(whole_ref, rows, place), own.at[0])
    local.start()
    vectors = []
    for away in range(4):
        for along in range(count):
            if away or along:
                mine = rows * count + place
                copy = remote(
                    v_ref, vectors_ref.at[mine], v_send.at[away, along], v_recv.at[away, along],
                    at(rows ^ away, lax.rem(place + along, count)),
                )
                copy.start()
                vectors.append(copy)
    local_v = pltpu.make_async_copy(v_ref, vectors_ref.at[rows * count + place], own.at[1])
    local_v.start()

    columns = pl.ds(pl.multiple_of(core * width, width), width)

    def token_copy(along):
        to = lax.rem(place + along, count)
        return remote(
            s_ref.at[to, :, columns], tokens_ref.at[place, :, columns], t_send.at[along], t_recv.at[along], at(rows, to)
        )

    def token_got(along):
        start = lax.rem(place + count - along, count)
        view = tokens_ref.at[start, :, columns]
        return remote(view, view, t_send.at[along], t_recv.at[along], at(rows, start))

    def token_on(along):
        view = tokens_ref.at[lax.rem(place + count - along, count), :, columns]
        return remote(view, view, c_send.at[along], c_recv.at[along], at(rows, place, 1 - core))

    def token_far(along):
        start = lax.rem(place + count - along, count)
        view = tokens_ref.at[start, :, pl.ds(pl.multiple_of((1 - core) * width, width), width)]
        return remote(view, view, c_send.at[along], c_recv.at[along], at(rows, place, 1 - core))

    local_t = pltpu.make_async_copy(s_ref.at[place], tokens_ref.at[place], own.at[2])
    local_t.start()

    def pass_on(t, side, seq):
        for got in arrived(t, side, seq):
            got.wait_recv()
        for copy in onward(t, side, seq):
            copy.start()

    for t in range(1, steps + 1):
        for side in range(2):
            @pl.when(has(t, side))
            def _(t=t, side=side):
                seq = origin(t, side)
                along_z(t, side, seq, None).wait_recv()
                if t < steps:
                    @pl.when(has_next(side))
                    def _():
                        along_z(t + 1, side, seq, None).start()
                for copy in spread(t, side, seq, None):
                    copy.start()
        if t == 1:
            for along in range(1, count):
                token_copy(along).start()
            pass_on(0, 0, place)
        else:
            for side in range(2):
                @pl.when(has(t - 1, side))
                def _(t=t, side=side):
                    pass_on(t - 1, side, origin(t - 1, side))
    for side in range(2):
        @pl.when(has(steps, side))
        def _(side=side):
            pass_on(steps, side, origin(steps, side))

    for along in range(1, count):
        token_got(along).wait_recv()
        token_on(along).start()

    def settle(t, side, seq, src):
        for copy in spread(t, side, seq, src):
            copy.wait_send()
        for copy in onward(t, side, seq):
            copy.wait_send()
        for got in far(t, side, seq):
            got.wait_recv()

    settle(0, 0, place, w_ref)
    for t in range(1, steps + 1):
        for side in range(2):
            @pl.when(has(t, side))
            def _(t=t, side=side):
                settle(t, side, origin(t, side), None)

            @pl.when(has(t - 1, side) & has_next(side))
            def _(t=t, side=side):
                along_z(t, side, origin(t - 1, side), w_ref if t == 1 else None).wait_send()
    for copy in vectors:
        copy.wait_send()
    for away in range(4):
        for along in range(count):
            if away or along:
                start = (rows ^ away) * count + lax.rem(place + count - along, count)
                view = vectors_ref.at[start]
                remote(
                    view, view, v_send.at[away, along], v_recv.at[away, along],
                    at(rows ^ away, lax.rem(place + count - along, count)),
                ).wait_recv()
    for along in range(1, count):
        token_copy(along).wait_send()
        token_on(along).wait_send()
        token_far(along).wait_recv()
    local.wait()
    local_v.wait()
    local_t.wait()


def opening(w, tokens, vector):
    count = tokens.shape[0]
    kinds, depth, half = w.shape
    dma = pltpu.SemaphoreType.DMA
    pair = [dma((count, 2)), dma((count, 2))]
    anywhere = pl.BlockSpec(memory_space=pl.ANY)
    return pl.pallas_call(
        opening_kernel,
        in_specs=[anywhere] * 3,
        out_specs=[anywhere] * 3,
        out_shape=[
            jax.ShapeDtypeStruct((kinds, depth * 4 * count, half), w.dtype),
            jax.ShapeDtypeStruct(tokens.shape, tokens.dtype),
            jax.ShapeDtypeStruct((4 * count,) + vector.shape, vector.dtype),
        ],
        scratch_shapes=pair * 5 + [dma((count,))] * 4 + [dma((4, count))] * 2 + [dma((3,))],
        compiler_params=pltpu.CompilerParams(collective_id=0, has_side_effects=True),
    )(w, tokens, vector)


def closing_kernel(s_ref, v_ref, tokens_ref, sum_ref, held, t_send, t_recv, c_send, c_recv, v_send, v_recv, own):
    rows, place, core = lax.axis_index("rows"), lax.axis_index("seq"), lax.axis_index("fsdp")
    count = s_ref.shape[0]
    width = s_ref.shape[2] // 2

    def at(row, seq, fsdp=None):
        return (row, seq, core if fsdp is None else fsdp)

    def hail(device):
        pl.semaphore_signal(barrier, inc=1, device_id=device, device_id_type=pl.DeviceIdType.MESH)

    barrier = pltpu.get_barrier_semaphore()
    for away in range(4):
        for along in range(count):
            if away or along:
                hail(at(rows ^ away, lax.rem(place + along, count)))
    hail(at(rows, place, 1 - core))
    pl.semaphore_wait(barrier, 4 * count)

    def remote(src, dst, send, recv, device):
        return pltpu.make_async_remote_copy(
            src_ref=src, dst_ref=dst, send_sem=send, recv_sem=recv, device_id=device,
            device_id_type=pl.DeviceIdType.MESH,
        )

    columns = pl.ds(pl.multiple_of(core * width, width), width)
    others = pl.ds(pl.multiple_of((1 - core) * width, width), width)

    def token_copy(along):
        to = lax.rem(place + along, count)
        return remote(
            s_ref.at[to, :, columns], tokens_ref.at[place, :, columns], t_send.at[along], t_recv.at[along], at(rows, to)
        )

    def token_got(along):
        start = lax.rem(place + count - along, count)
        view = tokens_ref.at[start, :, columns]
        return remote(view, view, t_send.at[along], t_recv.at[along], at(rows, start))

    def token_on(along):
        view = tokens_ref.at[lax.rem(place + count - along, count), :, columns]
        return remote(view, view, c_send.at[along], c_recv.at[along], at(rows, place, 1 - core))

    def token_far(along):
        view = tokens_ref.at[lax.rem(place + count - along, count), :, others]
        return remote(view, view, c_send.at[along], c_recv.at[along], at(rows, place, 1 - core))

    for along in range(1, count):
        token_copy(along).start()
    local_t = pltpu.make_async_copy(s_ref.at[place], tokens_ref.at[place], own.at[0])
    local_t.start()
    mine = rows * count + place
    vectors = []
    for away in range(4):
        for along in range(count):
            if away or along:
                to_row, to_seq = rows ^ away, lax.rem(place + along, count)
                copy = remote(
                    v_ref.at[to_row * count + to_seq], held.at[away * count + along],
                    v_send.at[away, along], v_recv.at[away, along], at(to_row, to_seq),
                )
                copy.start()
                vectors.append(copy)
    local_v = pltpu.make_async_copy(v_ref.at[mine], held.at[0], own.at[1])
    local_v.start()
    local_v.wait()
    for copy in vectors:
        copy.wait_recv()
    sum_ref[...] = jnp.sum(held[...], axis=0)
    for along in range(1, count):
        token_got(along).wait_recv()
        token_on(along).start()
    for copy in vectors:
        copy.wait_send()
    for along in range(1, count):
        token_copy(along).wait_send()
        token_on(along).wait_send()
        token_far(along).wait_recv()
    local_t.wait()


def closing(tokens, vectors):
    count = tokens.shape[0]
    dma = pltpu.SemaphoreType.DMA
    anywhere = pl.BlockSpec(memory_space=pl.ANY)
    return pl.pallas_call(
        closing_kernel,
        in_specs=[anywhere] * 2,
        out_specs=[anywhere, pl.BlockSpec(memory_space=pltpu.VMEM)],
        out_shape=[
            jax.ShapeDtypeStruct(tokens.shape, tokens.dtype),
            jax.ShapeDtypeStruct(vectors.shape[1:], F32),
        ],
        scratch_shapes=[pltpu.VMEM(vectors.shape, F32)]
        + [dma((count,))] * 4
        + [dma((4, count))] * 2
        + [dma((2,))],
        compiler_params=pltpu.CompilerParams(collective_id=1, has_side_effects=True),
    )(tokens, vectors)


def norm_back_kernel(field_ref, own_ref, other_ref, rest_ref, gain_ref, *outs):
    field = field_ref[...].astype(F32)
    width = field.shape[1]
    grad = own_ref[...].astype(F32) + other_ref[...].astype(F32)
    centered = field - jnp.sum(field, axis=1, keepdims=True) * (1.0 / width)
    variance = jnp.sum(centered * centered, axis=1, keepdims=True) * (1.0 / width)
    scale = lax.rsqrt(variance + norm_eps)
    unit = centered * scale
    scaled = grad * gain_ref[...]
    mean_one = jnp.sum(scaled, axis=1, keepdims=True) * (1.0 / width)
    mean_two = jnp.sum(scaled * unit, axis=1, keepdims=True) * (1.0 / width)
    total = rest_ref[...].astype(F32) + scale * (scaled - mean_one - unit * mean_two)
    sums_ref = outs[-1]
    for ref in outs[:-1]:
        ref[...] = total.astype(ref.dtype)

    @pl.when(pl.program_id(0) == 0)
    def _():
        sums_ref[...] = jnp.zeros_like(sums_ref)

    for n, item in enumerate((grad * unit, grad, total)):
        sums_ref[pl.ds(n, 1)] += jnp.sum(item, axis=0, keepdims=True)


def norm_back(field, own, other, rest, gain, kinds):
    tokens, width = field.shape
    rows = min(256, tokens)
    block = pl.BlockSpec((rows, width), lambda i: (i, 0))
    flat = lambda n: pl.BlockSpec((n, width), lambda i: (0, 0))
    return pl.pallas_call(
        norm_back_kernel,
        grid=(tokens // rows,),
        in_specs=[block] * 4 + [flat(1)],
        out_specs=[block] * len(kinds) + [flat(8)],
        out_shape=[jax.ShapeDtypeStruct(field.shape, kind) for kind in kinds]
        + [jax.ShapeDtypeStruct((8, width), F32)],
        cost_estimate=told(15.0),
        compiler_params=pltpu.CompilerParams(vmem_limit_bytes=48 * 2**20),
    )(field, own, other, rest, gain.reshape(1, width))


class Move:
    def __init__(self, alongs, src_ref, out_ref, sems):
        self.alongs, self.src, self.out = alongs, src_ref, out_ref
        self.t_send, self.t_recv, self.c_send, self.c_recv = sems
        self.rows, self.place, self.core = [lax.axis_index(name) for name in ("rows", "seq", "fsdp")]
        self.count = src_ref.shape[0]
        self.width = src_ref.shape[2] // 2

    def columns(self, core):
        return pl.ds(pl.multiple_of(core * self.width, self.width), self.width)

    def remote(self, src, dst, send, recv, seq, core):
        return pltpu.make_async_remote_copy(
            src_ref=src, dst_ref=dst, send_sem=send, recv_sem=recv, device_id=(self.rows, seq, core),
            device_id_type=pl.DeviceIdType.MESH,
        )

    def origin(self, along):
        return lax.rem(self.place + self.count - along, self.count)

    def sent(self, n, along):
        to = lax.rem(self.place + along, self.count)
        src, dst = self.src.at[to, :, self.columns(self.core)], self.out.at[self.place, :, self.columns(self.core)]
        return self.remote(src, dst, self.t_send.at[n], self.t_recv.at[n], to, self.core)

    def got(self, n, along):
        start = self.origin(along)
        view = self.out.at[start, :, self.columns(self.core)]
        return self.remote(view, view, self.t_send.at[n], self.t_recv.at[n], start, self.core)

    def passed(self, n, along, mine):
        view = self.out.at[self.origin(along), :, self.columns(self.core if mine else 1 - self.core)]
        return self.remote(view, view, self.c_send.at[n], self.c_recv.at[n], self.place, 1 - self.core)

    def begin(self):
        barrier = pltpu.get_barrier_semaphore()
        peers = sorted(set(self.alongs) | {self.count - along for along in self.alongs})
        for along in peers:
            device = (self.rows, lax.rem(self.place + along, self.count), self.core)
            pl.semaphore_signal(barrier, inc=1, device_id=device, device_id_type=pl.DeviceIdType.MESH)
        device = (self.rows, self.place, 1 - self.core)
        pl.semaphore_signal(barrier, inc=1, device_id=device, device_id_type=pl.DeviceIdType.MESH)
        pl.semaphore_wait(barrier, len(peers) + 1)
        for n, along in enumerate(self.alongs):
            self.sent(n, along).start()

    def end(self):
        for n, along in enumerate(self.alongs):
            self.got(n, along).wait_recv()
            self.passed(n, along, True).start()
        for n, along in enumerate(self.alongs):
            self.sent(n, along).wait_send()
            self.passed(n, along, True).wait_send()
            self.passed(n, along, False).wait_recv()


def product_kernel(mode, finish, n_extra, n_in, move, *refs):
    if move is None:
        return product_step(mode, finish, n_extra, refs[: 2 + n_extra], refs[n_in:-1], refs[-1])
    moving = Move(move, refs[2 + n_extra], refs[n_in + 1], refs[-4:])
    ids = [pl.program_id(n) for n in range(3)]
    ends = [pl.num_programs(n) - 1 for n in range(3)]

    @pl.when((ids[0] == 0) & (ids[1] == 0) & (ids[2] == 0))
    def _():
        moving.begin()

    product_step(mode, finish, n_extra, refs[: 2 + n_extra], refs[n_in : n_in + 1], refs[n_in + 2])

    @pl.when((ids[0] == ends[0]) & (ids[1] == ends[1]) & (ids[2] == ends[2]))
    def _():
        moving.end()


def product_step(mode, finish, n_extra, refs, outs, total):
    a_ref, b_ref = refs[:2]
    extra = refs[2:]
    k = pl.program_id(2)
    last = pl.num_programs(2) - 1
    dims = {"nn": ((1,), (0,)), "nt": ((1,), (1,)), "tn": ((0,), (0,))}[mode]
    part = lax.dot_general(a_ref[...], b_ref[...], (dims, ((), ())), preferred_element_type=F32)
    if last == 0:
        finish(part, extra, outs)
        return

    @pl.when(k == 0)
    def _():
        total[...] = part

    @pl.when((k > 0) & (k < last))
    def _():
        total[...] += part

    @pl.when(k == last)
    def _():
        finish(total[...] + part, extra, outs)


def finish_cast(total, extra, outs):
    outs[0][...] = total.astype(outs[0].dtype)


def finish_bias(scale, total, extra, outs):
    outs[0][...] = ((total + extra[0][...]) * scale).astype(BF)


def product(a, b, mode, finish=finish_cast, rows=(), deps=(), planes=(0,), blocks=(1024, 1024, 2048), move=None):
    plane = len(b.shape) == 3
    b_shape = b.shape[-2:]
    m, depth = a.shape if mode != "tn" else a.shape[::-1]
    n = b_shape[0] if mode == "nt" else b_shape[1]
    bm, bn, bk = min(blocks[0], m), min(blocks[1], n), min(blocks[2], depth)
    spec = pl.BlockSpec
    a_spec = (
        spec((bk, bm), lambda j, i, k: (k, i)) if mode == "tn" else spec((bm, bk), lambda j, i, k: (i, k))
    )
    first, turns = planes[0], len(planes)
    if plane and mode == "nt":
        b_spec = spec((None, bn, bk), lambda j, i, k: (first + k % turns, j, k // turns))
    elif plane:
        b_spec = spec((None, bk, bn), lambda j, i, k: (first, k, j))
    elif mode == "nt":
        b_spec = spec((bn, bk), lambda j, i, k: (j, k))
    else:
        b_spec = spec((bk, bn), lambda j, i, k: (k, j))
    row = spec((1, bn), lambda j, i, k: (0, j))
    field = spec((bm, bn), lambda j, i, k: (i, j))
    out_specs, out_shape = field, jax.ShapeDtypeStruct((m, n), BF)
    scratch, aliases, inputs = [pltpu.VMEM((bm, bn), F32)], {}, (a, b, *rows)
    params = dict(vmem_limit_bytes=48 * 2**20)
    if move is not None:
        src, target, alongs, ident = move
        out_specs, out_shape = (
            [field, spec(memory_space=pl.ANY)],
            [out_shape, jax.ShapeDtypeStruct(src.shape, src.dtype)],
        )
        dma = pltpu.SemaphoreType.DMA
        scratch += [dma((len(alongs),))] * 4
        aliases = {len(inputs) + 1: 1}
        inputs += (src, target)
        params.update(collective_id=ident, has_side_effects=True)
        move = alongs
    n_in = len(inputs) + len(deps)
    return pl.pallas_call(
        functools.partial(product_kernel, mode, finish, len(rows), n_in, move),
        grid=(n // bn, m // bm, depth // bk),
        in_specs=[a_spec, b_spec]
        + [row] * len(rows)
        + [spec(memory_space=pl.ANY)] * (n_in - 2 - len(rows)),
        out_specs=out_specs,
        out_shape=out_shape,
        scratch_shapes=scratch,
        input_output_aliases=aliases,
        cost_estimate=told(2.0 * m * n * depth / 8e8),
        compiler_params=pltpu.CompilerParams(**params),
    )(*inputs, *deps)


def dot_nt(a,b): return lax.dot_general(a,b,(((1,),(1,)),((),())),preferred_element_type=F32)
def dot_nn(a,b): return lax.dot_general(a,b,(((1,),(0,)),((),())),preferred_element_type=F32)

def fwd_kernel(tile, flags, q_ref, k_ref, v_ref, sk_ref, sv_ref, start_ref, doc_ref, sdoc_ref, *rest):
    o_ref, lse_ref, km, vt, acc, top, total = rest[-7:]
    i = pl.program_id(1)
    seg = k_ref.shape[0]
    lanes = lax.broadcasted_iota(jnp.int32, (1, 128), 1)
    masks = [(lanes < HEAD).astype(BF), (lanes >= HEAD).astype(BF)]
    @pl.when(i == 0)
    def _():
        for h in range(2):
            km[h, pl.ds(0, seg)] = k_ref[...] * masks[h]
            km[h, pl.ds(seg, 128)] = sk_ref[...] * masks[h]
        vt[:, pl.ds(0, seg)] = v_ref[...].T
        vt[:, pl.ds(seg, 128)] = sv_ref[...].T
    q = q_ref[...]
    allowed = sdoc_ref[...] == doc_ref[...]
    for h in range(2):
        s = dot_nt(km[h, pl.ds(seg, 128)], q)
        s = jnp.where(allowed, s, neg_big)
        m = jnp.max(s, axis=0, keepdims=True)
        p = jnp.where(allowed, jnp.exp(s - m), 0.0)
        top[h] = m
        total[h] = jnp.sum(p, axis=0, keepdims=True)
        acc[h] = dot_nn(vt[pl.ds(h * HEAD, HEAD), pl.ds(seg, 128)], p.astype(BF))
    def step(j, masked):
        at = pl.multiple_of(j * tile, tile)
        if masked:
            places = at + lax.broadcasted_iota(jnp.int32, (tile, tile), 0)
            mine = i * tile + lax.broadcasted_iota(jnp.int32, (tile, tile), 1)
            okay = (places <= mine) & (places >= start_ref[...])
        ss=[]
        for h in range(2):
            s = dot_nt(km[h, pl.ds(at, tile)], q)
            if masked:
                s = jnp.where(okay, s, neg_big)
            ss.append(s)
        for h in range(2):
            s = ss[h]
            m_old = top[h]
            m = jnp.maximum(m_old, jnp.max(s, axis=0, keepdims=True))
            p = jnp.exp(s - m)
            if masked:
                p = jnp.where(okay, p, 0.0)
            alpha = jnp.exp(m_old - m)
            top[h] = m
            total[h] = total[h] * alpha + jnp.sum(p, axis=0, keepdims=True)
            acc[h] = acc[h] * alpha + dot_nn(vt[pl.ds(h * HEAD, HEAD), pl.ds(at, tile)], p.astype(BF))
    count = pl.num_programs(1)
    def loop(j, _):
        flag = flags[i * count + j]
        @pl.when(flag == 2)
        def _(): step(j, False)
        @pl.when(flag == 1)
        def _(): step(j, True)
        return 0
    lax.fori_loop(0, i + 1, loop, 0)
    out = [acc[h] / total[h] for h in range(2)]
    o_ref[...] = jnp.concatenate(out, axis=0).T.astype(BF)
    for h in range(2):
        lse_ref[0, pl.ds(h, 1)] = top[h] + jnp.log(total[h])

def attn_fwd(q, k, v, sk, sv, start, doc, sdoc, flags, tile, base, pairs, earlier_out=(), deps=()):
    seg, width = q.shape
    count = seg // tile
    spec = pl.BlockSpec
    extra = tuple(earlier_out) + tuple(deps)
    return pl.pallas_call(
        functools.partial(fwd_kernel, tile),
        grid_spec=pltpu.PrefetchScalarGridSpec(
            num_scalar_prefetch=1,
            grid=(pairs, count),
            in_specs=[
                spec((tile, 128), lambda h, i, f: (i, h + base)),
                spec((seg, 128), lambda h, i, f: (0, h + base)),
                spec((seg, 128), lambda h, i, f: (0, h + base)),
                spec((128, 128), lambda h, i, f: (0, h + base)),
                spec((128, 128), lambda h, i, f: (0, h + base)),
                spec((1, tile), lambda h, i, f: (0, i)),
                spec((1, tile), lambda h, i, f: (0, i)),
                spec((128, 1), lambda h, i, f: (0, 0)),
            ]
            + [spec(memory_space=pl.ANY)] * len(extra),
            out_specs=[
                spec((tile, 128), lambda h, i, f: (i, h + base)),
                spec((1, 2, tile), lambda h, i, f: (h + base, 0, i)),
            ],
            scratch_shapes=[
                pltpu.VMEM((2, seg + 128, 128), BF),
                pltpu.VMEM((128, seg + 128), BF),
                pltpu.VMEM((2, HEAD, tile), F32),
                pltpu.VMEM((2, 1, tile), F32),
                pltpu.VMEM((2, 1, tile), F32),
            ],
        ),
        out_shape=[
            jax.ShapeDtypeStruct((seg, width), BF),
            jax.ShapeDtypeStruct((width // 128, 2, seg), F32),
        ],
        input_output_aliases={9: 0, 10: 1} if earlier_out else {},
        cost_estimate=told(4.2 * pairs * 4),
        compiler_params=pltpu.CompilerParams(vmem_limit_bytes=40 * 2**20),
    )(flags, q, k, v, sk, sv, start, doc, sdoc, *extra)


def bwd_kernel(tile, flags, q_ref, k_ref, v_ref, do_ref, o_ref, sk_ref, sv_ref, lse_ref, start_ref, doc_ref, sdoc_ref, *rest):
    dq_ref, dk_ref, dv_ref, dsk_ref, dsv_ref, qm, dom, dqt, delta = rest[-9:]
    j = pl.program_id(1)
    seg = q_ref.shape[0]
    count = seg // tile
    lanes = lax.broadcasted_iota(jnp.int32, (1, 128), 1)
    masks = [(lanes < HEAD).astype(BF), (lanes >= HEAD).astype(BF)]
    @pl.when(j == 0)
    def _():
        dqt[...] = jnp.zeros_like(dqt)
        for h in range(2):
            qm[h] = q_ref[...] * masks[h]
            dom[h] = do_ref[...] * masks[h]
        def one(i, _):
            at = pl.multiple_of(i * tile, tile)
            prod = (do_ref[pl.ds(at, tile)].astype(F32) * o_ref[pl.ds(at, tile)].astype(F32)).T
            for h in range(2):
                delta[h, :, pl.ds(at, tile)] = jnp.sum(prod[h * HEAD:(h + 1) * HEAD], axis=0, keepdims=True)
            return 0
        lax.fori_loop(0, count, one, 0)
    def block(i, kt, k_blk, v_blk, okay):
        at = pl.multiple_of(i * tile, tile)
        gk = gv = None
        for h in range(2):
            qh = qm[h, pl.ds(at, tile)]
            dh = dom[h, pl.ds(at, tile)]
            s = dot_nt(k_blk, qh)
            dp = dot_nt(v_blk, dh)
            p = jnp.exp(s - lse_ref[0, pl.ds(h, 1), pl.ds(at, tile)])
            if okay is not None:
                p = jnp.where(okay, p, 0.0)
            ds = (p * (dp - delta[h, :, pl.ds(at, tile)])).astype(BF)
            a = dot_nn(p.astype(BF), dh)
            b = dot_nn(ds, qh)
            gv = a if gv is None else gv + a
            gk = b if gk is None else gk + b
            dqt[pl.ds(h * HEAD, HEAD), pl.ds(at, tile)] += dot_nn(kt[h * HEAD:(h + 1) * HEAD], ds)
        return gk, gv
    @pl.when(j < count)
    def _():
        at_k = pl.multiple_of(j * tile, tile)
        k_blk = k_ref[...]
        v_blk = v_ref[...]
        kt = k_blk.T
        def masked_of(i):
            places = at_k + lax.broadcasted_iota(jnp.int32, (tile, tile), 0)
            mine = i * tile + lax.broadcasted_iota(jnp.int32, (tile, tile), 1)
            return (places <= mine) & (places >= start_ref[:, pl.ds(pl.multiple_of(i * tile, tile), tile)])
        gk, gv = block(j, kt, k_blk, v_blk, masked_of(j))
        dkacc, dvacc = gk, gv
        def loop(i, carry):
            flag = flags[i * count + j]
            def full(c):
                gk, gv = block(i, kt, k_blk, v_blk, None)
                return c[0] + gk, c[1] + gv
            def part(c):
                gk, gv = block(i, kt, k_blk, v_blk, masked_of(i))
                return c[0] + gk, c[1] + gv
            return lax.switch(flag, [lambda c: c, part, full], carry)
        dkacc, dvacc = lax.fori_loop(j + 1, count, loop, (dkacc, dvacc))
        dk_ref[...] = dkacc.astype(BF)
        dv_ref[...] = dvacc.astype(BF)
    @pl.when(j == count)
    def _():
        kt = sk_ref[...].T
        def loop(i, carry):
            okay = sdoc_ref[...] == doc_ref[:, pl.ds(pl.multiple_of(i * tile, tile), tile)]
            gk, gv = block(i, kt, sk_ref[...], sv_ref[...], okay)
            return carry[0] + gk, carry[1] + gv
        z = jnp.zeros((128, 128), F32)
        a, b = lax.fori_loop(0, count, loop, (z, z))
        dsk_ref[...] = a.astype(BF)
        dsv_ref[...] = b.astype(BF)
        def fin(i, _):
            at = pl.multiple_of(i * tile, tile)
            dq_ref[pl.ds(at, tile)] = (dqt[:, pl.ds(at, tile)].T.astype(BF).astype(F32) * HEAD ** -0.5).astype(BF)
            return 0
        lax.fori_loop(0, count, fin, 0)

def attn_bwd(q, k, v, do, o, sk, sv, lse, start, doc, sdoc, flags, tile, base, pairs, deps=()):
    seg = q.shape[0]
    count = seg // tile
    last = count - 1
    spec = pl.BlockSpec
    return pl.pallas_call(
        functools.partial(bwd_kernel, tile),
        grid_spec=pltpu.PrefetchScalarGridSpec(
            num_scalar_prefetch=1,
            grid=(pairs, count + 1),
            in_specs=[
                spec((seg, 128), lambda h, j, f: (0, h + base)),
                spec((tile, 128), lambda h, j, f: (jnp.minimum(j, last), h + base)),
                spec((tile, 128), lambda h, j, f: (jnp.minimum(j, last), h + base)),
                spec((seg, 128), lambda h, j, f: (0, h + base)),
                spec((seg, 128), lambda h, j, f: (0, h + base)),
                spec((128, 128), lambda h, j, f: (0, h + base)),
                spec((128, 128), lambda h, j, f: (0, h + base)),
                spec((1, 2, seg), lambda h, j, f: (h + base, 0, 0)),
                spec((1, seg), lambda h, j, f: (0, 0)),
                spec((1, seg), lambda h, j, f: (0, 0)),
                spec((128, 1), lambda h, j, f: (0, 0)),
            ]
            + [spec(memory_space=pl.ANY)] * len(deps),
            out_specs=[
                spec((seg, 128), lambda h, j, f: (0, h)),
                spec((tile, 128), lambda h, j, f: (jnp.minimum(j, last), h)),
                spec((tile, 128), lambda h, j, f: (jnp.minimum(j, last), h)),
                spec((128, 128), lambda h, j, f: (0, h)),
                spec((128, 128), lambda h, j, f: (0, h)),
            ],
            scratch_shapes=[
                pltpu.VMEM((2, seg, 128), BF),
                pltpu.VMEM((2, seg, 128), BF),
                pltpu.VMEM((128, seg), F32),
                pltpu.VMEM((2, 1, seg), F32),
            ],
        ),
        out_shape=[jax.ShapeDtypeStruct((seg, pairs * 128), BF)] * 3
        + [jax.ShapeDtypeStruct((128, pairs * 128), BF)] * 2,
        cost_estimate=told(5.5 * pairs * 4),
        compiler_params=pltpu.CompilerParams(vmem_limit_bytes=40 * 2**20),
    )(flags, q, k, v, do, o, sk, sv, lse, start, doc, sdoc, *deps)


def make_meta(doc, tile):
    seg=doc.shape[0]; count=seg//tile
    place=jnp.arange(seg,dtype=jnp.int32)
    new=jnp.concatenate([jnp.ones((1,),bool), doc[1:]!=doc[:-1]])
    start=lax.cummax(jnp.where(new,place,0))
    lo=doc[::tile]; hi=doc[tile-1::tile]
    i=jnp.arange(count)
    full=(lo[None,:]==hi[:,None])&(i[None,:]<i[:,None])
    none=(hi[None,:]<lo[:,None])
    flags=jnp.where(full,2,jnp.where(none,0,1)).astype(jnp.int32).reshape(-1)
    return start.reshape(1,seg), flags


def gate(value, *deps):
    anywhere = pl.BlockSpec(memory_space=pl.ANY)
    return pl.pallas_call(
        lambda *refs: None,
        in_specs=[anywhere] * (1 + len(deps)),
        out_specs=anywhere,
        out_shape=jax.ShapeDtypeStruct(value.shape, value.dtype),
        input_output_aliases={0: 0},
        cost_estimate=SMALL_COST,
    )(value, *deps)


def blank(shape, dtype):
    return pl.pallas_call(
        lambda ref: None,
        out_specs=pl.BlockSpec(memory_space=pl.ANY),
        out_shape=jax.ShapeDtypeStruct(shape, dtype),
        cost_estimate=SMALL_COST,
    )()


def copied(blocks):
    block = pl.BlockSpec((1,) + blocks.shape[1:], lambda i: (i, 0, 0))

    def kernel(source, target):
        target[...] = source[...]

    return pl.pallas_call(
        kernel,
        grid=blocks.shape[:1],
        in_specs=[block],
        out_specs=block,
        out_shape=jax.ShapeDtypeStruct(blocks.shape, blocks.dtype),
        cost_estimate=told(6.0),
        compiler_params=pltpu.CompilerParams(vmem_limit_bytes=24 * 2**20),
    )(blocks)


BOTH = ("rows", "seq")


def other_core(block):
    return lax.ppermute(block, "fsdp", ((0, 1), (1, 0)))


def along_line(field, begin, hold):
    count = lax.axis_size("seq")
    me = lax.axis_index("seq")
    core = lax.axis_index("fsdp")
    half = field.shape[2] // 2
    mine = gate(lax.dynamic_slice_in_dim(field, core * half, half, 2), begin)
    got = jnp.zeros_like(mine)
    own = lax.dynamic_slice_in_dim(mine, me, 1, 0)
    got = lax.dynamic_update_slice_in_dim(got, own, me, 0)
    for away in range(1, count):
        block = lax.dynamic_slice_in_dim(mine, lax.rem(me + away, count), 1, 0)
        moved = lax.ppermute(block, "seq", [(n, (n + away) % count) for n in range(count)])
        moved = gate(moved, *hold)
        got = lax.dynamic_update_slice_in_dim(got, moved, lax.rem(me + count - away, count), 0)
    return got


def between_cores(got, hold=()):
    core = lax.axis_index("fsdp")
    other = other_core(got)
    other = gate(other, *hold) if hold else other
    low_half = jnp.where(core == 0, got, other)
    high_half = jnp.where(core == 0, other, got)
    return jnp.concatenate((low_half, high_half), axis=2)


def shift_by(field, away):
    count = lax.axis_size("seq")
    perm = [(n, n + away) for n in range(count) if 0 <= n + away < count]
    return lax.ppermute(field, "seq", perm)


def both_halves(field):
    low = field.astype(BF)
    return low.astype(F32) + other_core(low).astype(F32)


def norm_forward(field, gain_vec, shift_vec):
    row_mean = jnp.mean(field, axis=-1, keepdims=True)
    centered = field - row_mean
    variance = jnp.mean(centered * centered, axis=-1, keepdims=True)
    scale = lax.rsqrt(variance + norm_eps)
    return (centered * scale * gain_vec + shift_vec).astype(BF)


def mm(a, b):
    return dot_nn(a, b)


def mm_tn(a, b):
    return lax.dot_general(a, b, (((0,), (0,)), ((), ())), preferred_element_type=F32)


def mm_nt(a, b):
    return dot_nt(a, b)


def layer_by_segment(
    states,
    doc_ids,
    w_qkv,
    w_out,
    w_up,
    w_down,
    bias_qv,
    bias_out,
    bias_up,
    bias_down,
    gain_one,
    shift_one,
    gain_two,
    shift_two,
    cotangent,
):
    segs, width, model = states.shape[1:]
    seg_len = segs * width
    place = lax.axis_index("seq")
    half = w_qkv.shape[2]
    hidden_units = w_up.shape[1]
    tile = 512

    small = (bias_qv, bias_out, bias_up, bias_down, gain_one, shift_one, gain_two, shift_two)
    sizes = [item.size for item in small]
    vector = jnp.concatenate([item.reshape(-1) for item in small])
    room = -(-vector.shape[0] // 2048) * 2048
    vector = jnp.pad(vector, (0, room - vector.shape[0])).reshape(-1, 128)
    attn_weights = jnp.concatenate((w_qkv, w_out.T[None]), axis=0)
    attn_full, tokens, packed = opening(attn_weights, states[0], vector)
    tokens = tokens.reshape(seg_len, model)
    packed = packed.reshape(packed.shape[0], -1)
    cuts = []
    at = 0
    for size in sizes:
        cuts.append(packed[:, at : at + size].astype(F32))
        at += size
    shards = packed.shape[0]

    def spread_last(field, lead):
        return jnp.moveaxis(field.reshape(shards, *lead, -1), 0, len(lead)).reshape(-1)

    bias_pair = jnp.moveaxis(cuts[0].reshape(shards, 2, half // HEAD, -1), 0, 2).reshape(2, half)
    bias_o = cuts[1].reshape(-1)
    bias_u = spread_last(cuts[2], (hidden_units // HEAD,))
    bias_d = cuts[3].reshape(-1)
    gain_a, shift_a, gain_b, shift_b = [item.reshape(-1) for item in cuts[4:]]

    docs = doc_ids[0]
    my_docs = lax.dynamic_index_in_dim(docs, place, 0, keepdims=False)
    start, flags = make_meta(my_docs, tile)
    tails = docs[:, seg_len - SUMM :]
    before_one = lax.dynamic_index_in_dim(tails, jnp.maximum(place - 1, 0), 0, keepdims=False)
    before_two = lax.dynamic_index_in_dim(tails, jnp.maximum(place - 2, 0), 0, keepdims=False)
    sum_docs = jnp.concatenate(
        (
            jnp.where(place >= 1, before_one, -1),
            jnp.where(place >= 2, before_two, -1),
            jnp.full((128 - 2 * SUMM,), -1, jnp.int32),
        )
    ).reshape(128, 1)
    doc_row = my_docs.reshape(1, seg_len)

    tokens_f = tokens.astype(F32)
    normed_one = norm_forward(tokens_f, gain_a, shift_a)
    query = product(
        normed_one, attn_full, "nn", functools.partial(finish_bias, HEAD**-0.5), (bias_pair[:1],), planes=(0,)
    )
    keys = product(normed_one, attn_full, "nn", planes=(1,))
    values = product(
        normed_one, attn_full, "nn", functools.partial(finish_bias, 1.0), (bias_pair[1:],), planes=(2,)
    )
    up_full = lax.all_gather(gate(w_up, tokens), BOTH, axis=0, tiled=True)
    tail = jnp.stack((keys[seg_len - SUMM :], values[seg_len - SUMM :]))
    lent = jnp.concatenate((shift_by(tail, 1), shift_by(tail, 2)), axis=1)
    lent = jnp.pad(lent, ((0, 0), (0, 128 - 2 * SUMM), (0, 0)))
    pairs = half // 128
    each = pairs // 4
    attended = ()
    done = []
    for n in range(4):
        attended = attn_fwd(
            query, keys, values, lent[0], lent[1], start, doc_row, sum_docs, flags, tile,
            n * each, each, attended,
        )
        done.append(attended[1])
    down_full = lax.all_gather(gate(w_down.T, values), BOTH, axis=0, tiled=True)
    mixed, log_sum = attended
    attended = product(mixed, attn_full, "nt", planes=(3,))
    grad_out = along_line(cotangent[0], query, (done[2],))
    grad_out = between_cores(grad_out, (attended,)).reshape(seg_len, model)
    hidden = tokens_f + both_halves(attended) + bias_o
    normed_two = norm_forward(hidden, gain_b, shift_b)
    up_proj = mm(normed_two, up_full) + bias_u
    bell = jnp.exp(-0.5 * up_proj * up_proj)
    area = 0.5 * (1.0 + lax.erf(up_proj * (0.5**0.5)))
    activated = (up_proj * area).astype(BF)
    slope = (area + up_proj * bell * 0.3989422804014327).astype(BF)

    def over_rows(partial):
        return lax.psum_scatter(partial, "rows", scatter_dimension=0, tiled=True)

    def over_seq(partial):
        return lax.psum_scatter(partial, "seq", scatter_dimension=0, tiled=True)

    down_sum = product(grad_out, activated, "tn")
    down_rows = over_rows(down_sum)
    slope = gate(slope, down_sum)
    d_up = (mm(grad_out, down_full) * slope.astype(F32)).astype(BF)
    up_sum = product(normed_two, d_up, "tn")
    def column_sum(field):
        return jnp.sum(field.astype(F32), axis=0)

    d_norm_part = product(d_up, up_full, "nt", deps=(up_sum,))
    sum_grad_out = column_sum(grad_out)
    d_norm_other = gate(other_core(d_norm_part), sum_grad_out)
    up_turn = gate(up_sum, down_rows, d_norm_other)
    up_rows = over_rows(up_turn)
    d_hidden, d_hidden_low, sums_two = norm_back(
        hidden, d_norm_part, d_norm_other, grad_out, gain_b, (F32, BF)
    )
    d_mixed = product(d_hidden_low, attn_full, "nn", deps=(up_turn,), planes=(3,))
    out_sum = product(d_hidden_low, mixed, "tn", deps=(d_mixed,))

    def back(n, count, deps):
        return attn_bwd(
            query, keys, values, d_mixed, mixed, lent[0], lent[1], log_sum, start, doc_row,
            sum_docs, flags, tile, n * each, count * each, deps,
        )

    def own_half(pieces, move, deps=()):
        d_pre, d_keys, d_values, d_lent_k, d_lent_v = [
            jnp.concatenate(pair, axis=1) if len(pair) > 1 else pair[0] for pair in zip(*pieces)
        ]
        d_lent = jnp.stack((d_lent_k, d_lent_v))
        back_home = shift_by(d_lent[:, :SUMM], -1).astype(F32) + shift_by(
            d_lent[:, SUMM : 2 * SUMM], -2
        ).astype(F32)
        ends = jnp.stack((d_keys[seg_len - SUMM :], d_values[seg_len - SUMM :])).astype(F32)
        ends = (ends + back_home).astype(BF)
        d_keys = lax.dynamic_update_slice(d_keys, ends[0], (seg_len - SUMM, 0))
        d_values = lax.dynamic_update_slice(d_values, ends[1], (seg_len - SUMM, 0))
        grads = jnp.concatenate((d_pre, d_keys, d_values), axis=1)
        return grads, product(
            normed_one, grads, "tn", blocks=(1024, grads.shape[1] // 2, 2048), move=move, deps=deps
        )

    piece_0 = back(0, 1, (out_sum,))
    out_partial = product(activated, down_full, "nt", deps=(piece_0[0],))
    down_turn = gate(down_rows, up_rows, out_partial)
    down_seq = over_seq(down_turn)
    grad_w_down = down_seq.astype(F32)
    out_tokens = (hidden + both_halves(out_partial) + bias_d).astype(BF).reshape(segs, width, model)
    out_own = lax.dynamic_slice_in_dim(out_tokens, place, 1, 0)
    out_begun = lax.dynamic_update_slice_in_dim(blank(out_tokens.shape, BF), out_own, place, 0)
    piece_1 = back(1, 1, (down_turn, out_begun))
    out_turn = gate(out_sum, down_seq, piece_1[0])
    out_rows = over_rows(out_turn)
    first_half, (first_sum, out_moved) = own_half((piece_0, piece_1), (out_tokens, out_begun, (1,), 2), (out_turn,))
    up_turn_two = gate(up_rows, out_rows, first_sum)
    up_seq = over_seq(up_turn_two)
    grad_w_up = up_seq.astype(F32)
    first_turn = gate(first_sum, up_turn_two)
    first_rows = over_rows(first_turn)
    piece_2 = back(2, 2, (first_turn,))
    second_half, (second_sum, out_moved) = own_half((piece_2,), (out_tokens, out_moved, (segs - 1,), 3))
    second_turn = gate(second_sum, first_rows, up_seq)
    second_rows = over_rows(second_turn)
    d_qkv = jnp.concatenate((first_half, second_half), axis=1)
    d_norm_part, out_moved = product(
        d_qkv, attn_full, "nt", deps=(second_turn,), blocks=(1024, 1024, half // 2), planes=(0, 1, 2),
        move=(out_tokens, out_moved, tuple(range(2, segs - 1)), 4),
    )
    out_states = copied(out_moved)[None]
    kind_sum = column_sum(d_qkv).reshape(2, 3, half // 2)
    d_norm_other = gate(other_core(d_norm_part), kind_sum, out_states)
    grad_tokens, sums_one = norm_back(
        tokens, d_norm_part, d_norm_other, d_hidden, gain_a, (BF,)
    )
    grad_w_down = grad_w_down.T
    qkv_rows = jnp.concatenate((out_rows, first_rows, gate(second_rows, d_norm_other)), axis=1)
    attn_seq = over_seq(qkv_rows)
    grad_w_out = attn_seq[:, :half].astype(F32).T
    piece = half // 2

    def columns_of(kind, part):
        first = half + (3 * part + kind) * piece
        return attn_seq[:, first : first + piece]

    grad_w_qkv = jnp.stack(
        [jnp.concatenate((columns_of(kind, 0), columns_of(kind, 1)), axis=1) for kind in range(3)]
    ).astype(F32)

    sums = (
        jnp.moveaxis(
            jnp.stack((kind_sum[:, 0], kind_sum[:, 2])).reshape(2, half // HEAD, shards, -1), 2, 0
        ),
        sums_two[2],
        jnp.moveaxis(column_sum(d_up).reshape(hidden_units // HEAD, shards, -1), 1, 0),
        sum_grad_out,
        sums_one[0],
        sums_one[1],
        sums_two[0],
        sums_two[1],
    )
    vectors = jnp.concatenate([item.reshape(shards, -1) for item in sums], axis=1)
    vectors = jnp.pad(vectors, ((0, 0), (0, room - vectors.shape[1]))).reshape(shards, -1, 128)
    grad_states, vector = closing(grad_tokens.reshape(segs, width, model), gate(vectors, qkv_rows))
    grad_states = grad_states[None]
    vector = vector.reshape(-1)
    small_grads = []
    at = 0
    for item, size in zip(small, sizes):
        small_grads.append(vector[at : at + size].reshape(item.shape))
        at += size
    return (out_states, grad_states, grad_w_qkv, grad_w_out, grad_w_up, grad_w_down, *small_grads)


def solution(mesh):
    whole_segments = mesh.shape["seq"] == SEGS and mesh.shape["rows"] == 4
    return jax.shard_map(
        layer_by_segment if whole_segments else local,
        mesh=mesh,
        in_specs=(
            P("rows", None, "seq", None),
            P("rows", None, None),
            P(None, ("rows", "seq"), "fsdp"),
            P("fsdp", ("rows", "seq")),
            P(("rows", "seq"), "fsdp"),
            P("fsdp", ("rows", "seq")),
            P(None, "fsdp", ("rows", "seq")),
            P(("rows", "seq")),
            P("fsdp", ("rows", "seq")),
            P(("rows", "seq")),
            P(("rows", "seq")),
            P(("rows", "seq")),
            P(("rows", "seq")),
            P(("rows", "seq")),
            P("rows", None, "seq", None),
        ),
        out_specs=(
            P("rows", None, "seq", None),
            P("rows", None, "seq", None),
            P(None, ("rows", "seq"), "fsdp"),
            P("fsdp", ("rows", "seq")),
            P(("rows", "seq"), "fsdp"),
            P("fsdp", ("rows", "seq")),
            P(None, "fsdp", ("rows", "seq")),
            P(("rows", "seq")),
            P("fsdp", ("rows", "seq")),
            P(("rows", "seq")),
            P(("rows", "seq")),
            P(("rows", "seq")),
            P(("rows", "seq")),
            P(("rows", "seq")),
        ),
        check_vma=False,
    )
```
